128 devices in a mesh: tensor: 8 (over y, x_lo), context: 16 (over x_hi, z, core).
Axes of the slice: x: 4 (x_hi: 2, x_lo: 2; x = x_hi * 2 + x_lo), y: 4, z: 4, core: 2. Of those that a mesh axis runs over, the one named last changes fastest.
Arguments:
- teacher_in: bfloat16 [16384, 4096], P('context', 'tensor'), may hold values from -6 to 6
- teacher_resid: bfloat16 [16384, 8192], P('context', 'tensor'), may hold values from -17 to 17
- teacher_wo: bfloat16 [4096, 8192], P('tensor'), may hold values from -0.09375 to 0.09375
- teacher_gain: float32 [8192], replicated, may hold values from 0.5 to 1.5
- input_history: float32 [16], replicated, may hold values from 1.5 to 3.5
- weight_history: float32 [16], replicated, as said below
- student_hidden: bfloat16 [16384, 4096], P(('context', 'tensor')), may hold values from -24 to 24
- student_gain: float32 [4096], replicated, may hold values from 0.5 to 1.5
- projection: bfloat16 [4096, 8192], P('context', 'tensor'), may hold values from -0.09375 to 0.09375
Outputs:
- proj_grad: float32 [4096, 8192], P('context', 'tensor')
- distill_loss: float32 [], replicated
- input_history_new: float32 [16], replicated
- weight_history_new: float32 [16], replicated
The draws below stay inside these ranges and needn't reach their ends.
Inputs may be any that keep to these rules, and one draw needn't show every extreme that they name: `weight_history`: entries lie between 1.6 and 3.2 times 4096 ** -0.5.
All inputs are finite; a program needn't handle non-finite values.
Results may differ from the reference program's by a relative error of at most 0.018.
Values may be sent and summed in bfloat16 or wider, within the bound.
A program may use at most 192 MiB of HBM per device.

```python
import math
import jax
import jax.numpy as jnp
from jax import lax

DT = 8192
DS = 4096
TIN = 4096
HIST = 16
LENGTH = 16384
N_TENSOR = 8
N_CONTEXT = 16


def draw_weight_history(key, part):
    key = jax.random.fold_in(key, 7)
    factor = jnp.exp(jax.random.uniform(key, (HIST,), jnp.float32, math.log(1.6), math.log(3.2)))
    return factor * (1.0 / math.sqrt(TIN))


def draw_teacher_resid(key, part):
    key = jax.random.fold_in(key, 11)
    rough_key, value_key = jax.random.split(key)
    column = jnp.arange(DT, dtype=jnp.float32) / float(max(DT - 1, 1))
    rough = jnp.exp(jax.random.uniform(rough_key, (DT,), jnp.float32, math.log(0.7), math.log(1.4)))
    ramp = 0.5 * jnp.exp(math.log(6.0) * column)
    values = jnp.clip(jax.random.normal(value_key, (LENGTH, DT), jnp.float32), -4.0, 4.0)
    return (values * (ramp * rough)[None, :]).astype(jnp.bfloat16)


def spiked(result, own_key, source, target, blocks, factor):
    owner, partner = [(jnp.arange(result.shape[dim]) // (result.shape[dim] // blocks)).reshape([-1 if axis == dim else 1 for axis in range(result.ndim)]) for dim in (source, target)]
    chosen = jax.random.permutation(own_key, blocks)[partner]
    strong = (owner == chosen) | (owner == (partner + blocks // 2) % blocks)
    return jnp.where(strong, factor * result, result)


def steps_of(stream_key, dims, cuts, least, top_value):
    def one(dim, parts):
        heights = jax.random.uniform(jax.random.fold_in(jax.random.fold_in(stream_key, 6), dim), (parts,), jnp.float32, least / len(cuts), top_value / len(cuts))
        return jnp.repeat(jnp.exp(heights), dims[dim] // parts).reshape((-1,) + (1,) * (len(dims) - dim - 1))

    gain = one(*cuts[0])
    for cut in cuts[1:]:
        gain = gain * one(*cut)
    return gain


def normal_values(key, dims, scale, reach, cuts=(), kind=jnp.bfloat16):
    level = steps_of(key, dims, cuts, -0.22, 0.18) if cuts else 1.0
    array = jax.random.normal(key, dims, jnp.float32) * scale * level
    return jnp.minimum(jnp.maximum(array, -reach), reach).astype(kind)


def noise_with(key, shape, spread, most, cuts, heavy, kind=jnp.bfloat16):
    result = spread * jax.random.normal(key, shape, jnp.float32)
    if cuts:
        result = result * steps_of(key, shape, cuts, -0.22, 0.18)
    return jnp.clip(spiked(result, jax.random.fold_in(key, 3), *heavy), -most, most).astype(kind)


def setup_inputs(seed: int = 0) -> dict:
    streams_of = jax.random.split(jax.random.key(seed), 10)
    return {
        "teacher_in": normal_values(streams_of[0], (LENGTH, TIN), 1.0, 6.0, ((0, 16), (1, 8))),
        "teacher_resid": draw_teacher_resid(jax.random.fold_in(streams_of[9], 71), 0),
        "teacher_wo": normal_values(streams_of[2], (TIN, DT), TIN ** -0.5, 0.09375, ((0, 8),)),
        "teacher_gain": jnp.clip(1.0 + 0.1 * jax.random.normal(streams_of[3], (DT,), jnp.float32), 0.5, 1.5),
        "input_history": jnp.clip(jnp.exp(jax.random.uniform(streams_of[4], (HIST,), jnp.float32, math.log(1.5), math.log(3.5))), 1.5, 3.5),
        "weight_history": draw_weight_history(jax.random.fold_in(streams_of[9], 71), 0),
        "student_hidden": noise_with(streams_of[6], (LENGTH, DS), 1.0, 24.0, ((0, 128),), (0, 1, 128, 5.5)),
        "student_gain": jnp.clip(1.0 + 0.1 * jax.random.normal(streams_of[7], (DS,), jnp.float32), 0.5, 1.5),
        "projection": normal_values(streams_of[8], (DS, DT), DS ** -0.5, 0.09375, ((0, 16), (1, 8))),
    }


def normalize(hidden_rows, gain_row):
    return hidden_rows * lax.rsqrt(lax.optimization_barrier(jnp.mean(hidden_rows * hidden_rows, axis=-1, keepdims=True)) + 1e-05) * gain_row

def reference(teacher_in, teacher_resid, teacher_wo, teacher_gain, input_history, weight_history, student_hidden, student_gain, projection):
    input_amax = jnp.max(jnp.abs(teacher_in.astype(jnp.float32)))
    weight_amax = jnp.max(jnp.abs(teacher_wo.astype(jnp.float32)))
    input_history_new = jnp.concatenate([input_amax.reshape(1), input_history[:-1]])
    weight_history_new = jnp.concatenate([weight_amax.reshape(1), weight_history[:-1]])
    input_limit = jnp.max(input_history)
    weight_limit = jnp.max(weight_history)
    input_sat = jnp.clip(teacher_in.astype(jnp.float32), -input_limit, input_limit).astype(jnp.bfloat16)
    weight_sat = jnp.clip(teacher_wo.astype(jnp.float32), -weight_limit, weight_limit).astype(jnp.bfloat16)
    block_len = TIN // N_TENSOR

    def add_block(running, position):
        inputs = lax.dynamic_slice_in_dim(input_sat, position * block_len, block_len, 1)
        weights = lax.dynamic_slice_in_dim(weight_sat, position * block_len, block_len, 0)
        partial_value = jnp.dot(inputs, weights, preferred_element_type=jnp.float32).astype(jnp.bfloat16)
        partial_value = lax.optimization_barrier(partial_value)
        return (running + partial_value.astype(jnp.float32), None)
    projected, _ = lax.scan(add_block, jnp.zeros((LENGTH, DT), jnp.float32), jnp.arange(N_TENSOR, dtype=jnp.int32))
    hidden = teacher_resid.astype(jnp.float32) + projected
    target = normalize(hidden, teacher_gain)
    student_norm = normalize(student_hidden.astype(jnp.float32), student_gain).astype(jnp.bfloat16)
    mapped = jnp.dot(student_norm, projection, preferred_element_type=jnp.float32)
    error = mapped - target
    distill_loss = 0.5 * jnp.sum(error * error) / (LENGTH * DT)
    error_low = error.astype(jnp.bfloat16)
    group_len = LENGTH // N_CONTEXT

    def add_group(running, position):
        rows_norm = lax.dynamic_slice_in_dim(student_norm, position * group_len, group_len, 0)
        rows_error = lax.dynamic_slice_in_dim(error_low, position * group_len, group_len, 0)
        partial_value = jnp.dot(rows_norm.T, rows_error, preferred_element_type=jnp.float32).astype(jnp.bfloat16)
        partial_value = lax.optimization_barrier(partial_value)
        return (running + partial_value.astype(jnp.float32), None)
    summed, _ = lax.scan(add_group, jnp.zeros((DS, DT), jnp.float32), jnp.arange(N_CONTEXT, dtype=jnp.int32))
    proj_grad = summed * (1.0 / math.sqrt(LENGTH))
    return (proj_grad, distill_loss, input_history_new, weight_history_new)
```

```python
import functools
import math

import jax
import jax.numpy as jnp
from jax import lax
from jax.experimental import pallas as pl
from jax.experimental.pallas import tpu as pltpu
from jax.sharding import PartitionSpec as P

MESH = pl.DeviceIdType.MESH
F32, BF16 = jnp.float32, jnp.bfloat16
EPS = 1e-05
COPIES = 100
XROWS = 80


def lanes(tile):
    rows, width = tile.shape
    return [
        tile[r : r + 8, c : c + 128]
        for r in range(0, rows, 8)
        for c in range(0, width, 128)
    ]


def fold(op, tile):
    parts = lanes(tile)
    while len(parts) > 1:
        parts = [op(a, b) for a, b in zip(parts[::2], parts[1::2])] + (
            [parts[-1]] if len(parts) % 2 else []
        )
    return parts[0]


def kernel(
    tokens_all,
    hist_in, hist_w, stu_gain, tea_gain, tin, resid, wo, stu, proj,
    grad, hist_in_new, hist_w_new, loss,
    T, W, S, PR, R, H, M, E, psend, precv, sraw, wraw, col, sq, scal, sib, rs, st,
    ssem, rsem, lsem,
):
    t, c = lax.axis_index("tensor"), lax.axis_index("context")
    y, xl = t // 2, t % 2
    xh, z, k = c // 8, (c // 2) % 4, c % 2

    def dev(dy=0, dxl=0, dxh=0, dz=0, dk=0):
        ny, nz = (y + dy) % 4, (z + dz) % 4
        nxl, nxh, nk = (xl + dxl) % 2, (xh + dxh) % 2, (k + dk) % 2
        return {"tensor": ny * 2 + nxl, "context": nxh * 8 + nz * 2 + nk}

    sends = []

    def send(src, dst, **to):
        i = len(sends)
        copy = pltpu.make_async_remote_copy(
            src_ref=src,
            dst_ref=dst,
            send_sem=ssem.at[i],
            recv_sem=rsem.at[i],
            device_id=dev(**to),
            device_id_type=MESH,
        )
        copy.start()
        sends.append(copy)
        return copy

    local = []

    def load(src, dst):
        copy = pltpu.make_async_copy(src, dst, lsem.at[len(local)])
        copy.start()
        local.append(copy)
        return copy

    TENSOR = [(dy, dx) for dy in range(4) for dx in range(2) if (dy, dx) != (0, 0)]
    CONTEXT = [(dx, dz) for dx in range(2) for dz in range(4) if (dx, dz) != (0, 0)]
    UP, DOWN = 1, 3

    j_own = 2 * z + k
    slab = pl.multiple_of(64 * j_own, 64)
    l_proj = load(proj, PR.at[pl.ds(pl.multiple_of(256 * c, 256), 256)])
    l_stu = load(stu, sraw)
    l_wraw = load(wo.at[pl.ds(slab, 64)], wraw)
    l_tin = load(tin, T.at[:, pl.ds(0, 512)])
    l_wown = load(wo.at[:, pl.ds(pl.multiple_of(2048 * y, 2048), 2048)], W.at[0])
    l_res = load(resid, R)

    barrier = pltpu.get_barrier_semaphore()
    for dy, dx in TENSOR:
        pl.semaphore_signal(barrier, 1, device_id=dev(dy=dy, dxl=dx), device_id_type=MESH)
    for dx, dz in CONTEXT:
        pl.semaphore_signal(barrier, 1, device_id=dev(dxh=dx, dz=dz), device_id_type=MESH)
    pl.semaphore_signal(barrier, 1, device_id=dev(dk=1), device_id_type=MESH)

    lim_in, lim_w = hist_in[0], hist_w[0]
    for i in range(1, 16):
        lim_in = jnp.maximum(lim_in, hist_in[i])
        lim_w = jnp.maximum(lim_w, hist_w[i])

    l_stu.wait()

    @pl.loop(0, 8)
    def _(i):
        rows = pl.ds(pl.multiple_of(16 * i, 16), 16)
        v = sraw[rows, :].astype(F32)
        mean = jnp.mean(v * v, axis=1, keepdims=True)
        S[0, rows, :] = (v * lax.rsqrt(mean + EPS) * stu_gain[...]).astype(BF16)

    pl.semaphore_wait(barrier, len(TENSOR) + len(CONTEXT) + 1)

    nx = XROWS
    ny = 128 - nx
    own_x, own_y = pl.ds(0, nx), pl.ds(nx, ny)
    far_x, far_y = pl.ds(128, nx), pl.ds(128 + nx, ny)
    sy_up = send(S.at[0, own_y], S.at[3, own_y], dy=UP)
    sy_dn = send(S.at[0, own_y], S.at[1, own_y], dy=DOWN)
    l_proj.wait()

    def pblock(dxh=0, dz=0):
        at = ((xh + dxh) % 2) * 8 + ((z + dz) % 4) * 2 + k
        return PR.at[pl.ds(pl.multiple_of(256 * at, 256), 256)]

    p_x = send(pblock(), pblock(), dxh=1)
    p_up = send(pblock(), pblock(), dz=UP)
    p_dn = send(pblock(), pblock(), dz=DOWN)
    p_sib = [send(pblock(), pblock(), dk=1)]
    sx = send(S.at[0, own_x], S.at[0, far_x], dxl=1)
    sxy = [send(S.at[0, own_y], S.at[0, far_y], dxl=1)]

    l_wraw.wait()

    def clip_w(i, amax):
        rows = pl.ds(pl.multiple_of(16 * i, 16), 16)
        for n in range(8):
            cols = pl.ds(1024 * n, 1024)
            v = wraw[rows, cols].astype(F32)
            amax = jnp.maximum(amax, fold(jnp.maximum, jnp.abs(v)))
            wraw[rows, cols] = jnp.clip(v, -lim_w, lim_w).astype(BF16)
        return amax

    amax_w = lax.fori_loop(0, 4, clip_w, jnp.zeros((8, 128), F32))

    def wcols(d):
        return pl.ds(pl.multiple_of(2048 * ((y + d) % 4), 2048), 2048)

    w_y = [
        send(wraw.at[:, wcols(d)], W.at[4 - d, pl.ds(slab, 64)], dy=d) for d in (1, 3, 2)
    ]

    l_tin.wait()

    def clip_t(i, amax):
        rows = pl.ds(pl.multiple_of(32 * i, 32), 32)
        v = T[rows, pl.ds(0, 512)].astype(F32)
        T[rows, pl.ds(0, 512)] = jnp.clip(v, -lim_in, lim_in).astype(BF16)
        return jnp.maximum(amax, fold(jnp.maximum, jnp.abs(v)))

    amax_in = lax.fori_loop(0, 32, clip_t, jnp.zeros((8, 128), F32))

    def tblock(r, rows=None):
        return T.at[pl.ds(0, 1024) if rows is None else rows, pl.ds(512 * r, 512)]

    t_up = send(tblock(0), tblock(3), dy=UP)
    t_dn = send(tblock(0), tblock(1), dy=DOWN)

    left, right = pl.ds(0, 2048), pl.ds(2048, 2048)
    sy_up.wait_recv()
    sy_up2 = send(S.at[3, own_y, left], S.at[2, own_y, left], dy=UP)
    sxy.append(send(S.at[3, own_y], S.at[3, far_y], dxl=1))
    sy_dn.wait_recv()
    sy_dn2 = send(S.at[1, own_y, right], S.at[2, own_y, right], dy=DOWN)
    sxy.append(send(S.at[1, own_y], S.at[1, far_y], dxl=1))

    p_x.wait_recv()
    q_up = send(pblock(1), pblock(1), dz=UP)
    q_dn = send(pblock(1), pblock(1), dz=DOWN)
    p_sib.append(send(pblock(1), pblock(1), dk=1))

    def wslab(dz=0, half=None):
        at = pl.multiple_of(64 * (2 * ((z + dz) % 4) + k), 64)
        if half is None:
            return W.at[pl.ds(1, 3), pl.ds(at, 64)]
        return W.at[pl.ds(1, 3), pl.ds(pl.multiple_of(at + 32 * half, 32), 32)]

    for copy in w_y:
        copy.wait_recv()
    w_up = send(wslab(), wslab(), dz=UP)
    w_dn = send(wslab(), wslab(), dz=DOWN)
    w_sib = [send(wslab(), wslab(), dk=1)]

    l_wown.wait()

    @pl.loop(0, 32)
    def _(i):
        rows = pl.ds(pl.multiple_of(16 * i, 16), 16)
        v = W[0, rows, :].astype(F32)
        W[0, rows, :] = jnp.clip(v, -lim_w, lim_w).astype(BF16)

    p_up.wait_recv()
    p_up2 = send(pblock(0, DOWN), pblock(0, DOWN), dz=UP)
    p_sib.append(send(pblock(0, DOWN), pblock(0, DOWN), dk=1))
    p_dn.wait_recv()
    p_sib.append(send(pblock(0, UP), pblock(0, UP), dk=1))
    sy_up2.wait_recv()
    sy_dn2.wait_recv()
    sxy.append(send(S.at[2, own_y], S.at[2, far_y], dxl=1))

    w_up.wait_recv()
    w_up2 = send(wslab(DOWN, 0), wslab(DOWN, 0), dz=UP)
    w_sib.append(send(wslab(DOWN), wslab(DOWN), dk=1))
    w_dn.wait_recv()
    w_dn2 = send(wslab(UP, 1), wslab(UP, 1), dz=DOWN)
    w_sib.append(send(wslab(UP), wslab(UP), dk=1))

    t_up.wait_recv()
    t_up2 = send(tblock(3, pl.ds(0, 512)), tblock(2, pl.ds(0, 512)), dy=UP)
    t_dn.wait_recv()
    t_dn2 = send(tblock(1, pl.ds(512, 512)), tblock(2, pl.ds(512, 512)), dy=DOWN)

    a_up = send(S.at[0, own_x], S.at[3, own_x], dy=UP)
    a_dn = send(S.at[0, own_x], S.at[1, own_x], dy=DOWN)
    sx.wait_recv()
    b_up = send(S.at[0, far_x], S.at[3, far_x], dy=UP)
    b_dn = send(S.at[0, far_x], S.at[1, far_x], dy=DOWN)

    q_dn.wait_recv()
    q_dn2 = send(pblock(1, UP), pblock(1, UP), dz=DOWN)
    p_sib.append(send(pblock(1, UP), pblock(1, UP), dk=1))
    q_up.wait_recv()
    p_sib.append(send(pblock(1, DOWN), pblock(1, DOWN), dk=1))
    w_up2.wait_recv()
    w_dn2.wait_recv()
    w_sib.append(send(wslab(2), wslab(2), dk=1))
    p_up2.wait_recv()
    p_sib.append(send(pblock(0, 2), pblock(0, 2), dk=1))
    q_dn2.wait_recv()
    p_sib.append(send(pblock(1, 2), pblock(1, 2), dk=1))

    for copy in w_sib:
        copy.wait_recv()
    t_up2.wait_recv()
    t_dn2.wait_recv()

    def product(rows, col0, n):
        cols = pl.ds(pl.multiple_of(col0 + 256 * n, 256), 256)
        w = W[:, :, cols].reshape(2048, 256)
        return jnp.dot(T[rows, :], w, preferred_element_type=F32)

    rs_t = []
    for q in range(4):
        rows = pl.ds(256 * q, 256)

        @pl.loop(0, 4)
        def _(n):
            cols = pl.ds(pl.multiple_of(256 * n, 256), 256)
            psend[rows, cols] = product(rows, 1024 * (1 - xl), n).astype(BF16)

        rs_t.append(send(psend.at[rows], precv.at[rows], dxl=1))

    a_up.wait_recv()
    a_up2 = send(S.at[3, own_x], S.at[2, own_x], dy=UP)

    l_res.wait()
    for q in range(4):
        rows = pl.ds(256 * q, 256)

        @pl.loop(0, 4)
        def _(n):
            cols = pl.ds(pl.multiple_of(256 * n, 256), 256)
            H[rows, cols] = product(rows, 1024 * xl, n) + R[rows, cols].astype(F32)

    b_dn.wait_recv()
    b_dn2 = send(S.at[1, far_x], S.at[2, far_x], dy=DOWN)

    def mapped(r):
        @pl.loop(0, 4)
        def _(n):
            cols = pl.ds(pl.multiple_of(256 * n, 256), 256)
            M[pl.ds(256 * r, 256), cols] = jnp.dot(
                S[r], PR[:, cols], preferred_element_type=F32
            )

    for copy in p_sib:
        copy.wait_recv()
    sxy[0].wait_recv()
    mapped(0)

    for q in range(4):
        rs_t[q].wait_recv()

        @pl.loop(0, 16)
        def _(i):
            rows = pl.ds(pl.multiple_of(256 * q + 16 * i, 16), 16)
            h = H[rows, :] + precv[rows, :].astype(F32)
            H[rows, :] = h
            col[rows, :] = jnp.broadcast_to(jnp.sum(h * h, axis=1, keepdims=True), (16, 128))

    sq[0] = col[...].T[0:8, :]
    sq_c = [send(sq.at[0], sq.at[dy * 2 + dx], dy=dy, dxl=dx) for dy, dx in TENSOR]

    a_dn.wait_recv()
    b_up.wait_recv()
    sxy[1].wait_recv()
    mapped(3)
    sxy[2].wait_recv()
    mapped(1)

    for copy in sq_c:
        copy.wait_recv()
    total = sq[0]
    for i in range(1, 8):
        total = total + sq[i]
    inv = lax.rsqrt(total * (1.0 / 8192) + EPS)
    col[...] = jnp.broadcast_to(inv[0:1, :], (128, 1024)).T

    gains = tea_gain[:, pl.ds(pl.multiple_of(1024 * t, 1024), 1024)]

    def errors(r, acc):
        for b in range(2):
            base = 128 * (2 * ((y + r) % 4) + (xl + b) % 2)

            def step(i, acc):
                there = pl.ds(pl.multiple_of(base + 16 * i, 16), 16)
                here = pl.ds(pl.multiple_of(256 * r + 128 * b + 16 * i, 16), 16)
                scale = jnp.concatenate([col[there, :]] * 8, axis=1)
                e = M[here, :] - H[there, :] * scale * gains
                E[here, :] = e.astype(BF16)
                return acc + fold(jnp.add, e * e)

            acc = lax.fori_loop(0, 8, step, acc)
        return acc

    acc = jnp.zeros((8, 128), F32)
    for r in (0, 3, 1):
        acc = errors(r, acc)
    a_up2.wait_recv()
    b_dn2.wait_recv()
    sxy[3].wait_recv()
    mapped(2)
    acc = errors(2, acc)

    row = lax.broadcasted_iota(jnp.int32, (8, 128), 0)
    tile = jnp.where(row == 0, jnp.max(amax_in), jnp.where(row == 1, jnp.max(amax_w), jnp.sum(acc)))

    def merge(first, count):
        out = scal[first]
        for i in range(1, count):
            v = scal[first + i]
            out = jnp.where(row < 2, jnp.maximum(out, v), out + v)
        return out

    scal[t] = tile
    sc1 = [send(scal.at[t], scal.at[t], dy=dy, dxl=dx) for dy, dx in TENSOR]

    for copy in w_up, w_dn, w_up2, w_dn2, *w_sib:
        copy.wait_send()

    def gslot(g, other):
        return W.at[g // 2, pl.ds(256 * (g % 2), 256), pl.ds(1024 * other, 1024)]

    def term(g, dxh, dz, other):
        dest = ((xh + dxh) % 2) * 8 + ((z + dz) % 4) * 2 + (k + other) % 2
        cols = pl.ds(pl.multiple_of(256 * dest, 256), 256)
        st[...] = S[:, :, cols].reshape(1024, 256).T

        @pl.loop(0, 4)
        def _(n):
            at = pl.multiple_of(256 * n, 256)
            W[g // 2, pl.ds(256 * (g % 2), 256), pl.ds(pl.multiple_of(1024 * other + at, 256), 256)] = jnp.dot(
                st[...], E[:, pl.ds(at, 256)], preferred_element_type=F32
            ).astype(BF16)

    ORDER = [(1, 2), (1, 1), (1, 3), (0, 2), (1, 0), (0, 1), (0, 3), (0, 0)]
    to_sib, out_c = [], []

    def finish(g):
        dxh, dz = ORDER[g]
        to_sib[g].wait_recv()

        @pl.loop(0, 16)
        def _(i):
            rows = pl.ds(pl.multiple_of(256 * (g % 2) + 16 * i, 16), 16)
            from_sib = sib[g, pl.ds(pl.multiple_of(16 * i, 16), 16), :].astype(F32)
            both = W[g // 2, rows, pl.ds(0, 1024)].astype(F32) + from_sib
            W[g // 2, rows, pl.ds(0, 1024)] = both.astype(BF16)

        if g < 7:
            out_c.append(send(gslot(g, 0), rs.at[g], dxh=dxh, dz=dz))

    sc2 = None
    for g, (dxh, dz) in enumerate(ORDER):
        term(g, dxh, dz, 1)
        to_sib.append(send(gslot(g, 1), sib.at[g], dk=1))
        term(g, dxh, dz, 0)
        if g > 0:
            finish(g - 1)
        if g == 3:
            for copy in sc1:
                copy.wait_recv()
            at = 8 + xh * 4 + z
            scal[at] = merge(0, 8)
            sc2 = [send(scal.at[at], scal.at[at], dxh=dx, dz=dz_) for dx, dz_ in CONTEXT]
    finish(7)

    for copy in sc2:
        copy.wait_recv()
    scal[16 + k] = merge(8, 8)
    sc3 = send(scal.at[16 + k], scal.at[16 + k], dk=1)

    for copy in out_c:
        copy.wait_recv()
    scale = 1.0 / math.sqrt(tokens_all)

    @pl.loop(0, 16)
    def _(i):
        rows = pl.ds(pl.multiple_of(16 * i, 16), 16)
        total = W[3, pl.ds(pl.multiple_of(256 + 16 * i, 16), 16), pl.ds(0, 1024)].astype(F32)
        for g in range(7):
            total = total + rs[g, rows, :].astype(F32)
        grad[rows, :] = total * scale

    sc3.wait_recv()
    final = merge(16, 2)
    hist_in_new[0] = jnp.max(jnp.where(row == 0, final, 0.0))
    hist_w_new[0] = jnp.max(jnp.where(row == 1, final, 0.0))
    loss[0] = jnp.max(jnp.where(row == 2, final, 0.0)) * (0.5 / (tokens_all * 8192))
    for i in range(15):
        hist_in_new[i + 1] = hist_in[i]
        hist_w_new[i + 1] = hist_w[i]

    waited = [w_up, w_dn, w_up2, w_dn2, *w_sib]
    for copy in sends:
        if not any(copy is w for w in waited):
            copy.wait_send()


def local(
    teacher_in, teacher_resid, teacher_wo, teacher_gain, input_history, weight_history,
    student_hidden, student_gain, projection,
):
    tokens_all = teacher_in.shape[0] * lax.axis_size("context")
    smem = pl.BlockSpec(memory_space=pltpu.SMEM)
    vmem = pl.BlockSpec(memory_space=pltpu.VMEM)
    hbm = pl.BlockSpec(memory_space=pl.ANY)
    grad, hist_in, hist_w, loss = pl.pallas_call(
        functools.partial(kernel, tokens_all),
        name="distill",
        out_shape=(
            jax.ShapeDtypeStruct((256, 1024), F32),
            jax.ShapeDtypeStruct((16,), F32),
            jax.ShapeDtypeStruct((16,), F32),
            jax.ShapeDtypeStruct((1,), F32),
        ),
        in_specs=[smem, smem, vmem, vmem, hbm, hbm, hbm, hbm, hbm],
        out_specs=(vmem, smem, smem, smem),
        scratch_shapes=[
            pltpu.VMEM((1024, 2048), BF16),
            pltpu.VMEM((4, 512, 2048), BF16),
            pltpu.VMEM((4, 256, 4096), BF16),
            pltpu.VMEM((4096, 1024), BF16),
            pltpu.VMEM((1024, 1024), BF16),
            pltpu.VMEM((1024, 1024), F32),
            pltpu.VMEM((1024, 1024), F32),
            pltpu.VMEM((1024, 1024), BF16),
            pltpu.VMEM((1024, 1024), BF16),
            pltpu.VMEM((1024, 1024), BF16),
            pltpu.VMEM((128, 4096), BF16),
            pltpu.VMEM((64, 8192), BF16),
            pltpu.VMEM((1024, 128), F32),
            pltpu.VMEM((8, 8, 1024), F32),
            pltpu.VMEM((18, 8, 128), F32),
            pltpu.VMEM((8, 256, 1024), BF16),
            pltpu.VMEM((7, 256, 1024), BF16),
            pltpu.VMEM((256, 1024), BF16),
            pltpu.SemaphoreType.DMA((COPIES,)),
            pltpu.SemaphoreType.DMA((COPIES,)),
            pltpu.SemaphoreType.DMA((6,)),
        ],
        compiler_params=pltpu.CompilerParams(
            collective_id=0, has_side_effects=True, vmem_limit_bytes=62 << 20
        ),
        cost_estimate=pl.CostEstimate(
            flops=3 * 2 * 1024 * 1024 * 4096, bytes_accessed=16 << 20, transcendentals=1024
        ),
    )(
        input_history,
        weight_history,
        student_gain.reshape(1, -1),
        teacher_gain.reshape(1, -1),
        teacher_in,
        teacher_resid,
        teacher_wo,
        student_hidden,
        projection,
    )
    return grad, loss.reshape(()), hist_in, hist_w


def solution(mesh):
    placed = (
        P("context", "tensor"),
        P("context", "tensor"),
        P("tensor", None),
        P(),
        P(),
        P(),
        P(("context", "tensor"), None),
        P(),
        P("context", "tensor"),
    )
    return jax.shard_map(
        local,
        mesh=mesh,
        in_specs=placed,
        out_specs=(P("context", "tensor"), P(), P(), P()),
        check_vma=False,
    )
```

```python
import functools
import math

import jax
import jax.numpy as jnp
from jax import lax
from jax.experimental import pallas as pl
from jax.experimental.pallas import tpu as pltpu
from jax.sharding import PartitionSpec as P

MESH = pl.DeviceIdType.MESH
F32, BF16 = jnp.float32, jnp.bfloat16
EPS = 1e-05
COPIES = 100
XROWS = 96
ACOLS = 640


def lanes(tile):
    rows, width = tile.shape
    return [
        tile[r : r + 8, c : c + 128]
        for r in range(0, rows, 8)
        for c in range(0, width, 128)
    ]


def fold(op, tile):
    parts = lanes(tile)
    while len(parts) > 1:
        parts = [op(a, b) for a, b in zip(parts[::2], parts[1::2])] + (
            [parts[-1]] if len(parts) % 2 else []
        )
    return parts[0]


def kernel(
    tokens_all,
    hist_in, hist_w, stu_gain, tea_gain, tin, resid, wo, stu, proj,
    grad, hist_in_new, hist_w_new, loss,
    T, W, S, PR, R, H, M, E, psend, precv, sraw, wraw, col, sq, scal, sib, ra1, ra2, rb1, rb2, st,
    ssem, rsem, lsem,
):
    t, c = lax.axis_index("tensor"), lax.axis_index("context")
    y, xl = t // 2, t % 2
    xh, z, k = c // 8, (c // 2) % 4, c % 2

    def dev(dy=0, dxl=0, dxh=0, dz=0, dk=0):
        ny, nz = (y + dy) % 4, (z + dz) % 4
        nxl, nxh, nk = (xl + dxl) % 2, (xh + dxh) % 2, (k + dk) % 2
        return {"tensor": ny * 2 + nxl, "context": nxh * 8 + nz * 2 + nk}

    sends = []

    def send(src, dst, **to):
        i = len(sends)
        copy = pltpu.make_async_remote_copy(
            src_ref=src,
            dst_ref=dst,
            send_sem=ssem.at[i],
            recv_sem=rsem.at[i],
            device_id=dev(**to),
            device_id_type=MESH,
        )
        copy.start()
        sends.append(copy)
        return copy

    local = []

    def load(src, dst):
        copy = pltpu.make_async_copy(src, dst, lsem.at[len(local)])
        copy.start()
        local.append(copy)
        return copy

    TENSOR = [(dy, dx) for dy in range(4) for dx in range(2) if (dy, dx) != (0, 0)]
    CONTEXT = [(dx, dz) for dx in range(2) for dz in range(4) if (dx, dz) != (0, 0)]
    UP, DOWN = 1, 3

    slab = pl.multiple_of(64 * (2 * z + k), 64)
    l_wraw = load(wo.at[pl.ds(slab, 64)], wraw)
    l_stu = load(stu, sraw)
    l_proj = load(proj, PR.at[pl.ds(pl.multiple_of(256 * c, 256), 256)])
    l_tin = load(tin, T.at[:, pl.ds(0, 512)])
    l_wown = load(wo.at[:, pl.ds(pl.multiple_of(2048 * y, 2048), 2048)], W.at[0])
    l_res = load(resid, R)

    barrier = pltpu.get_barrier_semaphore()
    for dy, dx in TENSOR:
        pl.semaphore_signal(barrier, 1, device_id=dev(dy=dy, dxl=dx), device_id_type=MESH)
    for dx, dz in CONTEXT:
        pl.semaphore_signal(barrier, 1, device_id=dev(dxh=dx, dz=dz), device_id_type=MESH)
    pl.semaphore_signal(barrier, 1, device_id=dev(dk=1), device_id_type=MESH)

    lim_in, lim_w = hist_in[0], hist_w[0]
    for i in range(1, 16):
        lim_in = jnp.maximum(lim_in, hist_in[i])
        lim_w = jnp.maximum(lim_w, hist_w[i])

    l_wraw.wait()

    def clip_w(i, amax):
        rows = pl.ds(pl.multiple_of(16 * i, 16), 16)
        for n in range(8):
            cols = pl.ds(1024 * n, 1024)
            v = wraw[rows, cols].astype(F32)
            amax = jnp.maximum(amax, fold(jnp.maximum, jnp.abs(v)))
            wraw[rows, cols] = jnp.clip(v, -lim_w, lim_w).astype(BF16)
        return amax

    amax_w = lax.fori_loop(0, 4, clip_w, jnp.zeros((8, 128), F32))

    l_stu.wait()

    @pl.loop(0, 8)
    def _(i):
        rows = pl.ds(pl.multiple_of(16 * i, 16), 16)
        v = sraw[rows, :].astype(F32)
        mean = jnp.mean(v * v, axis=1, keepdims=True)
        S[0, rows, :] = (v * lax.rsqrt(mean + EPS) * stu_gain[...]).astype(BF16)

    pl.semaphore_wait(barrier, len(TENSOR) + len(CONTEXT) + 1)

    nx = XROWS
    ny = 128 - nx
    own_x, own_y = pl.ds(0, nx), pl.ds(nx, ny)
    far_x, far_y = pl.ds(128, nx), pl.ds(128 + nx, ny)
    sy_up = send(S.at[0, own_y], S.at[3, own_y], dy=UP)
    sy_dn = send(S.at[0, own_y], S.at[1, own_y], dy=DOWN)

    def wcols(d):
        return pl.ds(pl.multiple_of(2048 * ((y + d) % 4), 2048), 2048)

    w_y = [
        send(wraw.at[:, wcols(d)], W.at[4 - d, pl.ds(slab, 64)], dy=d) for d in (2, 1, 3)
    ]
    l_proj.wait()

    def pblock(dxh=0, dz=0):
        at = ((xh + dxh) % 2) * 8 + ((z + dz) % 4) * 2 + k
        return PR.at[pl.ds(pl.multiple_of(256 * at, 256), 256)]

    p_x = send(pblock(), pblock(), dxh=1)
    p_up = send(pblock(), pblock(), dz=UP)
    p_dn = send(pblock(), pblock(), dz=DOWN)
    p_sib = [send(pblock(), pblock(), dk=1)]
    sx = send(S.at[0, own_x], S.at[0, far_x], dxl=1)
    sxy = [send(S.at[0, own_y], S.at[0, far_y], dxl=1)]

    l_tin.wait()

    def clip_t(i, amax):
        rows = pl.ds(pl.multiple_of(32 * i, 32), 32)
        v = T[rows, pl.ds(0, 512)].astype(F32)
        T[rows, pl.ds(0, 512)] = jnp.clip(v, -lim_in, lim_in).astype(BF16)
        return jnp.maximum(amax, fold(jnp.maximum, jnp.abs(v)))

    amax_in = lax.fori_loop(0, 32, clip_t, jnp.zeros((8, 128), F32))

    left, right = pl.ds(0, 2048), pl.ds(2048, 2048)
    sy_up.wait_recv()
    sy_up2 = send(S.at[3, own_y, left], S.at[2, own_y, left], dy=UP)
    sxy.append(send(S.at[3, own_y], S.at[3, far_y], dxl=1))
    sy_dn.wait_recv()
    sy_dn2 = send(S.at[1, own_y, right], S.at[2, own_y, right], dy=DOWN)
    sxy.append(send(S.at[1, own_y], S.at[1, far_y], dxl=1))

    low, high = pl.ds(0, 512), pl.ds(512, 512)

    def tblock(r, rows):
        return T.at[rows, pl.ds(512 * r, 512)]

    t_up = send(tblock(0, low), tblock(3, low), dy=UP)
    t_dn = send(tblock(0, high), tblock(1, high), dy=DOWN)
    t_up1 = send(tblock(0, high), tblock(3, high), dy=UP)
    t_dn1 = send(tblock(0, low), tblock(1, low), dy=DOWN)

    def wslab(dz=0, half=None):
        at = pl.multiple_of(64 * (2 * ((z + dz) % 4) + k), 64)
        if half is None:
            return W.at[pl.ds(1, 3), pl.ds(at, 64)]
        return W.at[pl.ds(1, 3), pl.ds(pl.multiple_of(at + 32 * half, 32), 32)]

    p_x.wait_recv()
    p_sib.append(send(pblock(1), pblock(1), dk=1))
    for copy in w_y:
        copy.wait_recv()
    w_up = send(wslab(), wslab(), dz=UP)
    w_dn = send(wslab(), wslab(), dz=DOWN)
    w_sib = [send(wslab(), wslab(), dk=1)]

    l_wown.wait()

    @pl.loop(0, 32)
    def _(i):
        rows = pl.ds(pl.multiple_of(16 * i, 16), 16)
        v = W[0, rows, :].astype(F32)
        W[0, rows, :] = jnp.clip(v, -lim_w, lim_w).astype(BF16)

    sy_up2.wait_recv()
    sy_dn2.wait_recv()
    sxy.append(send(S.at[2, own_y], S.at[2, far_y], dxl=1))

    t_up.wait_recv()
    t_up2 = send(tblock(3, low), tblock(2, low), dy=UP)
    t_dn.wait_recv()
    t_dn2 = send(tblock(1, high), tblock(2, high), dy=DOWN)
    a_up = send(S.at[0, own_x], S.at[3, own_x], dy=UP)
    sx.wait_recv()
    b_dn = send(S.at[0, far_x], S.at[1, far_x], dy=DOWN)
    b_up = send(S.at[0, far_x], S.at[3, far_x], dy=UP)
    a_dn = send(S.at[0, own_x], S.at[1, own_x], dy=DOWN)

    w_up.wait_recv()
    w_up2 = send(wslab(DOWN, 0), wslab(DOWN, 0), dz=UP)
    w_sib.append(send(wslab(DOWN), wslab(DOWN), dk=1))
    w_dn.wait_recv()
    w_dn2 = send(wslab(UP, 1), wslab(UP, 1), dz=DOWN)
    w_sib.append(send(wslab(UP), wslab(UP), dk=1))
    q_dn = send(pblock(1), pblock(1), dz=DOWN)
    q_up = send(pblock(1), pblock(1), dz=UP)
    p_up.wait_recv()
    p_up2 = send(pblock(0, DOWN), pblock(0, DOWN), dz=UP)
    p_sib.append(send(pblock(0, DOWN), pblock(0, DOWN), dk=1))
    p_dn.wait_recv()
    p_sib.append(send(pblock(0, UP), pblock(0, UP), dk=1))
    w_up2.wait_recv()
    w_dn2.wait_recv()
    w_sib.append(send(wslab(2), wslab(2), dk=1))

    for copy in t_up1, t_dn1, t_up2, t_dn2, *w_sib:
        copy.wait_recv()

    def product(rows, col0, n):
        cols = pl.ds(pl.multiple_of(col0 + 256 * n, 256), 256)
        w = W[:, :, cols].reshape(2048, 256)
        return jnp.dot(T[rows, :], w, preferred_element_type=F32)

    rs_t = []
    for q in range(4):
        rows = pl.ds(256 * q, 256)

        @pl.loop(0, 4)
        def _(n):
            cols = pl.ds(pl.multiple_of(256 * n, 256), 256)
            psend[rows, cols] = product(rows, 1024 * (1 - xl), n).astype(BF16)

        rs_t.append(send(psend.at[rows], precv.at[rows], dxl=1))
        if q == 1:
            q_dn.wait_recv()
            q_dn2 = send(pblock(1, UP), pblock(1, UP), dz=DOWN)
            p_sib.append(send(pblock(1, UP), pblock(1, UP), dk=1))
            q_up.wait_recv()
            p_sib.append(send(pblock(1, DOWN), pblock(1, DOWN), dk=1))

    l_res.wait()
    for q in range(4):
        rows = pl.ds(256 * q, 256)

        @pl.loop(0, 4)
        def _(n):
            cols = pl.ds(pl.multiple_of(256 * n, 256), 256)
            H[rows, cols] = product(rows, 1024 * xl, n) + R[rows, cols].astype(F32)

    p_up2.wait_recv()
    p_sib.append(send(pblock(0, 2), pblock(0, 2), dk=1))
    q_dn2.wait_recv()
    p_sib.append(send(pblock(1, 2), pblock(1, 2), dk=1))
    a_up.wait_recv()
    a_up2 = send(S.at[3, own_x], S.at[2, own_x], dy=UP)
    b_dn.wait_recv()
    b_dn2 = send(S.at[1, far_x], S.at[2, far_x], dy=DOWN)

    def mapped(r):
        @pl.loop(0, 4)
        def _(n):
            cols = pl.ds(pl.multiple_of(256 * n, 256), 256)
            M[pl.ds(256 * r, 256), cols] = jnp.dot(
                S[r], PR[:, cols], preferred_element_type=F32
            )

    def squares(q):
        rs_t[q].wait_recv()

        @pl.loop(0, 16)
        def _(i):
            rows = pl.ds(pl.multiple_of(256 * q + 16 * i, 16), 16)
            h = H[rows, :] + precv[rows, :].astype(F32)
            H[rows, :] = h
            col[rows, :] = jnp.broadcast_to(jnp.sum(h * h, axis=1, keepdims=True), (16, 128))

    for copy in p_sib:
        copy.wait_recv()
    sxy[0].wait_recv()
    mapped(0)
    squares(0)
    squares(1)
    squares(2)
    b_up.wait_recv()
    sxy[1].wait_recv()
    mapped(3)
    a_dn.wait_recv()
    sxy[2].wait_recv()
    mapped(1)
    squares(3)
    sq[0] = col[...].T[0:8, :]
    sq_c = [send(sq.at[0], sq.at[dy * 2 + dx], dy=dy, dxl=dx) for dy, dx in TENSOR]
    for copy in sq_c:
        copy.wait_recv()
    total = sq[0]
    for i in range(1, 8):
        total = total + sq[i]
    inv = lax.rsqrt(total * (1.0 / 8192) + EPS)
    col[...] = jnp.broadcast_to(inv[0:1, :], (128, 1024)).T

    gains = tea_gain[:, pl.ds(pl.multiple_of(1024 * t, 1024), 1024)]

    def errors(r, acc):
        for b in range(2):
            base = 128 * (2 * ((y + r) % 4) + (xl + b) % 2)

            def step(i, acc):
                there = pl.ds(pl.multiple_of(base + 16 * i, 16), 16)
                here = pl.ds(pl.multiple_of(256 * r + 128 * b + 16 * i, 16), 16)
                scale = jnp.concatenate([col[there, :]] * 8, axis=1)
                e = M[here, :] - H[there, :] * scale * gains
                E[here, :] = e.astype(BF16)
                return acc + fold(jnp.add, e * e)

            acc = lax.fori_loop(0, 8, step, acc)
        return acc

    acc = jnp.zeros((8, 128), F32)
    for r in (0, 3, 1):
        acc = errors(r, acc)
    a_up2.wait_recv()
    b_dn2.wait_recv()
    sxy[3].wait_recv()
    mapped(2)
    acc = errors(2, acc)

    row = lax.broadcasted_iota(jnp.int32, (8, 128), 0)
    tile = jnp.where(row == 0, jnp.max(amax_in), jnp.where(row == 1, jnp.max(amax_w), jnp.sum(acc)))

    def merge(first, count):
        out = scal[first]
        for i in range(1, count):
            v = scal[first + i]
            out = jnp.where(row < 2, jnp.maximum(out, v), out + v)
        return out

    scal[t] = tile
    sc1 = [send(scal.at[t], scal.at[t], dy=dy, dxl=dx) for dy, dx in TENSOR]

    for copy in w_up, w_dn, w_up2, w_dn2, *w_sib:
        copy.wait_send()

    ORDER = [(1, 2), (0, 2), (1, 1), (0, 1), (1, 3), (0, 3), (1, 0), (0, 0)]
    a_cols, b_cols = pl.ds(0, ACOLS), pl.ds(ACOLS, 1024 - ACOLS)

    def gslot(dxh, dz, cols):
        g = ORDER.index((dxh, dz))
        return W.at[g // 2, pl.ds(256 * (g % 2), 256), cols]

    to_sib, a_1, b_1, a_2 = [], {}, {}, {}

    def term(g):
        dxh, dz = ORDER[g]
        chip = ((xh + dxh) % 2) * 4 + (z + dz) % 4
        for other in (1, 0):
            cols = pl.ds(pl.multiple_of(512 * chip + 256 * ((k + other) % 2), 256), 256)
            st[pl.ds(256 * (1 - other), 256), :] = S[:, :, cols].reshape(1024, 256).T

        @pl.loop(0, 4)
        def _(n):
            at = pl.multiple_of(256 * n, 256)
            both = jnp.dot(st[...], E[:, pl.ds(at, 256)], preferred_element_type=F32).astype(BF16)
            rows = pl.ds(256 * (g % 2), 256)
            W[g // 2, rows, pl.ds(pl.multiple_of(1024 + at, 256), 256)] = both[:256]
            W[g // 2, rows, pl.ds(at, 256)] = both[256:]

        to_sib.append(send(gslot(dxh, dz, pl.ds(1024, 1024)), sib.at[g], dk=1))

    def add(dxh, dz, start, count, others):
        g = ORDER.index((dxh, dz))

        @pl.loop(0, 16)
        def _(i):
            here = pl.ds(pl.multiple_of(16 * i, 16), 16)
            rows = pl.ds(pl.multiple_of(256 * (g % 2) + 16 * i, 16), 16)
            cols = pl.ds(start, count)
            total = W[g // 2, rows, cols].astype(F32)
            for ref, index in others:
                total = total + ref[index, here, :].astype(F32)
            W[g // 2, rows, cols] = total.astype(BF16)

    def finish(g):
        dxh, dz = ORDER[g]
        to_sib[g].wait_recv()
        add(dxh, dz, 0, 1024, [(sib, g)])
        if dxh:
            a_1[dz] = send(gslot(dxh, dz, a_cols), ra1.at[dz], dxh=1)
        if dz:
            b_1[dxh, dz] = send(gslot(dxh, dz, b_cols), rb1.at[dxh * 3 + dz - 1], dz=dz)

    def second_a(dz):
        a_1[dz].wait_recv()
        add(0, dz, 0, ACOLS, [(ra1, dz)])
        if dz:
            a_2[dz] = send(gslot(0, dz, a_cols), ra2.at[dz - 1], dz=dz)

    for g in range(8):
        term(g)
        if g == 1:
            for copy in sc1:
                copy.wait_recv()
            at = 8 + xh * 4 + z
            scal[at] = merge(0, 8)
            sc2 = [send(scal.at[at], scal.at[at], dxh=dx, dz=dz) for dx, dz in CONTEXT]
        if g:
            finish(g - 1)
        if g == 4:
            second_a(2)
        if g == 6:
            second_a(1)
    finish(7)
    second_a(3)

    for copy in sc2:
        copy.wait_recv()
    scal[16 + k] = merge(8, 8)
    sc3 = send(scal.at[16 + k], scal.at[16 + k], dk=1)

    for dz in (1, 2, 3):
        b_1[1, dz].wait_recv()
    add(1, 0, ACOLS, 1024 - ACOLS, [(rb1, 3), (rb1, 4), (rb1, 5)])
    b_2 = send(gslot(1, 0, b_cols), rb2.at[0], dxh=1)
    second_a(0)

    for dz in (1, 2, 3):
        b_1[0, dz].wait_recv()
        a_2[dz].wait_recv()
    b_2.wait_recv()
    scale = 1.0 / math.sqrt(tokens_all)

    @pl.loop(0, 16)
    def _(i):
        rows = pl.ds(pl.multiple_of(16 * i, 16), 16)
        mine = pl.ds(pl.multiple_of(256 + 16 * i, 16), 16)
        total = W[3, mine, a_cols].astype(F32)
        for n in range(3):
            total = total + ra2[n, rows, :].astype(F32)
        grad[rows, a_cols] = total * scale
        total = W[3, mine, b_cols].astype(F32) + rb2[0, rows, :].astype(F32)
        for n in range(3):
            total = total + rb1[n, rows, :].astype(F32)
        grad[rows, b_cols] = total * scale

    sc3.wait_recv()
    final = merge(16, 2)
    hist_in_new[0] = jnp.max(jnp.where(row == 0, final, 0.0))
    hist_w_new[0] = jnp.max(jnp.where(row == 1, final, 0.0))
    loss[0] = jnp.max(jnp.where(row == 2, final, 0.0)) * (0.5 / (tokens_all * 8192))
    for i in range(15):
        hist_in_new[i + 1] = hist_in[i]
        hist_w_new[i + 1] = hist_w[i]

    waited = [w_up, w_dn, w_up2, w_dn2, *w_sib]
    for copy in sends:
        if not any(copy is w for w in waited):
            copy.wait_send()


def local(
    teacher_in, teacher_resid, teacher_wo, teacher_gain, input_history, weight_history,
    student_hidden, student_gain, projection,
):
    tokens_all = teacher_in.shape[0] * lax.axis_size("context")
    smem = pl.BlockSpec(memory_space=pltpu.SMEM)
    vmem = pl.BlockSpec(memory_space=pltpu.VMEM)
    hbm = pl.BlockSpec(memory_space=pl.ANY)
    grad, hist_in, hist_w, loss = pl.pallas_call(
        functools.partial(kernel, tokens_all),
        name="distill",
        out_shape=(
            jax.ShapeDtypeStruct((256, 1024), F32),
            jax.ShapeDtypeStruct((16,), F32),
            jax.ShapeDtypeStruct((16,), F32),
            jax.ShapeDtypeStruct((1,), F32),
        ),
        in_specs=[smem, smem, vmem, vmem, hbm, hbm, hbm, hbm, hbm],
        out_specs=(vmem, smem, smem, smem),
        scratch_shapes=[
            pltpu.VMEM((1024, 2048), BF16),
            pltpu.VMEM((4, 512, 2048), BF16),
            pltpu.VMEM((4, 256, 4096), BF16),
            pltpu.VMEM((4096, 1024), BF16),
            pltpu.VMEM((1024, 1024), BF16),
            pltpu.VMEM((1024, 1024), F32),
            pltpu.VMEM((1024, 1024), F32),
            pltpu.VMEM((1024, 1024), BF16),
            pltpu.VMEM((1024, 1024), BF16),
            pltpu.VMEM((1024, 1024), BF16),
            pltpu.VMEM((128, 4096), BF16),
            pltpu.VMEM((64, 8192), BF16),
            pltpu.VMEM((1024, 128), F32),
            pltpu.VMEM((8, 8, 1024), F32),
            pltpu.VMEM((18, 8, 128), F32),
            pltpu.VMEM((8, 256, 1024), BF16),
            pltpu.VMEM((4, 256, ACOLS), BF16),
            pltpu.VMEM((3, 256, ACOLS), BF16),
            pltpu.VMEM((6, 256, 1024 - ACOLS), BF16),
            pltpu.VMEM((1, 256, 1024 - ACOLS), BF16),
            pltpu.VMEM((512, 1024), BF16),
            pltpu.SemaphoreType.DMA((COPIES,)),
            pltpu.SemaphoreType.DMA((COPIES,)),
            pltpu.SemaphoreType.DMA((6,)),
        ],
        compiler_params=pltpu.CompilerParams(
            collective_id=0, has_side_effects=True, vmem_limit_bytes=62 << 20
        ),
        cost_estimate=pl.CostEstimate(
            flops=3 * 2 * 1024 * 1024 * 4096, bytes_accessed=16 << 20, transcendentals=1024
        ),
    )(
        input_history,
        weight_history,
        student_gain.reshape(1, -1),
        teacher_gain.reshape(1, -1),
        teacher_in,
        teacher_resid,
        teacher_wo,
        student_hidden,
        projection,
    )
    return grad, loss.reshape(()), hist_in, hist_w


def solution(mesh):
    placed = (
        P("context", "tensor"),
        P("context", "tensor"),
        P("tensor", None),
        P(),
        P(),
        P(),
        P(("context", "tensor"), None),
        P(),
        P("context", "tensor"),
    )
    return jax.shard_map(
        local,
        mesh=mesh,
        in_specs=placed,
        out_specs=(P("context", "tensor"), P(), P(), P()),
        check_vma=False,
    )
```

```python
import functools
import math

import jax
import jax.numpy as jnp
from jax import lax
from jax.experimental import pallas as pl
from jax.experimental.pallas import tpu as pltpu
from jax.sharding import PartitionSpec as P

MESH = pl.DeviceIdType.MESH
F32, BF16 = jnp.float32, jnp.bfloat16
EPS = 1e-05
COPIES = 100
XROWS = 96
ACOLS = 384


def lanes(tile):
    rows, width = tile.shape
    return [
        tile[r : r + 8, c : c + 128]
        for r in range(0, rows, 8)
        for c in range(0, width, 128)
    ]


def fold(op, tile):
    parts = lanes(tile)
    while len(parts) > 1:
        parts = [op(a, b) for a, b in zip(parts[::2], parts[1::2])] + (
            [parts[-1]] if len(parts) % 2 else []
        )
    return parts[0]


def kernel(
    tokens_all,
    hist_in, hist_w, stu_gain, tea_gain, tin, resid, wo, stu, proj,
    parts,
    T, W, S, PR, R, H, M, E, psend, precv, sraw, wraw, col, sq, scal, sib, ra1, ra2, rb1, rb2, am, bm, total_g,
    ssem, rsem, lsem,
):
    t, c = lax.axis_index("tensor"), lax.axis_index("context")
    y, xl = t // 2, t % 2
    xh, z, k = c // 8, (c // 2) % 4, c % 2

    def dev(dy=0, dxl=0, dxh=0, dz=0, dk=0):
        ny, nz = (y + dy) % 4, (z + dz) % 4
        nxl, nxh, nk = (xl + dxl) % 2, (xh + dxh) % 2, (k + dk) % 2
        return {"tensor": ny * 2 + nxl, "context": nxh * 8 + nz * 2 + nk}

    sends = []

    def send(src, dst, **to):
        i = len(sends)
        copy = pltpu.make_async_remote_copy(
            src_ref=src,
            dst_ref=dst,
            send_sem=ssem.at[i],
            recv_sem=rsem.at[i],
            device_id=dev(**to),
            device_id_type=MESH,
        )
        copy.start()
        sends.append(copy)
        return copy

    local = []

    def load(src, dst):
        copy = pltpu.make_async_copy(src, dst, lsem.at[len(local)])
        copy.start()
        local.append(copy)
        return copy

    TENSOR = [(dy, dx) for dy in range(4) for dx in range(2) if (dy, dx) != (0, 0)]
    CONTEXT = [(dx, dz) for dx in range(2) for dz in range(4) if (dx, dz) != (0, 0)]
    UP, DOWN = 1, 3

    slab = pl.multiple_of(64 * (2 * z + k), 64)
    l_wraw = load(wo.at[pl.ds(slab, 64)], wraw)
    l_stu = load(stu, sraw)
    l_proj = load(proj, PR.at[pl.ds(pl.multiple_of(256 * c, 256), 256)])
    l_tin = load(tin, T.at[:, pl.ds(0, 512)])
    l_wown = load(wo.at[:, pl.ds(pl.multiple_of(2048 * y, 2048), 2048)], W.at[0])
    l_res = load(resid, R)

    barrier = pltpu.get_barrier_semaphore()
    for dy, dx in TENSOR:
        pl.semaphore_signal(barrier, 1, device_id=dev(dy=dy, dxl=dx), device_id_type=MESH)
    for dx, dz in CONTEXT:
        pl.semaphore_signal(barrier, 1, device_id=dev(dxh=dx, dz=dz), device_id_type=MESH)
    pl.semaphore_signal(barrier, 1, device_id=dev(dk=1), device_id_type=MESH)

    lim_in, lim_w = hist_in[0], hist_w[0]
    for i in range(1, 16):
        lim_in = jnp.maximum(lim_in, hist_in[i])
        lim_w = jnp.maximum(lim_w, hist_w[i])

    l_wraw.wait()

    def clip_w(i, amax):
        rows = pl.ds(pl.multiple_of(16 * i, 16), 16)
        for n in range(8):
            cols = pl.ds(1024 * n, 1024)
            v = wraw[rows, cols].astype(F32)
            amax = jnp.maximum(amax, fold(jnp.maximum, jnp.abs(v)))
            wraw[rows, cols] = jnp.clip(v, -lim_w, lim_w).astype(BF16)
        return amax

    amax_w = lax.fori_loop(0, 4, clip_w, jnp.zeros((8, 128), F32))

    l_stu.wait()

    @pl.loop(0, 8)
    def _(i):
        rows = pl.ds(pl.multiple_of(16 * i, 16), 16)
        v = sraw[rows, :].astype(F32)
        mean = jnp.mean(v * v, axis=1, keepdims=True)
        S[0, rows, :] = (v * lax.rsqrt(mean + EPS) * stu_gain[...]).astype(BF16)

    pl.semaphore_wait(barrier, len(TENSOR) + len(CONTEXT) + 1)

    nx = XROWS
    ny = 128 - nx
    own_x, own_y = pl.ds(0, nx), pl.ds(nx, ny)
    far_x, far_y = pl.ds(128, nx), pl.ds(128 + nx, ny)
    sy_up = send(S.at[0, own_y], S.at[3, own_y], dy=UP)
    sy_dn = send(S.at[0, own_y], S.at[1, own_y], dy=DOWN)

    def wcols(d):
        return pl.ds(pl.multiple_of(2048 * ((y + d) % 4), 2048), 2048)

    w_y = [
        send(wraw.at[:, wcols(d)], W.at[4 - d, pl.ds(slab, 64)], dy=d) for d in (2, 1, 3)
    ]
    l_proj.wait()

    def pblock(dxh=0, dz=0):
        at = ((xh + dxh) % 2) * 8 + ((z + dz) % 4) * 2 + k
        return PR.at[pl.ds(pl.multiple_of(256 * at, 256), 256)]

    p_x = send(pblock(), pblock(), dxh=1)
    p_up = send(pblock(), pblock(), dz=UP)
    p_dn = send(pblock(), pblock(), dz=DOWN)
    p_sib = [send(pblock(), pblock(), dk=1)]
    sx = send(S.at[0, own_x], S.at[0, far_x], dxl=1)
    sxy = [send(S.at[0, own_y], S.at[0, far_y], dxl=1)]

    l_tin.wait()

    def clip_t(i, amax):
        rows = pl.ds(pl.multiple_of(32 * i, 32), 32)
        v = T[rows, pl.ds(0, 512)].astype(F32)
        T[rows, pl.ds(0, 512)] = jnp.clip(v, -lim_in, lim_in).astype(BF16)
        return jnp.maximum(amax, fold(jnp.maximum, jnp.abs(v)))

    amax_in = lax.fori_loop(0, 32, clip_t, jnp.zeros((8, 128), F32))

    low, high = pl.ds(0, 512), pl.ds(512, 512)

    def tblock(r, rows):
        return T.at[rows, pl.ds(512 * r, 512)]

    t_up = send(tblock(0, low), tblock(3, low), dy=UP)
    t_dn = send(tblock(0, high), tblock(1, high), dy=DOWN)

    left, right = pl.ds(0, 2048), pl.ds(2048, 2048)
    sy_up.wait_recv()
    sy_up2 = send(S.at[3, own_y, left], S.at[2, own_y, left], dy=UP)
    sxy.append(send(S.at[3, own_y], S.at[3, far_y], dxl=1))
    sy_dn.wait_recv()
    sy_dn2 = send(S.at[1, own_y, right], S.at[2, own_y, right], dy=DOWN)
    sxy.append(send(S.at[1, own_y], S.at[1, far_y], dxl=1))

    t_up1 = send(tblock(0, high), tblock(3, high), dy=UP)
    t_dn1 = send(tblock(0, low), tblock(1, low), dy=DOWN)

    def wslab(dz=0, half=None):
        at = pl.multiple_of(64 * (2 * ((z + dz) % 4) + k), 64)
        if half is None:
            return W.at[pl.ds(1, 3), pl.ds(at, 64)]
        return W.at[pl.ds(1, 3), pl.ds(pl.multiple_of(at + 32 * half, 32), 32)]

    p_x.wait_recv()
    p_sib.append(send(pblock(1), pblock(1), dk=1))
    for copy in w_y:
        copy.wait_recv()
    w_up = send(wslab(), wslab(), dz=UP)
    w_dn = send(wslab(), wslab(), dz=DOWN)
    w_sib = [send(wslab(), wslab(), dk=1)]

    l_wown.wait()

    @pl.loop(0, 32)
    def _(i):
        rows = pl.ds(pl.multiple_of(16 * i, 16), 16)
        v = W[0, rows, :].astype(F32)
        W[0, rows, :] = jnp.clip(v, -lim_w, lim_w).astype(BF16)

    sy_up2.wait_recv()
    sy_dn2.wait_recv()
    sxy.append(send(S.at[2, own_y], S.at[2, far_y], dxl=1))

    t_up.wait_recv()
    t_up2 = send(tblock(3, low), tblock(2, low), dy=UP)
    t_dn.wait_recv()
    t_dn2 = send(tblock(1, high), tblock(2, high), dy=DOWN)
    a_up = send(S.at[0, own_x], S.at[3, own_x], dy=UP)
    sx.wait_recv()
    b_dn = send(S.at[0, far_x], S.at[1, far_x], dy=DOWN)
    b_up = send(S.at[0, far_x], S.at[3, far_x], dy=UP)
    a_dn = send(S.at[0, own_x], S.at[1, own_x], dy=DOWN)

    w_up.wait_recv()
    w_up2 = send(wslab(DOWN, 0), wslab(DOWN, 0), dz=UP)
    w_sib.append(send(wslab(DOWN), wslab(DOWN), dk=1))
    w_dn.wait_recv()
    w_dn2 = send(wslab(UP, 1), wslab(UP, 1), dz=DOWN)
    w_sib.append(send(wslab(UP), wslab(UP), dk=1))
    q_dn = send(pblock(1), pblock(1), dz=DOWN)
    q_up = send(pblock(1), pblock(1), dz=UP)
    p_up.wait_recv()
    p_up2 = send(pblock(0, DOWN), pblock(0, DOWN), dz=UP)
    p_sib.append(send(pblock(0, DOWN), pblock(0, DOWN), dk=1))
    p_dn.wait_recv()
    p_sib.append(send(pblock(0, UP), pblock(0, UP), dk=1))
    w_up2.wait_recv()
    w_dn2.wait_recv()
    w_sib.append(send(wslab(2), wslab(2), dk=1))

    for copy in t_up1, t_dn1, t_up2, t_dn2, *w_sib:
        copy.wait_recv()

    def product(rows, col0, n):
        cols = pl.ds(pl.multiple_of(col0 + 256 * n, 256), 256)
        w = W[:, :, cols].reshape(2048, 256)
        return jnp.dot(T[rows, :], w, preferred_element_type=F32)

    rs_t = []
    for q in range(4):
        rows = pl.ds(256 * q, 256)

        @pl.loop(0, 4)
        def _(n):
            cols = pl.ds(pl.multiple_of(256 * n, 256), 256)
            psend[rows, cols] = product(rows, 1024 * (1 - xl), n).astype(BF16)

        rs_t.append(send(psend.at[rows], precv.at[rows], dxl=1))
        if q == 1:
            q_dn.wait_recv()
            q_dn2 = send(pblock(1, UP), pblock(1, UP), dz=DOWN)
            p_sib.append(send(pblock(1, UP), pblock(1, UP), dk=1))
            q_up.wait_recv()
            p_sib.append(send(pblock(1, DOWN), pblock(1, DOWN), dk=1))

    l_res.wait()
    for q in range(4):
        rows = pl.ds(256 * q, 256)

        @pl.loop(0, 4)
        def _(n):
            cols = pl.ds(pl.multiple_of(256 * n, 256), 256)
            H[rows, cols] = product(rows, 1024 * xl, n) + R[rows, cols].astype(F32)

    p_up2.wait_recv()
    p_sib.append(send(pblock(0, 2), pblock(0, 2), dk=1))
    q_dn2.wait_recv()
    p_sib.append(send(pblock(1, 2), pblock(1, 2), dk=1))
    a_up.wait_recv()
    a_up2 = send(S.at[3, own_x], S.at[2, own_x], dy=UP)
    b_dn.wait_recv()
    b_dn2 = send(S.at[1, far_x], S.at[2, far_x], dy=DOWN)

    def mapped(r):
        @pl.loop(0, 2)
        def _(n):
            cols = pl.ds(pl.multiple_of(512 * n, 512), 512)
            M[pl.ds(256 * r, 256), cols] = jnp.dot(
                S[r], PR[:, cols], preferred_element_type=F32
            )

    ORDER = [(1, 2), (0, 2), (1, 1), (1, 3), (1, 0), (0, 1), (0, 3), (0, 0)]

    def turned(g):
        if g < 4:
            return T, 512 * (g % 2), 1024 * (g // 2)
        return (R, psend)[g // 2 - 2], 512 * (g % 2), 0

    def turn(g, r):
        dxh, dz = ORDER[g]
        chip = ((xh + dxh) % 2) * 4 + (z + dz) % 4
        ref, row0, col0 = turned(g)
        for own in (0, 1):
            cols = pl.ds(pl.multiple_of(512 * chip + 256 * ((k + 1 - own) % 2), 256), 256)
            ref[pl.ds(row0 + 256 * own, 256), pl.ds(col0 + 256 * r, 256)] = S[r, :, cols].T

    def turn_first(r):
        for g in range(4):
            turn(g, r)

    def squares(q):
        rs_t[q].wait_recv()

        @pl.loop(0, 16)
        def _(i):
            rows = pl.ds(pl.multiple_of(256 * q + 16 * i, 16), 16)
            h = H[rows, :] + precv[rows, :].astype(F32)
            H[rows, :] = h
            col[rows, :] = jnp.broadcast_to(jnp.sum(h * h, axis=1, keepdims=True), (16, 128))

    for copy in p_sib:
        copy.wait_recv()
    sxy[0].wait_recv()
    mapped(0)
    for copy in t_up, t_dn, t_up1, t_dn1, t_up2, t_dn2:
        copy.wait_send()
    turn_first(0)
    squares(0)
    squares(1)
    squares(2)
    b_up.wait_recv()
    sxy[1].wait_recv()
    mapped(3)
    turn_first(3)
    a_dn.wait_recv()
    sxy[2].wait_recv()
    mapped(1)
    squares(3)
    sq[0] = col[...].T[0:8, :]
    sq_c = [send(sq.at[0], sq.at[dy * 2 + dx], dy=dy, dxl=dx) for dy, dx in TENSOR]
    turn_first(1)
    a_up2.wait_recv()
    b_dn2.wait_recv()
    sxy[3].wait_recv()
    mapped(2)
    turn_first(2)
    for copy in sq_c:
        copy.wait_recv()
    total = sq[0]
    for i in range(1, 8):
        total = total + sq[i]
    inv = lax.rsqrt(total * (1.0 / 8192) + EPS)
    col[...] = jnp.broadcast_to(inv[0:1, :], (128, 1024)).T

    gains = tea_gain[:, pl.ds(pl.multiple_of(1024 * t, 1024), 1024)]

    def errors(r, acc):
        for b in range(2):
            base = 128 * (2 * ((y + r) % 4) + (xl + b) % 2)

            def step(i, acc):
                there = pl.ds(pl.multiple_of(base + 16 * i, 16), 16)
                here = pl.ds(pl.multiple_of(256 * r + 128 * b + 16 * i, 16), 16)
                scale = jnp.concatenate([col[there, :]] * 8, axis=1)
                e = M[here, :] - H[there, :] * scale * gains
                E[here, :] = e.astype(BF16)
                return acc + fold(jnp.add, e * e)

            acc = lax.fori_loop(0, 8, step, acc)
        return acc

    acc = jnp.zeros((8, 128), F32)
    for r in range(4):
        acc = errors(r, acc)

    row = lax.broadcasted_iota(jnp.int32, (8, 128), 0)
    tile = jnp.where(row == 0, jnp.max(amax_in), jnp.where(row == 1, jnp.max(amax_w), jnp.sum(acc)))

    def merge(first, count):
        out = scal[first]
        for i in range(1, count):
            v = scal[first + i]
            out = jnp.where(row < 2, jnp.maximum(out, v), out + v)
        return out

    scal[t] = tile
    sc1 = [send(scal.at[t], scal.at[t], dy=dy, dxl=dx) for dy, dx in TENSOR]

    for copy in w_up, w_dn, w_up2, w_dn2, *w_sib, *rs_t:
        copy.wait_send()

    a_cols, b_cols = pl.ds(0, ACOLS), pl.ds(ACOLS, 1024 - ACOLS)

    def gslot(dxh, dz, cols, first=0, count=256):
        g = ORDER.index((dxh, dz))
        return W.at[g // 2, pl.ds(256 * (g % 2) + first, count), cols]

    to_sib, a_1, b_1, a_2, a_m, b_m = [], {}, {}, {}, {}, {}

    def term(g):
        dxh, dz = ORDER[g]
        ref, row0, col0 = turned(g)

        @pl.loop(0, 2)
        def _(n):
            at = pl.multiple_of(512 * n, 512)
            both = jnp.dot(
                ref[pl.ds(row0, 512), pl.ds(col0, 1024)],
                E[:, pl.ds(at, 512)],
                preferred_element_type=F32,
            ).astype(BF16)
            rows = pl.ds(256 * (g % 2), 256)
            W[g // 2, rows, pl.ds(pl.multiple_of(1024 + at, 512), 512)] = both[:256]
            W[g // 2, rows, pl.ds(at, 512)] = both[256:]

        to_sib.append(send(gslot(dxh, dz, pl.ds(1024, 1024)), sib.at[g], dk=1))

    def add(dxh, dz, cols, others, first=0, count=256):
        g = ORDER.index((dxh, dz))

        @pl.loop(0, count // 16)
        def _(i):
            here = pl.ds(pl.multiple_of(16 * i, 16), 16)
            there = pl.ds(pl.multiple_of(first + 16 * i, 16), 16)
            rows = pl.ds(pl.multiple_of(256 * (g % 2) + first + 16 * i, 16), 16)
            total = W[g // 2, rows, cols].astype(F32)
            for ref, index, whole in others:
                total = total + ref[index, there if whole else here, :].astype(F32)
            W[g // 2, rows, cols] = total.astype(BF16)

    def along_z(dxh, dz, cols, mid, at, far, sent, passed):
        if dz == 2:
            passed[dxh, UP] = send(gslot(dxh, 2, cols, 0, 128), mid.at[at], dz=UP)
            passed[dxh, DOWN] = send(gslot(dxh, 2, cols, 128, 128), mid.at[at + 1], dz=DOWN)
        elif dz:
            passed[dxh, dz].wait_recv()
            add(dxh, dz, cols, [(mid, at + dz // 2, False)], 64 * (dz - 1), 128)
            sent[dxh, dz] = send(gslot(dxh, dz, cols), far.at[at + dz // 2], dz=dz)

    def finish(g):
        dxh, dz = ORDER[g]
        to_sib[g].wait_recv()
        add(dxh, dz, pl.ds(0, 1024), [(sib, g, True)])
        if dxh:
            a_1[dz] = send(gslot(dxh, dz, a_cols), ra1.at[dz], dxh=1)

    def second_b(dxh, dz):
        along_z(dxh, dz, b_cols, bm, 2 * dxh, rb1, b_1, b_m)

    def second_a(dz):
        a_1[dz].wait_recv()
        add(0, dz, a_cols, [(ra1, dz, True)])
        along_z(0, dz, a_cols, am, 0, ra2, a_2, a_m)

    def term_of(g):
        if g >= 4:
            for r in range(4):
                turn(g, r)
        term(g)

    term_of(0)
    term_of(1)
    for copy in sc1:
        copy.wait_recv()
    at = 8 + xh * 4 + z
    scal[at] = merge(0, 8)
    sc2 = [send(scal.at[at], scal.at[at], dxh=dx, dz=dz) for dx, dz in CONTEXT]
    finish(0)
    second_b(1, 2)
    term_of(2)
    finish(1)
    second_b(0, 2)
    term_of(3)
    finish(2)
    second_b(1, 1)
    term_of(4)
    finish(3)
    second_b(1, 3)
    second_a(2)
    term_of(5)
    finish(4)
    term_of(6)
    finish(5)
    second_b(0, 1)
    term_of(7)
    finish(6)
    second_b(0, 3)
    for n in (UP, DOWN):
        b_1[1, n].wait_recv()
    add(1, 0, b_cols, [(rb1, 2, True), (rb1, 3, True)])
    b_2 = send(gslot(1, 0, b_cols), rb2.at[0], dxh=1)
    second_a(1)
    second_a(3)
    for copy in sc2:
        copy.wait_recv()
    scal[16 + k] = merge(8, 8)
    sc3 = send(scal.at[16 + k], scal.at[16 + k], dk=1)
    finish(7)
    second_a(0)
    sc3.wait_recv()
    scal[18] = merge(16, 2)
    written = [load(scal.at[18], parts.at[pl.ds(256, 8), pl.ds(0, 128)])]

    for n in (UP, DOWN):
        b_1[0, n].wait_recv()
        a_2[0, n].wait_recv()
    b_2.wait_recv()
    scale = 1.0 / math.sqrt(tokens_all)
    for q in range(2):

        @pl.loop(0, 8)
        def _(i):
            rows = pl.ds(pl.multiple_of(128 * q + 16 * i, 16), 16)
            mine = pl.ds(pl.multiple_of(256 + 128 * q + 16 * i, 16), 16)
            total = W[3, mine, a_cols].astype(F32)
            for n in range(2):
                total = total + ra2[n, rows, :].astype(F32)
            total_g[rows, a_cols] = total * scale
            total = W[3, mine, b_cols].astype(F32) + rb2[0, rows, :].astype(F32)
            for n in range(2):
                total = total + rb1[n, rows, :].astype(F32)
            total_g[rows, b_cols] = total * scale

        rows = pl.ds(128 * q, 128)
        written.append(load(total_g.at[rows], parts.at[rows]))

    waited = [w_up, w_dn, w_up2, w_dn2, *w_sib, t_up, t_dn, t_up1, t_dn1, t_up2, t_dn2, *rs_t]
    for copy in sends:
        if not any(copy is w for w in waited):
            copy.wait_send()
    for copy in written:
        copy.wait()


def results(
    tokens_all, parts, hist_in, hist_w, grad, loss, hist_in_new, hist_w_new, held, tile, sem_in, sem_out
):
    scalars = pltpu.make_async_copy(parts.at[pl.ds(256, 8), pl.ds(0, 128)], tile, sem_in.at[4])
    scalars.start()
    pieces = [pl.ds(64 * i, 64) for i in range(4)]
    ins = [
        pltpu.make_async_copy(parts.at[rows], held.at[rows], sem_in.at[i])
        for i, rows in enumerate(pieces)
    ]
    outs = [
        pltpu.make_async_copy(held.at[rows], grad.at[rows], sem_out.at[i])
        for i, rows in enumerate(pieces)
    ]
    for copy in ins:
        copy.start()
    for i in range(15):
        hist_in_new[i + 1] = hist_in[i]
        hist_w_new[i + 1] = hist_w[i]
    for copy, back in zip(ins, outs):
        copy.wait()
        back.start()
    scalars.wait()
    hist_in_new[0] = jnp.max(tile[0:1, :])
    hist_w_new[0] = jnp.max(tile[1:2, :])
    loss[0] = jnp.max(tile[2:3, :]) * (0.5 / (tokens_all * 8192))
    for back in outs:
        back.wait()


def local(
    teacher_in, teacher_resid, teacher_wo, teacher_gain, input_history, weight_history,
    student_hidden, student_gain, projection,
):
    tokens_all = teacher_in.shape[0] * lax.axis_size("context")
    smem = pl.BlockSpec(memory_space=pltpu.SMEM)
    vmem = pl.BlockSpec(memory_space=pltpu.VMEM)
    hbm = pl.BlockSpec(memory_space=pl.ANY)
    parts = pl.pallas_call(
        functools.partial(kernel, tokens_all),
        name="distill",
        out_shape=jax.ShapeDtypeStruct((264, 1024), F32),
        in_specs=[smem, smem, vmem, vmem, hbm, hbm, hbm, hbm, hbm],
        out_specs=hbm,
        scratch_shapes=[
            pltpu.VMEM((1024, 2048), BF16),
            pltpu.VMEM((4, 512, 2048), BF16),
            pltpu.VMEM((4, 256, 4096), BF16),
            pltpu.VMEM((4096, 1024), BF16),
            pltpu.VMEM((1024, 1024), BF16),
            pltpu.VMEM((1024, 1024), F32),
            pltpu.VMEM((1024, 1024), F32),
            pltpu.VMEM((1024, 1024), BF16),
            pltpu.VMEM((1024, 1024), BF16),
            pltpu.VMEM((1024, 1024), BF16),
            pltpu.VMEM((128, 4096), BF16),
            pltpu.VMEM((64, 8192), BF16),
            pltpu.VMEM((1024, 128), F32),
            pltpu.VMEM((8, 8, 1024), F32),
            pltpu.VMEM((19, 8, 128), F32),
            pltpu.VMEM((8, 256, 1024), BF16),
            pltpu.VMEM((4, 256, ACOLS), BF16),
            pltpu.VMEM((2, 256, ACOLS), BF16),
            pltpu.VMEM((4, 256, 1024 - ACOLS), BF16),
            pltpu.VMEM((1, 256, 1024 - ACOLS), BF16),
            pltpu.VMEM((2, 128, ACOLS), BF16),
            pltpu.VMEM((4, 128, 1024 - ACOLS), BF16),
            pltpu.VMEM((256, 1024), F32),
            pltpu.SemaphoreType.DMA((COPIES,)),
            pltpu.SemaphoreType.DMA((COPIES,)),
            pltpu.SemaphoreType.DMA((10,)),
        ],
        compiler_params=pltpu.CompilerParams(
            collective_id=0, has_side_effects=True, vmem_limit_bytes=62 << 20
        ),
        cost_estimate=pl.CostEstimate(
            flops=3 * 2 * 1024 * 1024 * 4096, bytes_accessed=16 << 20, transcendentals=1024
        ),
    )(
        input_history,
        weight_history,
        student_gain.reshape(1, -1),
        teacher_gain.reshape(1, -1),
        teacher_in,
        teacher_resid,
        teacher_wo,
        student_hidden,
        projection,
    )
    grad, loss, hist_in, hist_w = pl.pallas_call(
        functools.partial(results, tokens_all),
        name="results",
        out_shape=(
            jax.ShapeDtypeStruct((256, 1024), F32),
            jax.ShapeDtypeStruct((1,), F32),
            jax.ShapeDtypeStruct((16,), F32),
            jax.ShapeDtypeStruct((16,), F32),
        ),
        in_specs=[hbm, smem, smem],
        out_specs=(hbm, smem, smem, smem),
        scratch_shapes=[
            pltpu.VMEM((256, 1024), F32),
            pltpu.VMEM((8, 128), F32),
            pltpu.SemaphoreType.DMA((5,)),
            pltpu.SemaphoreType.DMA((4,)),
        ],
    )(parts, input_history, weight_history)
    return grad, loss.reshape(()), hist_in, hist_w


def solution(mesh):
    placed = (
        P("context", "tensor"),
        P("context", "tensor"),
        P("tensor", None),
        P(),
        P(),
        P(),
        P(("context", "tensor"), None),
        P(),
        P("context", "tensor"),
    )
    return jax.shard_map(
        local,
        mesh=mesh,
        in_specs=placed,
        out_specs=(P("context", "tensor"), P(), P(), P()),
        check_vma=False,
    )
```

```python
import functools
import math

import jax
import jax.numpy as jnp
from jax import lax
from jax.experimental import pallas as pl
from jax.experimental.pallas import tpu as pltpu
from jax.sharding import PartitionSpec as P

MESH = pl.DeviceIdType.MESH
F32, BF16 = jnp.float32, jnp.bfloat16
EPS = 1e-05
SEND_SEMS, RECV_SEMS = 7, 84
GROUP = 8 << 20
XROWS = 112
ACOLS = 384


def lanes(tile):
    rows, width = tile.shape
    return [
        tile[r : r + 8, c : c + 128]
        for r in range(0, rows, 8)
        for c in range(0, width, 128)
    ]


def fold(op, tile):
    parts = lanes(tile)
    while len(parts) > 1:
        parts = [op(a, b) for a, b in zip(parts[::2], parts[1::2])] + (
            [parts[-1]] if len(parts) % 2 else []
        )
    return parts[0]


def kernel(
    tokens_all,
    hist_in, hist_w, stu_gain, tea_gain, tin, resid, wo, stu, proj,
    parts,
    T, W, S, PR, R, H, M, E, psend, precv, sraw, wraw, col, sq, scal, sib, ra1, ra2, rb1, rb2, am, bm, total_g, sgain, tgain,
    ssem, rsem, lsem,
):
    t, c = lax.axis_index("tensor"), lax.axis_index("context")
    y, xl = t // 2, t % 2
    xh, z, k = c // 8, (c // 2) % 4, c % 2

    def dev(dy=0, dxl=0, dxh=0, dz=0, dk=0):
        ny, nz = (y + dy) % 4, (z + dz) % 4
        nxl, nxh, nk = (xl + dxl) % 2, (xh + dxh) % 2, (k + dk) % 2
        return {"tensor": ny * 2 + nxl, "context": nxh * 8 + nz * 2 + nk}

    received, groups = [], {}

    def remote(src, dst, send_sem, recv_sem, to):
        return pltpu.make_async_remote_copy(
            src_ref=src,
            dst_ref=dst,
            send_sem=ssem.at[send_sem],
            recv_sem=rsem.at[recv_sem],
            device_id=to,
            device_id_type=MESH,
        )

    def size(ref):
        return math.prod(ref.shape) * jnp.dtype(ref.dtype).itemsize

    def send(src, dst, group=None, **to):
        if group is None:
            group = next((n for n in range(50) if groups.get(n, (0, 0))[1] + size(src) <= GROUP), 0)
        index, held = groups.get(group, (len(groups), 0))
        groups[group] = index, held + size(src)
        received.append(len(received))
        copy = remote(src, dst, index, received[-1], dev(**to))
        copy.start()
        return copy

    def span(count):
        if count % 32768 == 0:
            return PR.at[pl.ds(0, count // 2048)]
        return col.at[pl.ds(0, count // 512)]

    def sent(group):
        index, held = groups[group]
        rows = span(held)
        remote(rows, rows, index, 0, dev(dk=1)).wait_send()

    def send_all(pieces, group=None):
        received.append(len(received))
        at, total = received[-1], 0
        for src, dst, to in pieces:
            key = group
            if key is None:
                key = next(n for n in range(50) if groups.get(n, (0, 0))[1] + size(src) <= GROUP)
            index, held = groups.get(key, (len(groups), 0))
            groups[key] = index, held + size(src)
            remote(src, dst, index, at, dev(**to)).start()
            total += size(src)
        return at, total

    def await_group(landed):
        at, total = landed
        rows = span(total)
        remote(rows, rows, 0, at, dev(dk=1)).wait_recv()

    local = []

    def load(src, dst):
        copy = pltpu.make_async_copy(src, dst, lsem.at[len(local)])
        copy.start()
        local.append(copy)
        return copy

    TENSOR = [(dy, dx) for dy in range(4) for dx in range(2) if (dy, dx) != (0, 0)]
    CONTEXT = [(dx, dz) for dx in range(2) for dz in range(4) if (dx, dz) != (0, 0)]
    UP, DOWN = 1, 3

    slab = pl.multiple_of(64 * (2 * z + k) + 32 * xh, 32)
    l_wraw = load(wo.at[pl.ds(slab, 32)], wraw)
    l_sgain = load(stu_gain, sgain)
    l_tgain = load(tea_gain.at[:, pl.ds(pl.multiple_of(1024 * t, 1024), 1024)], tgain)
    l_proj = load(proj, PR.at[pl.ds(pl.multiple_of(256 * c, 256), 256)])
    l_stu = load(stu, sraw)
    l_tin = load(tin, T.at[:, pl.ds(0, 512)])
    l_wown = load(wo.at[:, pl.ds(pl.multiple_of(2048 * y, 2048), 2048)], W.at[0])
    l_res = load(resid, R)

    barrier = pltpu.get_barrier_semaphore()
    for dy, dx in TENSOR:
        pl.semaphore_signal(barrier, 1, device_id=dev(dy=dy, dxl=dx), device_id_type=MESH)
    for dx, dz in CONTEXT:
        pl.semaphore_signal(barrier, 1, device_id=dev(dxh=dx, dz=dz), device_id_type=MESH)
    pl.semaphore_signal(barrier, 1, device_id=dev(dk=1), device_id_type=MESH)

    lim_in, lim_w = hist_in[0], hist_w[0]
    for i in range(1, 16):
        lim_in = jnp.maximum(lim_in, hist_in[i])
        lim_w = jnp.maximum(lim_w, hist_w[i])

    l_wraw.wait()

    def clip_w(i, amax):
        rows = pl.ds(pl.multiple_of(16 * i, 16), 16)
        for n in range(8):
            cols = pl.ds(1024 * n, 1024)
            v = wraw[rows, cols].astype(F32)
            amax = jnp.maximum(amax, fold(jnp.maximum, jnp.abs(v)))
            wraw[rows, cols] = jnp.clip(v, -lim_w, lim_w).astype(BF16)
        return amax

    amax_w = lax.fori_loop(0, 2, clip_w, jnp.zeros((8, 128), F32))

    pl.semaphore_wait(barrier, len(TENSOR) + len(CONTEXT) + 1)

    def wcols(d):
        return pl.ds(pl.multiple_of(2048 * ((y + d) % 4), 2048), 2048)

    w_y = send_all(
        [(wraw.at[:, wcols(d)], W.at[4 - d, pl.ds(slab, 32)], {"dy": d}) for d in (2, 1, 3)]
    )
    l_proj.wait()

    def pblock(dxh=0, dz=0):
        at = ((xh + dxh) % 2) * 8 + ((z + dz) % 4) * 2 + k
        return PR.at[pl.ds(pl.multiple_of(256 * at, 256), 256)]

    p_up = send(pblock(), pblock(), dz=UP)
    p_dn = send(pblock(), pblock(), dz=DOWN)
    p_sib = [send(pblock(), pblock(), dk=1)]

    l_stu.wait()
    l_sgain.wait()

    @pl.loop(0, 8)
    def _(i):
        rows = pl.ds(pl.multiple_of(16 * i, 16), 16)
        v = sraw[rows, :].astype(F32)
        mean = jnp.mean(v * v, axis=1, keepdims=True)
        S[0, rows, :] = (v * lax.rsqrt(mean + EPS) * sgain[...]).astype(BF16)

    nx = XROWS
    ny = 128 - nx
    own_x, own_y = pl.ds(0, nx), pl.ds(nx, ny)
    far_x, far_y = pl.ds(128, nx), pl.ds(128 + nx, ny)
    sy_up = send(S.at[0, own_y], S.at[3, own_y], dy=UP)
    sy_dn = send(S.at[0, own_y], S.at[1, own_y], dy=DOWN)
    sxy = [send(S.at[0, own_y], S.at[0, far_y], dxl=1)]

    l_tin.wait()

    def clip_t(i, amax):
        rows = pl.ds(pl.multiple_of(32 * i, 32), 32)
        v = T[rows, pl.ds(0, 512)].astype(F32)
        T[rows, pl.ds(0, 512)] = jnp.clip(v, -lim_in, lim_in).astype(BF16)
        return jnp.maximum(amax, fold(jnp.maximum, jnp.abs(v)))

    amax_in = lax.fori_loop(0, 32, clip_t, jnp.zeros((8, 128), F32))
    low, high = pl.ds(0, 512), pl.ds(512, 512)

    def tblock(r, rows):
        return T.at[rows, pl.ds(512 * r, 512)]

    t_up = send(tblock(0, low), tblock(3, low), "t", dy=UP)
    t_dn = send(tblock(0, high), tblock(1, high), "t", dy=DOWN)
    t_up1 = send(tblock(0, high), tblock(3, high), "t", dy=UP)
    t_dn1 = send(tblock(0, low), tblock(1, low), "t", dy=DOWN)

    def wslab(dz=0, dxh=None):
        at = pl.multiple_of(64 * (2 * ((z + dz) % 4) + k), 64)
        if dxh is None:
            return W.at[pl.ds(1, 3), pl.ds(at, 64)]
        return W.at[pl.ds(1, 3), pl.ds(pl.multiple_of(at + 32 * ((xh + dxh) % 2), 32), 32)]

    await_group(w_y)
    w_x = send(wslab(0, 0), wslab(0, 0), "w", dxh=1)
    w_up = send(wslab(0, 0), wslab(0, 0), "w", dz=UP)
    w_dn = send(wslab(0, 0), wslab(0, 0), "w", dz=DOWN)
    sx = send(S.at[0, own_x], S.at[0, far_x], dxl=1)
    p_x = send(pblock(), pblock(), dxh=1)

    l_wown.wait()

    @pl.loop(0, 32)
    def _(i):
        rows = pl.ds(pl.multiple_of(16 * i, 16), 16)
        v = W[0, rows, :].astype(F32)
        W[0, rows, :] = jnp.clip(v, -lim_w, lim_w).astype(BF16)

    sy_up.wait_recv()
    sxy.append(send(S.at[3, own_y], S.at[3, far_y], dxl=1))
    sy_dn.wait_recv()
    sxy.append(send(S.at[1, own_y], S.at[1, far_y], dxl=1))
    w_x.wait_recv()
    v_dn = send(wslab(0, 1), wslab(0, 1), "w", dz=DOWN)
    v_up = send(wslab(0, 1), wslab(0, 1), "w", dz=UP)
    w_sib = [send(wslab(), wslab(), "w", dk=1)]

    left, right = pl.ds(0, 2048), pl.ds(2048, 2048)
    t_up.wait_recv()
    t_up2 = send(tblock(3, low), tblock(2, low), "t", dy=UP)
    t_dn.wait_recv()
    t_dn2 = send(tblock(1, high), tblock(2, high), "t", dy=DOWN)
    sy_up2 = send(S.at[3, own_y, left], S.at[2, own_y, left], dy=UP)
    sy_dn2 = send(S.at[1, own_y, right], S.at[2, own_y, right], dy=DOWN)
    a_up = send(S.at[0, own_x], S.at[3, own_x], dy=UP)

    w_up.wait_recv()
    w_up2 = send(wslab(DOWN, 0), wslab(DOWN, 0), "w", dz=UP)
    v_dn.wait_recv()
    v_dn2 = send(wslab(UP, 1), wslab(UP, 1), "w", dz=DOWN)
    v_up.wait_recv()
    w_sib.append(send(wslab(DOWN), wslab(DOWN), "w", dk=1))
    w_dn.wait_recv()
    w_sib.append(send(wslab(UP), wslab(UP), "w", dk=1))

    sx.wait_recv()
    b_dn = send(S.at[0, far_x], S.at[1, far_x], dy=DOWN)
    b_up = send(S.at[0, far_x], S.at[3, far_x], dy=UP)
    a_dn = send(S.at[0, own_x], S.at[1, own_x], dy=DOWN)

    w_up2.wait_recv()
    v_dn2.wait_recv()
    w_sib.append(send(wslab(2), wslab(2), "w", dk=1))
    p_up.wait_recv()
    p_up2 = send(pblock(0, DOWN), pblock(0, DOWN), dz=UP)
    p_sib.append(send(pblock(0, DOWN), pblock(0, DOWN), dk=1))
    p_dn.wait_recv()
    p_sib.append(send(pblock(0, UP), pblock(0, UP), dk=1))

    for copy in t_up1, t_dn1, t_up2, t_dn2, *w_sib:
        copy.wait_recv()

    def product(rows, col0, n):
        cols = pl.ds(pl.multiple_of(col0 + 256 * n, 256), 256)
        w = W[:, :, cols].reshape(2048, 256)
        return jnp.dot(T[rows, :], w, preferred_element_type=F32)

    rs_t = []
    for q in range(4):
        rows = pl.ds(256 * q, 256)

        @pl.loop(0, 4)
        def _(n):
            cols = pl.ds(pl.multiple_of(256 * n, 256), 256)
            psend[rows, cols] = product(rows, 1024 * (1 - xl), n).astype(BF16)

        for rows in (rows,) if q < 3 else (pl.ds(768, 128), pl.ds(896, 128)):
            rs_t.append(send(psend.at[rows], precv.at[rows], "r", dxl=1))
        if q == 0:
            p_x.wait_recv()
            p_sib.append(send(pblock(1), pblock(1), dk=1))
            q_dn = send(pblock(1), pblock(1), dz=DOWN)
            q_up = send(pblock(1), pblock(1), dz=UP)


    sy_up2.wait_recv()
    sy_dn2.wait_recv()
    sxy.append(send(S.at[2, own_y], S.at[2, far_y], dxl=1))
    l_res.wait()
    for q in range(4):
        rows = pl.ds(256 * q, 256)

        @pl.loop(0, 4)
        def _(n):
            cols = pl.ds(pl.multiple_of(256 * n, 256), 256)
            H[rows, cols] = product(rows, 1024 * xl, n) + R[rows, cols].astype(F32)

    q_dn.wait_recv()
    q_dn2 = send(pblock(1, UP), pblock(1, UP), dz=DOWN)
    p_sib.append(send(pblock(1, UP), pblock(1, UP), dk=1))
    q_up.wait_recv()
    p_sib.append(send(pblock(1, DOWN), pblock(1, DOWN), dk=1))
    p_up2.wait_recv()
    p_sib.append(send(pblock(0, 2), pblock(0, 2), dk=1))
    parts_x = [(pl.ds(0, 64), pl.ds(64, nx - 64)), (pl.ds(128, 64), pl.ds(192, nx - 64))]
    a_up.wait_recv()
    a_up2, a_up3 = [send(S.at[3, rows], S.at[2, rows], dy=UP) for rows in parts_x[0]]
    b_dn.wait_recv()
    b_dn2, b_dn3 = [send(S.at[1, rows], S.at[2, rows], dy=DOWN) for rows in parts_x[1]]
    q_dn2.wait_recv()
    p_sib.append(send(pblock(1, 2), pblock(1, 2), dk=1))

    def mapped(r):
        @pl.loop(0, 2)
        def _(n):
            cols = pl.ds(pl.multiple_of(512 * n, 512), 512)
            M[pl.ds(256 * r, 256), cols] = jnp.dot(
                S[r], PR[:, cols], preferred_element_type=F32
            )

    def mapped_part(first):
        @pl.loop(0, 2)
        def _(n):
            cols = pl.ds(pl.multiple_of(512 * n, 512), 512)
            rows = jnp.concatenate([S[2, pl.ds(first, 64)], S[2, pl.ds(128 + first, 64)]], axis=0)
            out = jnp.dot(rows, PR[:, cols], preferred_element_type=F32)
            M[pl.ds(512 + first, 64), cols] = out[:64]
            M[pl.ds(640 + first, 64), cols] = out[64:]

    ORDER = [(1, 2), (0, 2), (1, 1), (1, 3), (1, 0), (0, 1), (0, 3), (0, 0)]

    def turned(g):
        if g < 4:
            return T, 512 * (g % 2), 1024 * (g // 2)
        return (R, psend)[g // 2 - 2], 512 * (g % 2), 0

    def turn(g, r):
        dxh, dz = ORDER[g]
        chip = ((xh + dxh) % 2) * 4 + (z + dz) % 4
        ref, row0, col0 = turned(g)
        for own in (0, 1):
            cols = pl.ds(pl.multiple_of(512 * chip + 256 * ((k + 1 - own) % 2), 256), 256)
            ref[pl.ds(row0 + 256 * own, 256), pl.ds(col0 + 256 * r, 256)] = S[r, :, cols].T

    def turn_first(r):
        for g in range(4):
            turn(g, r)

    l_tgain.wait()
    gains = tgain[...]

    def squares(q):
        rs_t[q].wait_recv()
        first, count = (256 * q, 256) if q < 3 else (128 * q + 384, 128)

        @pl.loop(0, count // 16)
        def _(i):
            rows = pl.ds(pl.multiple_of(first + 16 * i, 16), 16)
            h = H[rows, :] + precv[rows, :].astype(F32)
            H[rows, :] = h * gains
            col[rows, :] = jnp.broadcast_to(jnp.sum(h * h, axis=1, keepdims=True), (16, 128))

    for copy in p_sib:
        copy.wait_recv()
    sxy[0].wait_recv()
    mapped(0)
    sent("t")
    turn_first(0)
    squares(0)
    squares(1)
    squares(2)
    b_up.wait_recv()
    sxy[1].wait_recv()
    mapped(3)
    turn_first(3)
    a_dn.wait_recv()
    sxy[2].wait_recv()
    mapped(1)
    squares(3)
    squares(4)
    row = lax.broadcasted_iota(jnp.int32, (8, 128), 0)
    packed = jnp.zeros((8, 128), F32)
    for i in range(8):
        packed = jnp.where(row == i, col[pl.ds(128 * i, 128), :].T[0:8, :], packed)
    sq[0] = packed
    sq_c = send_all(
        [(sq.at[0], sq.at[dy * 2 + dx], {"dy": dy, "dxl": dx}) for dy, dx in TENSOR], "s"
    )
    turn_first(1)

    def errors(r, acc):
        for b in range(2):
            base = 128 * (2 * ((y + r) % 4) + (xl + b) % 2)

            def step(i, acc):
                there = pl.ds(pl.multiple_of(base + 16 * i, 16), 16)
                here = pl.ds(pl.multiple_of(256 * r + 128 * b + 16 * i, 16), 16)
                scale = jnp.concatenate([col[there, :]] * 8, axis=1)
                e = M[here, :] - H[there, :] * scale
                E[here, :] = e.astype(BF16)
                return acc + fold(jnp.add, e * e)

            acc = lax.fori_loop(0, 8, step, acc)
        return acc

    a_up2.wait_recv()
    b_dn2.wait_recv()
    mapped_part(0)
    sxy[3].wait_recv()
    a_up3.wait_recv()
    b_dn3.wait_recv()
    mapped_part(64)
    await_group(sq_c)
    total = sq[0]
    for i in range(1, 8):
        total = total + sq[i]
    inv = lax.rsqrt(total * (1.0 / 8192) + EPS)
    for i in range(8):
        col[pl.ds(128 * i, 128), :] = jnp.broadcast_to(inv[i : i + 1, :], (128, 128)).T
    acc = jnp.zeros((8, 128), F32)
    for r in range(4):
        acc = errors(r, acc)

    tile = jnp.where(row == 0, jnp.max(amax_in), jnp.where(row == 1, jnp.max(amax_w), jnp.sum(acc)))

    def merge(first, count):
        out = scal[first]
        for i in range(1, count):
            v = scal[first + i]
            out = jnp.where(row < 2, jnp.maximum(out, v), out + v)
        return out

    scal[t] = tile
    sc1 = send_all([(scal.at[t], scal.at[t], {"dy": dy, "dxl": dx}) for dy, dx in TENSOR], "s")

    sent("w")
    sent("r")

    a_cols, b_cols = pl.ds(0, ACOLS), pl.ds(ACOLS, 1024 - ACOLS)

    def gslot(dxh, dz, cols, first=0, count=256):
        g = ORDER.index((dxh, dz))
        return W.at[g // 2, pl.ds(256 * (g % 2) + first, count), cols]

    to_sib, a_1, b_1, a_2, a_m, b_m = [], {}, {}, {}, {}, {}

    def term(g):
        dxh, dz = ORDER[g]
        ref, row0, col0 = turned(g)

        if g == 0:
            for own in (0, 1):

                @pl.loop(0, 2)
                def _(n):
                    at = pl.multiple_of(512 * n, 512)
                    one = jnp.dot(
                        ref[pl.ds(row0 + 256 * own, 256), pl.ds(col0, 1024)],
                        E[:, pl.ds(at, 512)],
                        preferred_element_type=F32,
                    )
                    start = pl.multiple_of(1024 * (1 - own) + at, 512)
                    W[0, pl.ds(0, 256), pl.ds(start, 512)] = one.astype(BF16)

                if own == 0:
                    to_sib.append(send(gslot(dxh, dz, pl.ds(1024, 1024)), sib.at[g], dk=1))
            return

        @pl.loop(0, 2)
        def _(n):
            at = pl.multiple_of(512 * n, 512)
            both = jnp.dot(
                ref[pl.ds(row0, 512), pl.ds(col0, 1024)],
                E[:, pl.ds(at, 512)],
                preferred_element_type=F32,
            ).astype(BF16)
            rows = pl.ds(256 * (g % 2), 256)
            W[g // 2, rows, pl.ds(pl.multiple_of(1024 + at, 512), 512)] = both[:256]
            W[g // 2, rows, pl.ds(at, 512)] = both[256:]

        to_sib.append(send(gslot(dxh, dz, pl.ds(1024, 1024)), sib.at[g], dk=1))

    def add(dxh, dz, cols, others, first=0, count=256):
        g = ORDER.index((dxh, dz))

        @pl.loop(0, count // 16)
        def _(i):
            here = pl.ds(pl.multiple_of(16 * i, 16), 16)
            there = pl.ds(pl.multiple_of(first + 16 * i, 16), 16)
            rows = pl.ds(pl.multiple_of(256 * (g % 2) + first + 16 * i, 16), 16)
            total = W[g // 2, rows, cols].astype(F32)
            for ref, index, whole in others:
                total = total + ref[index, there if whole else here, :].astype(F32)
            W[g // 2, rows, cols] = total.astype(BF16)

    def along_z(dxh, dz, cols, mid, at, far, sent, passed):
        if dz == 2:
            passed[dxh, UP] = send(gslot(dxh, 2, cols, 0, 128), mid.at[at], dz=UP)
            passed[dxh, DOWN] = send(gslot(dxh, 2, cols, 128, 128), mid.at[at + 1], dz=DOWN)
        elif dz:
            passed[dxh, dz].wait_recv()
            add(dxh, dz, cols, [(mid, at + dz // 2, False)], 64 * (dz - 1), 128)
            sent[dxh, dz] = send(gslot(dxh, dz, cols), far.at[at + dz // 2], dz=dz)

    def finish(g):
        dxh, dz = ORDER[g]
        to_sib[g].wait_recv()
        add(dxh, dz, pl.ds(0, 1024), [(sib, g, True)])
        if dxh:
            a_1[dz] = send(gslot(dxh, dz, a_cols), ra1.at[dz], dxh=1)

    def second_b(dxh, dz):
        along_z(dxh, dz, b_cols, bm, 2 * dxh, rb1, b_1, b_m)

    def second_a(dz):
        a_1[dz].wait_recv()
        add(0, dz, a_cols, [(ra1, dz, True)])
        along_z(0, dz, a_cols, am, 0, ra2, a_2, a_m)

    def term_of(g):
        for r in range(4) if g >= 4 else (2,):
            turn(g, r)
        term(g)

    term_of(0)
    term_of(1)
    finish(0)
    second_b(1, 2)
    await_group(sc1)
    at = 8 + xh * 4 + z
    scal[at] = merge(0, 8)
    sc2 = send_all([(scal.at[at], scal.at[at], {"dxh": dx, "dz": dz}) for dx, dz in CONTEXT], "s")
    term_of(2)
    finish(1)
    second_b(0, 2)
    term_of(3)
    finish(2)
    second_b(1, 1)
    term_of(4)
    finish(3)
    second_b(1, 3)
    second_a(2)
    term_of(5)
    finish(4)
    term_of(6)
    finish(5)
    second_b(0, 1)
    term_of(7)
    finish(6)
    second_b(0, 3)
    for n in (UP, DOWN):
        b_1[1, n].wait_recv()
    add(1, 0, b_cols, [(rb1, 2, True), (rb1, 3, True)])
    b_2 = send(gslot(1, 0, b_cols), rb2.at[0], dxh=1)
    second_a(1)
    second_a(3)
    await_group(sc2)
    scal[16 + k] = merge(8, 8)
    sc3 = send(scal.at[16 + k], scal.at[16 + k], "s", dk=1)
    finish(7)
    second_a(0)
    sc3.wait_recv()
    scal[18] = merge(16, 2)
    written = [load(scal.at[18], parts.at[pl.ds(256, 8), pl.ds(0, 128)])]

    for n in (UP, DOWN):
        b_1[0, n].wait_recv()
        a_2[0, n].wait_recv()
    b_2.wait_recv()
    scale = 1.0 / math.sqrt(tokens_all)
    for q in range(2):

        @pl.loop(0, 8)
        def _(i):
            rows = pl.ds(pl.multiple_of(128 * q + 16 * i, 16), 16)
            mine = pl.ds(pl.multiple_of(256 + 128 * q + 16 * i, 16), 16)
            total = W[3, mine, a_cols].astype(F32)
            for n in range(2):
                total = total + ra2[n, rows, :].astype(F32)
            total_g[rows, a_cols] = total * scale
            total = W[3, mine, b_cols].astype(F32) + rb2[0, rows, :].astype(F32)
            for n in range(2):
                total = total + rb1[n, rows, :].astype(F32)
            total_g[rows, b_cols] = total * scale

        rows = pl.ds(128 * q, 128)
        written.append(load(total_g.at[rows], parts.at[rows]))

    for group in groups:
        if group not in ("t", "w", "r"):
            sent(group)
    for copy in written:
        copy.wait()


def results(
    tokens_all, parts, hist_in, hist_w, grad, loss, hist_in_new, hist_w_new, held, tile, sem_in, sem_out
):
    scalars = pltpu.make_async_copy(parts.at[pl.ds(256, 8), pl.ds(0, 128)], tile, sem_in.at[4])
    scalars.start()
    pieces = [pl.ds(64 * i, 64) for i in range(4)]
    ins = [
        pltpu.make_async_copy(parts.at[rows], held.at[rows], sem_in.at[i])
        for i, rows in enumerate(pieces)
    ]
    outs = [
        pltpu.make_async_copy(held.at[rows], grad.at[rows], sem_out.at[i])
        for i, rows in enumerate(pieces)
    ]
    for copy in ins:
        copy.start()
    for i in range(15):
        hist_in_new[i + 1] = hist_in[i]
        hist_w_new[i + 1] = hist_w[i]
    for copy, back in zip(ins, outs):
        copy.wait()
        back.start()
    scalars.wait()
    hist_in_new[0] = jnp.max(tile[0:1, :])
    hist_w_new[0] = jnp.max(tile[1:2, :])
    loss[0] = jnp.max(tile[2:3, :]) * (0.5 / (tokens_all * 8192))
    for back in outs:
        back.wait()


def local(
    teacher_in, teacher_resid, teacher_wo, teacher_gain, input_history, weight_history,
    student_hidden, student_gain, projection,
):
    tokens_all = teacher_in.shape[0] * lax.axis_size("context")
    smem = pl.BlockSpec(memory_space=pltpu.SMEM)
    hbm = pl.BlockSpec(memory_space=pl.ANY)
    parts = pl.pallas_call(
        functools.partial(kernel, tokens_all),
        name="distill",
        out_shape=jax.ShapeDtypeStruct((264, 1024), F32),
        in_specs=[smem, smem] + [hbm] * 7,
        out_specs=hbm,
        scratch_shapes=[
            pltpu.VMEM((1024, 2048), BF16),
            pltpu.VMEM((4, 512, 2048), BF16),
            pltpu.VMEM((4, 256, 4096), BF16),
            pltpu.VMEM((4096, 1024), BF16),
            pltpu.VMEM((1024, 1024), BF16),
            pltpu.VMEM((1024, 1024), F32),
            pltpu.VMEM((1024, 1024), F32),
            pltpu.VMEM((1024, 1024), BF16),
            pltpu.VMEM((1024, 1024), BF16),
            pltpu.VMEM((1024, 1024), BF16),
            pltpu.VMEM((128, 4096), BF16),
            pltpu.VMEM((32, 8192), BF16),
            pltpu.VMEM((1024, 128), F32),
            pltpu.VMEM((8, 8, 128), F32),
            pltpu.VMEM((19, 8, 128), F32),
            pltpu.VMEM((8, 256, 1024), BF16),
            pltpu.VMEM((4, 256, ACOLS), BF16),
            pltpu.VMEM((2, 256, ACOLS), BF16),
            pltpu.VMEM((4, 256, 1024 - ACOLS), BF16),
            pltpu.VMEM((1, 256, 1024 - ACOLS), BF16),
            pltpu.VMEM((2, 128, ACOLS), BF16),
            pltpu.VMEM((4, 128, 1024 - ACOLS), BF16),
            pltpu.VMEM((256, 1024), F32),
            pltpu.VMEM((1, 4096), F32),
            pltpu.VMEM((1, 1024), F32),
            pltpu.SemaphoreType.DMA((SEND_SEMS,)),
            pltpu.SemaphoreType.DMA((RECV_SEMS,)),
            pltpu.SemaphoreType.DMA((11,)),
        ],
        compiler_params=pltpu.CompilerParams(
            collective_id=0, has_side_effects=True, vmem_limit_bytes=62 << 20
        ),
        cost_estimate=pl.CostEstimate(
            flops=3 * 2 * 1024 * 1024 * 4096, bytes_accessed=16 << 20, transcendentals=1024
        ),
    )(
        input_history,
        weight_history,
        student_gain.reshape(1, -1),
        teacher_gain.reshape(1, -1),
        teacher_in,
        teacher_resid,
        teacher_wo,
        student_hidden,
        projection,
    )
    grad, loss, hist_in, hist_w = pl.pallas_call(
        functools.partial(results, tokens_all),
        name="results",
        out_shape=(
            jax.ShapeDtypeStruct((256, 1024), F32),
            jax.ShapeDtypeStruct((1,), F32),
            jax.ShapeDtypeStruct((16,), F32),
            jax.ShapeDtypeStruct((16,), F32),
        ),
        in_specs=[hbm, smem, smem],
        out_specs=(hbm, smem, smem, smem),
        scratch_shapes=[
            pltpu.VMEM((256, 1024), F32),
            pltpu.VMEM((8, 128), F32),
            pltpu.SemaphoreType.DMA((5,)),
            pltpu.SemaphoreType.DMA((4,)),
        ],
    )(parts, input_history, weight_history)
    return grad, loss.reshape(()), hist_in, hist_w


def solution(mesh):
    placed = (
        P("context", "tensor"),
        P("context", "tensor"),
        P("tensor", None),
        P(),
        P(),
        P(),
        P(("context", "tensor"), None),
        P(),
        P("context", "tensor"),
    )
    return jax.shard_map(
        local,
        mesh=mesh,
        in_specs=placed,
        out_specs=(P("context", "tensor"), P(), P(), P()),
        check_vma=False,
    )
```

```python
import functools
import math

import jax
import jax.numpy as jnp
from jax import lax
from jax.experimental import pallas as pl
from jax.experimental.pallas import tpu as pltpu
from jax.sharding import PartitionSpec as P

MESH = pl.DeviceIdType.MESH
F32, BF16 = jnp.float32, jnp.bfloat16
EPS = 1e-05
SEND_SEMS, RECV_SEMS = 7, 84
GROUP = 8 << 20
XROWS = 112
FIRST = 80
AROWS = 112


def lanes(tile):
    rows, width = tile.shape
    return [
        tile[r : r + 8, c : c + 128]
        for r in range(0, rows, 8)
        for c in range(0, width, 128)
    ]


def fold(op, tile):
    parts = lanes(tile)
    while len(parts) > 1:
        parts = [op(a, b) for a, b in zip(parts[::2], parts[1::2])] + (
            [parts[-1]] if len(parts) % 2 else []
        )
    return parts[0]


def kernel(
    tokens_all,
    hist_in_all, hist_w_all, stu_gain, tea_gain, tin, resid, wo, stu, proj,
    parts,
    T, W, S, PR, R, H, M, E, psend, precv, sraw, wraw, col, sq, scal, sib, ra1, ra2, rb1, rb2, am, bm, total_g, sgain, tgain, hist_in, hist_w,
    ssem, rsem, lsem,
):
    t, c = lax.axis_index("tensor"), lax.axis_index("context")
    y, xl = t // 2, t % 2
    xh, z, k = c // 8, (c // 2) % 4, c % 2

    def dev(dy=0, dxl=0, dxh=0, dz=0, dk=0):
        ny, nz = (y + dy) % 4, (z + dz) % 4
        nxl, nxh, nk = (xl + dxl) % 2, (xh + dxh) % 2, (k + dk) % 2
        return {"tensor": ny * 2 + nxl, "context": nxh * 8 + nz * 2 + nk}

    received, groups = [], {}

    def remote(src, dst, send_sem, recv_sem, to):
        return pltpu.make_async_remote_copy(
            src_ref=src,
            dst_ref=dst,
            send_sem=ssem.at[send_sem],
            recv_sem=rsem.at[recv_sem],
            device_id=to,
            device_id_type=MESH,
        )

    def size(ref):
        return math.prod(ref.shape) * jnp.dtype(ref.dtype).itemsize

    def send(src, dst, group=None, **to):
        if group is None:
            group = next((n for n in range(50) if groups.get(n, (0, 0))[1] + size(src) <= GROUP), 0)
        index, held = groups.get(group, (len(groups), 0))
        groups[group] = index, held + size(src)
        received.append(len(received))
        copy = remote(src, dst, index, received[-1], dev(**to))
        copy.start()
        return copy

    def span(count):
        if count % 32768 == 0:
            return PR.at[pl.ds(0, count // 2048)]
        return col.at[pl.ds(0, count // 512)]

    def sent(group):
        index, held = groups[group]
        rows = span(held)
        remote(rows, rows, index, 0, dev(dk=1)).wait_send()

    def send_all(pieces, group=None):
        received.append(len(received))
        at, total = received[-1], 0
        for src, dst, to in pieces:
            key = group
            if key is None:
                key = next(n for n in range(50) if groups.get(n, (0, 0))[1] + size(src) <= GROUP)
            index, held = groups.get(key, (len(groups), 0))
            groups[key] = index, held + size(src)
            remote(src, dst, index, at, dev(**to)).start()
            total += size(src)
        return at, total

    def await_group(landed):
        at, total = landed
        rows = span(total)
        remote(rows, rows, 0, at, dev(dk=1)).wait_recv()

    local = []

    def load(src, dst):
        copy = pltpu.make_async_copy(src, dst, lsem.at[len(local)])
        copy.start()
        local.append(copy)
        return copy

    TENSOR = [(dy, dx) for dy in range(4) for dx in range(2) if (dy, dx) != (0, 0)]
    CONTEXT = [(dx, dz) for dx in range(2) for dz in range(4) if (dx, dz) != (0, 0)]
    UP, DOWN = 1, 3

    slab = pl.multiple_of(64 * (2 * z + k) + 32 * xh, 32)
    l_wraw = load(wo.at[pl.ds(slab, 32)], wraw)
    l_hist = load(hist_in_all, hist_in), load(hist_w_all, hist_w)
    l_sgain = load(stu_gain, sgain)
    l_tgain = load(tea_gain.at[:, pl.ds(pl.multiple_of(1024 * t, 1024), 1024)], tgain)
    l_proj = load(proj, PR.at[pl.ds(pl.multiple_of(256 * c, 256), 256)])
    l_stu = load(stu, sraw)
    l_tin = load(tin, T.at[:, pl.ds(0, 512)])
    l_wown = load(wo.at[:, pl.ds(pl.multiple_of(2048 * y, 2048), 2048)], W.at[0])
    l_res = load(resid, R)

    barrier = pltpu.get_barrier_semaphore()
    for dy, dx in TENSOR:
        pl.semaphore_signal(barrier, 1, device_id=dev(dy=dy, dxl=dx), device_id_type=MESH)
    for dx, dz in CONTEXT:
        pl.semaphore_signal(barrier, 1, device_id=dev(dxh=dx, dz=dz), device_id_type=MESH)
    pl.semaphore_signal(barrier, 1, device_id=dev(dk=1), device_id_type=MESH)

    for copy in l_hist:
        copy.wait()
    lim_in, lim_w = hist_in[0], hist_w[0]
    for i in range(1, 16):
        lim_in = jnp.maximum(lim_in, hist_in[i])
        lim_w = jnp.maximum(lim_w, hist_w[i])

    l_wraw.wait()

    def clip_w(i, amax):
        rows = pl.ds(pl.multiple_of(16 * i, 16), 16)
        for n in range(8):
            cols = pl.ds(1024 * n, 1024)
            v = wraw[rows, cols].astype(F32)
            amax = jnp.maximum(amax, fold(jnp.maximum, jnp.abs(v)))
            wraw[rows, cols] = jnp.clip(v, -lim_w, lim_w).astype(BF16)
        return amax

    amax_w = lax.fori_loop(0, 2, clip_w, jnp.zeros((8, 128), F32))

    pl.semaphore_wait(barrier, len(TENSOR) + len(CONTEXT) + 1)

    def wcols(d):
        return pl.ds(pl.multiple_of(2048 * ((y + d) % 4), 2048), 2048)

    w_y = send_all(
        [(wraw.at[:, wcols(d)], W.at[4 - d, pl.ds(slab, 32)], {"dy": d}) for d in (2, 1, 3)]
    )
    l_proj.wait()

    def pblock(dxh=0, dz=0):
        at = ((xh + dxh) % 2) * 8 + ((z + dz) % 4) * 2 + k
        return PR.at[pl.ds(pl.multiple_of(256 * at, 256), 256)]

    p_x = send(pblock(), pblock(), dxh=1)
    p_up = send(pblock(), pblock(), dz=UP)
    p_dn = send(pblock(), pblock(), dz=DOWN)
    p_sib = [send(pblock(), pblock(), dk=1)]

    l_stu.wait()
    l_sgain.wait()

    @pl.loop(0, 8)
    def _(i):
        rows = pl.ds(pl.multiple_of(16 * i, 16), 16)
        v = sraw[rows, :].astype(F32)
        mean = jnp.mean(v * v, axis=1, keepdims=True)
        S[0, rows, :] = (v * lax.rsqrt(mean + EPS) * sgain[...]).astype(BF16)

    nx = XROWS
    ny = 128 - nx
    own_x, own_y = pl.ds(0, nx), pl.ds(nx, ny)
    far_x, far_y = pl.ds(128, nx), pl.ds(128 + nx, ny)
    sy_up = send(S.at[0, own_y], S.at[3, own_y], dy=UP)
    sy_dn = send(S.at[0, own_y], S.at[1, own_y], dy=DOWN)
    sxy = [send(S.at[0, own_y], S.at[0, far_y], dxl=1)]

    l_tin.wait()

    def clip_t(i, amax):
        rows = pl.ds(pl.multiple_of(32 * i, 32), 32)
        v = T[rows, pl.ds(0, 512)].astype(F32)
        T[rows, pl.ds(0, 512)] = jnp.clip(v, -lim_in, lim_in).astype(BF16)
        return jnp.maximum(amax, fold(jnp.maximum, jnp.abs(v)))

    amax_in = lax.fori_loop(0, 32, clip_t, jnp.zeros((8, 128), F32))
    low, high = pl.ds(0, 512), pl.ds(512, 512)

    def tblock(r, rows):
        return T.at[rows, pl.ds(512 * r, 512)]

    t_up = send(tblock(0, low), tblock(3, low), "t", dy=UP)
    t_dn = send(tblock(0, high), tblock(1, high), "t", dy=DOWN)
    t_up1 = send(tblock(0, high), tblock(3, high), "t", dy=UP)
    t_dn1 = send(tblock(0, low), tblock(1, low), "t", dy=DOWN)

    def wslab(dz=0, dxh=None):
        at = pl.multiple_of(64 * (2 * ((z + dz) % 4) + k), 64)
        if dxh is None:
            return W.at[pl.ds(1, 3), pl.ds(at, 64)]
        return W.at[pl.ds(1, 3), pl.ds(pl.multiple_of(at + 32 * ((xh + dxh) % 2), 32), 32)]

    await_group(w_y)
    w_x = send(wslab(0, 0), wslab(0, 0), "w", dxh=1)
    w_up = send(wslab(0, 0), wslab(0, 0), "w", dz=UP)
    w_dn = send(wslab(0, 0), wslab(0, 0), "w", dz=DOWN)
    sx = send(S.at[0, own_x], S.at[0, far_x], dxl=1)

    l_wown.wait()

    @pl.loop(0, 32)
    def _(i):
        rows = pl.ds(pl.multiple_of(16 * i, 16), 16)
        v = W[0, rows, :].astype(F32)
        W[0, rows, :] = jnp.clip(v, -lim_w, lim_w).astype(BF16)

    sy_up.wait_recv()
    sxy.append(send(S.at[3, own_y], S.at[3, far_y], dxl=1))
    sy_dn.wait_recv()
    sxy.append(send(S.at[1, own_y], S.at[1, far_y], dxl=1))
    w_x.wait_recv()
    v_dn = send(wslab(0, 1), wslab(0, 1), "w", dz=DOWN)
    v_up = send(wslab(0, 1), wslab(0, 1), "w", dz=UP)
    w_sib = [send(wslab(), wslab(), "w", dk=1)]

    left, right = pl.ds(0, 2048), pl.ds(2048, 2048)
    t_up.wait_recv()
    t_up2 = send(tblock(3, low), tblock(2, low), "t", dy=UP)
    t_dn.wait_recv()
    t_dn2 = send(tblock(1, high), tblock(2, high), "t", dy=DOWN)
    sy_up2 = send(S.at[3, own_y, left], S.at[2, own_y, left], dy=UP)
    sy_dn2 = send(S.at[1, own_y, right], S.at[2, own_y, right], dy=DOWN)
    a_up = send(S.at[0, own_x], S.at[3, own_x], dy=UP)

    w_up.wait_recv()
    w_up2 = send(wslab(DOWN, 0), wslab(DOWN, 0), "w", dz=UP)
    v_dn.wait_recv()
    v_dn2 = send(wslab(UP, 1), wslab(UP, 1), "w", dz=DOWN)
    v_up.wait_recv()
    w_sib.append(send(wslab(DOWN), wslab(DOWN), "w", dk=1))
    w_dn.wait_recv()
    w_sib.append(send(wslab(UP), wslab(UP), "w", dk=1))

    sx.wait_recv()
    b_dn = send(S.at[0, far_x], S.at[1, far_x], dy=DOWN)
    b_up = send(S.at[0, far_x], S.at[3, far_x], dy=UP)
    a_dn = send(S.at[0, own_x], S.at[1, own_x], dy=DOWN)

    w_up2.wait_recv()
    v_dn2.wait_recv()
    w_sib.append(send(wslab(2), wslab(2), "w", dk=1))
    p_x.wait_recv()
    p_sib.append(send(pblock(1), pblock(1), dk=1))
    q_dn = send(pblock(1), pblock(1), dz=DOWN)
    q_up = send(pblock(1), pblock(1), dz=UP)
    p_up.wait_recv()
    p_up2 = send(pblock(0, DOWN), pblock(0, DOWN), dz=UP)
    p_sib.append(send(pblock(0, DOWN), pblock(0, DOWN), dk=1))
    p_dn.wait_recv()
    p_sib.append(send(pblock(0, UP), pblock(0, UP), dk=1))

    for copy in t_up1, t_dn1, t_up2, t_dn2, *w_sib:
        copy.wait_recv()

    def product(rows, col0, n):
        cols = pl.ds(pl.multiple_of(col0 + 256 * n, 256), 256)
        w = W[:, :, cols].reshape(2048, 256)
        return jnp.dot(T[rows, :], w, preferred_element_type=F32)

    rs_t = []
    for q in range(4):
        rows = pl.ds(256 * q, 256)

        @pl.loop(0, 4)
        def _(n):
            cols = pl.ds(pl.multiple_of(256 * n, 256), 256)
            psend[rows, cols] = product(rows, 1024 * (1 - xl), n).astype(BF16)

        for rows in (rows,) if q < 3 else (pl.ds(768, 128), pl.ds(896, 128)):
            rs_t.append(send(psend.at[rows], precv.at[rows], "r", dxl=1))


    sy_up2.wait_recv()
    sy_dn2.wait_recv()
    sxy.append(send(S.at[2, own_y], S.at[2, far_y], dxl=1))
    l_res.wait()
    for q in range(4):
        rows = pl.ds(256 * q, 256)

        @pl.loop(0, 4)
        def _(n):
            cols = pl.ds(pl.multiple_of(256 * n, 256), 256)
            H[rows, cols] = product(rows, 1024 * xl, n) + R[rows, cols].astype(F32)

    q_dn.wait_recv()
    q_dn2 = send(pblock(1, UP), pblock(1, UP), dz=DOWN)
    p_sib.append(send(pblock(1, UP), pblock(1, UP), dk=1))
    q_up.wait_recv()
    p_sib.append(send(pblock(1, DOWN), pblock(1, DOWN), dk=1))
    p_up2.wait_recv()
    p_sib.append(send(pblock(0, 2), pblock(0, 2), dk=1))
    first_x = pl.ds(0, FIRST), pl.ds(128, FIRST)
    last_x = pl.ds(FIRST, nx - FIRST), pl.ds(128 + FIRST, nx - FIRST)
    a_up.wait_recv()
    a_up2 = send(S.at[3, first_x[0]], S.at[2, first_x[0]], dy=UP)
    b_dn.wait_recv()
    b_dn2 = send(S.at[1, first_x[1]], S.at[2, first_x[1]], dy=DOWN)
    q_dn2.wait_recv()
    p_sib.append(send(pblock(1, 2), pblock(1, 2), dk=1))

    def mapped(r):
        @pl.loop(0, 2)
        def _(n):
            cols = pl.ds(pl.multiple_of(512 * n, 512), 512)
            M[pl.ds(256 * r, 256), cols] = jnp.dot(
                S[r], PR[:, cols], preferred_element_type=F32
            )

    def mapped_part(first, count):
        @pl.loop(0, 2)
        def _(n):
            cols = pl.ds(pl.multiple_of(512 * n, 512), 512)
            own, far = pl.ds(first, count), pl.ds(128 + first, count)
            rows = jnp.concatenate([S[2, own], S[2, far]], axis=0)
            out = jnp.dot(rows, PR[:, cols], preferred_element_type=F32)
            M[pl.ds(512 + first, count), cols] = out[:count]
            M[pl.ds(640 + first, count), cols] = out[count:]

    ORDER = [(1, 2), (0, 2), (1, 1), (1, 3), (1, 0), (0, 1), (0, 3), (0, 0)]

    def turned(g):
        if g < 4:
            return T, 512 * (g % 2), 1024 * (g // 2)
        return (R, psend)[g // 2 - 2], 512 * (g % 2), 0

    def turn(g, r):
        dxh, dz = ORDER[g]
        chip = ((xh + dxh) % 2) * 4 + (z + dz) % 4
        ref, row0, col0 = turned(g)
        for own in (0, 1):
            cols = pl.ds(pl.multiple_of(512 * chip + 256 * ((k + 1 - own) % 2), 256), 256)
            ref[pl.ds(row0 + 256 * own, 256), pl.ds(col0 + 256 * r, 256)] = S[r, :, cols].T

    def turn_first(r):
        for g in range(4):
            turn(g, r)

    l_tgain.wait()
    gains = tgain[...]

    def squares(q):
        rs_t[q].wait_recv()
        first, count = (256 * q, 256) if q < 3 else (128 * q + 384, 128)

        @pl.loop(0, count // 16)
        def _(i):
            rows = pl.ds(pl.multiple_of(first + 16 * i, 16), 16)
            h = H[rows, :] + precv[rows, :].astype(F32)
            H[rows, :] = h * gains
            col[rows, :] = jnp.broadcast_to(jnp.sum(h * h, axis=1, keepdims=True), (16, 128))

    for copy in p_sib:
        copy.wait_recv()
    sxy[0].wait_recv()
    mapped(0)
    sent("t")
    turn_first(0)
    squares(0)
    squares(1)
    squares(2)
    b_up.wait_recv()
    sxy[1].wait_recv()
    mapped(3)
    turn_first(3)
    a_dn.wait_recv()
    sxy[2].wait_recv()
    mapped(1)
    squares(3)
    squares(4)
    row = lax.broadcasted_iota(jnp.int32, (8, 128), 0)
    packed = jnp.zeros((8, 128), F32)
    for i in range(8):
        packed = jnp.where(row == i, col[pl.ds(128 * i, 128), :].T[0:8, :], packed)
    sq[0] = packed
    sq_c = send_all(
        [(sq.at[0], sq.at[dy * 2 + dx], {"dy": dy, "dxl": dx}) for dy, dx in TENSOR], "s"
    )
    a_up3 = send(S.at[3, last_x[0]], S.at[2, last_x[0]], dy=UP)
    b_dn3 = send(S.at[1, last_x[1]], S.at[2, last_x[1]], dy=DOWN)
    turn_first(1)

    def errors(r, acc):
        for b in range(2):
            base = 128 * (2 * ((y + r) % 4) + (xl + b) % 2)

            def step(i, acc):
                there = pl.ds(pl.multiple_of(base + 16 * i, 16), 16)
                here = pl.ds(pl.multiple_of(256 * r + 128 * b + 16 * i, 16), 16)
                scale = jnp.concatenate([col[there, :]] * 8, axis=1)
                e = M[here, :] - H[there, :] * scale
                E[here, :] = e.astype(BF16)
                return acc + fold(jnp.add, e * e)

            acc = lax.fori_loop(0, 8, step, acc, unroll=2)
        return acc

    a_up2.wait_recv()
    b_dn2.wait_recv()
    mapped_part(0, FIRST)
    await_group(sq_c)
    total = sq[0]
    for i in range(1, 8):
        total = total + sq[i]
    inv = lax.rsqrt(total * (1.0 / 8192) + EPS)
    for i in range(8):
        col[pl.ds(128 * i, 128), :] = jnp.broadcast_to(inv[i : i + 1, :], (128, 128)).T
    acc = jnp.zeros((8, 128), F32)
    for r in (0, 3, 1):
        acc = errors(r, acc)
    sxy[3].wait_recv()
    a_up3.wait_recv()
    b_dn3.wait_recv()
    mapped_part(FIRST, 128 - FIRST)
    acc = errors(2, acc)

    tile = jnp.where(row == 0, jnp.max(amax_in), jnp.where(row == 1, jnp.max(amax_w), jnp.sum(acc)))

    def merge(first, count):
        out = scal[first]
        for i in range(1, count):
            v = scal[first + i]
            out = jnp.where(row < 2, jnp.maximum(out, v), out + v)
        return out

    scal[t] = tile
    sc1 = send_all([(scal.at[t], scal.at[t], {"dy": dy, "dxl": dx}) for dy, dx in TENSOR], "s")

    sent("w")
    sent("r")

    a_rows, b_rows = (0, AROWS), (AROWS, 256 - AROWS)
    a_up_rows, a_dn_rows = (0, 48), (48, AROWS - 48)
    b_up_rows, b_dn_rows = (AROWS, 80), (AROWS + 80, 176 - AROWS)

    def gslot(dxh, dz, rows=(0, 256), other=0):
        g = ORDER.index((dxh, dz))
        return W.at[g // 2, pl.ds(256 * (g % 2) + rows[0], rows[1]), pl.ds(1024 * other, 1024)]

    to_sib, a_1, b_1, a_2, a_m, b_m = [], {}, {}, {}, {}, {}

    def half_term(g, own):
        dxh, dz = ORDER[g]
        ref, row0, col0 = turned(g)

        @pl.loop(0, 2)
        def _(n):
            at = pl.multiple_of(512 * n, 512)
            one = jnp.dot(
                ref[pl.ds(row0 + 256 * own, 256), pl.ds(col0, 1024)],
                E[:, pl.ds(at, 512)],
                preferred_element_type=F32,
            )
            start = pl.multiple_of(1024 * (1 - own) + at, 512)
            W[g // 2, pl.ds(256 * (g % 2), 256), pl.ds(start, 512)] = one.astype(BF16)

        if own == 0:
            to_sib.append(send(gslot(dxh, dz, other=1), sib.at[g], dk=1))

    def term(g):
        dxh, dz = ORDER[g]
        ref, row0, col0 = turned(g)

        @pl.loop(0, 2)
        def _(n):
            at = pl.multiple_of(512 * n, 512)
            both = jnp.dot(
                ref[pl.ds(row0, 512), pl.ds(col0, 1024)],
                E[:, pl.ds(at, 512)],
                preferred_element_type=F32,
            ).astype(BF16)
            rows = pl.ds(256 * (g % 2), 256)
            W[g // 2, rows, pl.ds(pl.multiple_of(1024 + at, 512), 512)] = both[:256]
            W[g // 2, rows, pl.ds(at, 512)] = both[256:]

        to_sib.append(send(gslot(dxh, dz, other=1), sib.at[g], dk=1))

    def add(dxh, dz, rows, others):
        g = ORDER.index((dxh, dz))

        @pl.loop(0, rows[1] // 16)
        def _(i):
            here = pl.ds(pl.multiple_of(16 * i, 16), 16)
            there = pl.ds(pl.multiple_of(256 * (g % 2) + rows[0] + 16 * i, 16), 16)
            total = W[g // 2, there, pl.ds(0, 1024)].astype(F32)
            for ref, index in others:
                total = total + ref[index, here, :].astype(F32)
            W[g // 2, there, pl.ds(0, 1024)] = total.astype(BF16)

    def along_z(dxh, dz, rows, up, dn, mid, at, far, gone, passed):
        if dz == 2:
            passed[dxh, UP] = send(gslot(dxh, 2, up), mid.at[at, pl.ds(0, up[1])], dz=UP)
            passed[dxh, DOWN] = send(gslot(dxh, 2, dn), mid.at[at + 1, pl.ds(0, dn[1])], dz=DOWN)
        elif dz:
            passed[dxh, dz].wait_recv()
            add(dxh, dz, up if dz == UP else dn, [(mid, at + dz // 2)])
            gone[dxh, dz] = send(gslot(dxh, dz, rows), far.at[at + dz // 2], dz=dz)

    def finish(g):
        dxh, dz = ORDER[g]
        to_sib[g].wait_recv()
        add(dxh, dz, (0, 256), [(sib, g)])
        if dxh:
            a_1[dz] = send(gslot(dxh, dz, a_rows), ra1.at[dz], dxh=1)

    def second_b(dxh, dz):
        along_z(dxh, dz, b_rows, b_up_rows, b_dn_rows, bm, 2 * dxh, rb1, b_1, b_m)

    def second_a(dz):
        a_1[dz].wait_recv()
        add(0, dz, a_rows, [(ra1, dz)])
        along_z(0, dz, a_rows, a_up_rows, a_dn_rows, am, 0, ra2, a_2, a_m)

    def term_of(g):
        for r in range(4) if g >= 4 else (2,):
            turn(g, r)
        term(g)

    turn(0, 2)
    half_term(0, 0)
    half_term(0, 1)
    turn(1, 2)
    half_term(1, 0)
    finish(0)
    second_b(1, 2)
    half_term(1, 1)
    await_group(sc1)
    at = 8 + xh * 4 + z
    scal[at] = merge(0, 8)
    sc2 = send_all([(scal.at[at], scal.at[at], {"dxh": dx, "dz": dz}) for dx, dz in CONTEXT], "s")
    term_of(2)
    finish(1)
    second_b(0, 2)
    term_of(3)
    finish(2)
    second_b(1, 1)
    term_of(4)
    finish(3)
    second_b(1, 3)
    second_a(2)
    term_of(5)
    finish(4)
    term_of(6)
    finish(5)
    second_b(0, 1)
    term_of(7)
    finish(6)
    second_b(0, 3)
    for n in (UP, DOWN):
        b_1[1, n].wait_recv()
    add(1, 0, b_rows, [(rb1, 2), (rb1, 3)])
    b_2 = send(gslot(1, 0, b_rows), rb2.at[0], dxh=1)
    second_a(1)
    second_a(3)
    await_group(sc2)
    scal[16 + k] = merge(8, 8)
    sc3 = send(scal.at[16 + k], scal.at[16 + k], "s", dk=1)
    finish(7)
    second_a(0)
    sc3.wait_recv()
    scal[18] = merge(16, 2)
    written = [load(scal.at[18], parts.at[pl.ds(256, 8), pl.ds(0, 128)])]

    for n in (UP, DOWN):
        b_1[0, n].wait_recv()
        a_2[0, n].wait_recv()
    b_2.wait_recv()
    scale = 1.0 / math.sqrt(tokens_all)
    for (first, count), landed in (
        (b_rows, [(rb1, 0), (rb1, 1), (rb2, 0)]),
        (a_rows, [(ra2, 0), (ra2, 1)]),
    ):

        @pl.loop(0, count // 16)
        def _(i):
            here = pl.ds(pl.multiple_of(16 * i, 16), 16)
            mine = pl.ds(pl.multiple_of(256 + first + 16 * i, 16), 16)
            total = W[3, mine, pl.ds(0, 1024)].astype(F32)
            for ref, index in landed:
                total = total + ref[index, here, :].astype(F32)
            total_g[pl.ds(pl.multiple_of(first + 16 * i, 16), 16), :] = total * scale

        rows = pl.ds(first, count)
        written.append(load(total_g.at[rows], parts.at[rows]))

    assert len(groups) <= SEND_SEMS and len(received) <= RECV_SEMS
    for group in groups:
        if group not in ("t", "w", "r"):
            sent(group)
    for copy in written:
        copy.wait()


def results(
    tokens_all, parts, hist_in, hist_w, grad, loss, hist_in_new, hist_w_new,
    held, tile, s_in, s_w, s_in_new, s_w_new, s_loss, sem_in, sem_out,
):
    pieces = [pl.ds(64 * i, 64) for i in range(4)]
    copies = [
        (parts.at[pl.ds(256, 8), pl.ds(0, 128)], tile),
        (hist_in, s_in),
        (hist_w, s_w),
        *((parts.at[rows], held.at[rows]) for rows in pieces),
    ]
    copies = [pltpu.make_async_copy(a, b, sem_in.at[i]) for i, (a, b) in enumerate(copies)]
    for copy in copies:
        copy.start()
    backs = [
        *((held.at[rows], grad.at[rows]) for rows in pieces),
        (s_in_new, hist_in_new),
        (s_w_new, hist_w_new),
        (s_loss, loss),
    ]
    backs = [pltpu.make_async_copy(a, b, sem_out.at[i]) for i, (a, b) in enumerate(backs)]
    for copy in copies[:3]:
        copy.wait()
    s_in_new[0] = jnp.max(tile[0:1, :])
    s_w_new[0] = jnp.max(tile[1:2, :])
    s_loss[0] = jnp.max(tile[2:3, :]) * (0.5 / (tokens_all * 8192))
    for i in range(15):
        s_in_new[i + 1] = s_in[i]
        s_w_new[i + 1] = s_w[i]
    for back in backs[4:]:
        back.start()
    for copy, back in zip(copies[3:], backs):
        copy.wait()
        back.start()
    for back in backs:
        back.wait()


def local(
    teacher_in, teacher_resid, teacher_wo, teacher_gain, input_history, weight_history,
    student_hidden, student_gain, projection,
):
    tokens_all = teacher_in.shape[0] * lax.axis_size("context")
    hbm = pl.BlockSpec(memory_space=pl.ANY)
    parts = pl.pallas_call(
        functools.partial(kernel, tokens_all),
        name="distill",
        out_shape=jax.ShapeDtypeStruct((264, 1024), F32),
        in_specs=[hbm] * 9,
        out_specs=hbm,
        scratch_shapes=[
            pltpu.VMEM((1024, 2048), BF16),
            pltpu.VMEM((4, 512, 2048), BF16),
            pltpu.VMEM((4, 256, 4096), BF16),
            pltpu.VMEM((4096, 1024), BF16),
            pltpu.VMEM((1024, 1024), BF16),
            pltpu.VMEM((1024, 1024), F32),
            pltpu.VMEM((1024, 1024), F32),
            pltpu.VMEM((1024, 1024), BF16),
            pltpu.VMEM((1024, 1024), BF16),
            pltpu.VMEM((1024, 1024), BF16),
            pltpu.VMEM((128, 4096), BF16),
            pltpu.VMEM((32, 8192), BF16),
            pltpu.VMEM((1024, 128), F32),
            pltpu.VMEM((8, 8, 128), F32),
            pltpu.VMEM((19, 8, 128), F32),
            pltpu.VMEM((8, 256, 1024), BF16),
            pltpu.VMEM((4, AROWS, 1024), BF16),
            pltpu.VMEM((2, AROWS, 1024), BF16),
            pltpu.VMEM((4, 256 - AROWS, 1024), BF16),
            pltpu.VMEM((1, 256 - AROWS, 1024), BF16),
            pltpu.VMEM((2, 64, 1024), BF16),
            pltpu.VMEM((4, 80, 1024), BF16),
            pltpu.VMEM((256, 1024), F32),
            pltpu.VMEM((1, 4096), F32),
            pltpu.VMEM((1, 1024), F32),
            pltpu.SMEM((16,), F32),
            pltpu.SMEM((16,), F32),
            pltpu.SemaphoreType.DMA((SEND_SEMS,)),
            pltpu.SemaphoreType.DMA((RECV_SEMS,)),
            pltpu.SemaphoreType.DMA((13,)),
        ],
        compiler_params=pltpu.CompilerParams(
            collective_id=0, has_side_effects=True, vmem_limit_bytes=62 << 20
        ),
        cost_estimate=pl.CostEstimate(
            flops=3 * 2 * 1024 * 1024 * 4096, bytes_accessed=16 << 20, transcendentals=1024
        ),
    )(
        input_history,
        weight_history,
        student_gain.reshape(1, -1),
        teacher_gain.reshape(1, -1),
        teacher_in,
        teacher_resid,
        teacher_wo,
        student_hidden,
        projection,
    )
    grad, loss, hist_in, hist_w = pl.pallas_call(
        functools.partial(results, tokens_all),
        name="results",
        out_shape=(
            jax.ShapeDtypeStruct((256, 1024), F32),
            jax.ShapeDtypeStruct((1,), F32),
            jax.ShapeDtypeStruct((16,), F32),
            jax.ShapeDtypeStruct((16,), F32),
        ),
        in_specs=[hbm] * 3,
        out_specs=(hbm,) * 4,
        scratch_shapes=[
            pltpu.VMEM((256, 1024), F32),
            pltpu.VMEM((8, 128), F32),
            *(pltpu.SMEM((n,), F32) for n in (16, 16, 16, 16, 1)),
            pltpu.SemaphoreType.DMA((7,)),
            pltpu.SemaphoreType.DMA((7,)),
        ],
    )(parts, input_history, weight_history)
    return grad, loss.reshape(()), hist_in, hist_w


def solution(mesh):
    placed = (
        P("context", "tensor"),
        P("context", "tensor"),
        P("tensor", None),
        P(),
        P(),
        P(),
        P(("context", "tensor"), None),
        P(),
        P("context", "tensor"),
    )
    return jax.shard_map(
        local,
        mesh=mesh,
        in_specs=placed,
        out_specs=(P("context", "tensor"), P(), P(), P()),
        check_vma=False,
    )
```

```python
import functools
import math

import jax
import jax.numpy as jnp
from jax import lax
from jax.experimental import pallas as pl
from jax.experimental.pallas import tpu as pltpu
from jax.sharding import PartitionSpec as P

MESH = pl.DeviceIdType.MESH
F32, BF16 = jnp.float32, jnp.bfloat16
EPS = 1e-05
SEND_SEMS, RECV_SEMS = 7, 88
GROUP = 8 << 20
XCOLS = 3456
PIECES = (0, 1408), (1408, 1408), (2816, 640)
AROWS = 112


def lanes(tile):
    rows, width = tile.shape
    return [
        tile[r : r + 8, c : c + 128]
        for r in range(0, rows, 8)
        for c in range(0, width, 128)
    ]


def fold(op, tile):
    parts = lanes(tile)
    while len(parts) > 1:
        parts = [op(a, b) for a, b in zip(parts[::2], parts[1::2])] + (
            [parts[-1]] if len(parts) % 2 else []
        )
    return parts[0]


def kernel(
    tokens_all,
    hist_in_all, hist_w_all, stu_gain, tea_gain, tin, resid, wo, stu, proj,
    parts,
    T, W, S, PR, R, H, M, E, psend, precv, sraw, wraw, col, sq, scal, sib, ra1, ra2, rb1, rb2, am, bm, total_g, sgain, tgain, hist_in, hist_w,
    ssem, rsem, lsem,
):
    t, c = lax.axis_index("tensor"), lax.axis_index("context")
    y, xl = t // 2, t % 2
    xh, z, k = c // 8, (c // 2) % 4, c % 2

    def dev(dy=0, dxl=0, dxh=0, dz=0, dk=0):
        ny, nz = (y + dy) % 4, (z + dz) % 4
        nxl, nxh, nk = (xl + dxl) % 2, (xh + dxh) % 2, (k + dk) % 2
        return {"tensor": ny * 2 + nxl, "context": nxh * 8 + nz * 2 + nk}

    received, groups = [], {}

    def remote(src, dst, send_sem, recv_sem, to):
        return pltpu.make_async_remote_copy(
            src_ref=src,
            dst_ref=dst,
            send_sem=ssem.at[send_sem],
            recv_sem=rsem.at[recv_sem],
            device_id=to,
            device_id_type=MESH,
        )

    def size(ref):
        return math.prod(ref.shape) * jnp.dtype(ref.dtype).itemsize

    def send(src, dst, group=None, **to):
        if group is None:
            group = next((n for n in range(50) if groups.get(n, (0, 0))[1] + size(src) <= GROUP), 0)
        index, held = groups.get(group, (len(groups), 0))
        groups[group] = index, held + size(src)
        received.append(len(received))
        copy = remote(src, dst, index, received[-1], dev(**to))
        copy.start()
        return copy

    def span(count):
        if count % 32768 == 0:
            return PR.at[pl.ds(0, count // 2048)]
        return col.at[pl.ds(0, count // 512)]

    def sent(group):
        index, held = groups[group]
        rows = span(held)
        remote(rows, rows, index, 0, dev(dk=1)).wait_send()

    def send_all(pieces, group=None):
        received.append(len(received))
        at, total = received[-1], 0
        for src, dst, to in pieces:
            key = group
            if key is None:
                key = next(n for n in range(50) if groups.get(n, (0, 0))[1] + size(src) <= GROUP)
            index, held = groups.get(key, (len(groups), 0))
            groups[key] = index, held + size(src)
            remote(src, dst, index, at, dev(**to)).start()
            total += size(src)
        return at, total

    def await_group(landed):
        at, total = landed
        rows = span(total)
        remote(rows, rows, 0, at, dev(dk=1)).wait_recv()

    local = []

    def load(src, dst):
        copy = pltpu.make_async_copy(src, dst, lsem.at[len(local)])
        copy.start()
        local.append(copy)
        return copy

    TENSOR = [(dy, dx) for dy in range(4) for dx in range(2) if (dy, dx) != (0, 0)]
    CONTEXT = [(dx, dz) for dx in range(2) for dz in range(4) if (dx, dz) != (0, 0)]
    UP, DOWN = 1, 3

    slab = pl.multiple_of(64 * (2 * z + k) + 32 * xh, 32)
    l_wraw = load(wo.at[pl.ds(slab, 32)], wraw)
    l_hist = load(hist_in_all, hist_in), load(hist_w_all, hist_w)
    l_sgain = load(stu_gain, sgain)
    l_tgain = load(tea_gain.at[:, pl.ds(pl.multiple_of(1024 * t, 1024), 1024)], tgain)
    l_proj = load(proj, PR.at[pl.ds(pl.multiple_of(256 * c, 256), 256)])
    l_stu = load(stu, sraw)
    l_tin = load(tin, T.at[:, pl.ds(0, 512)])
    l_wown = load(wo.at[:, pl.ds(pl.multiple_of(2048 * y, 2048), 2048)], W.at[0])
    l_res = load(resid, R)

    barrier = pltpu.get_barrier_semaphore()
    for dy, dx in TENSOR:
        pl.semaphore_signal(barrier, 1, device_id=dev(dy=dy, dxl=dx), device_id_type=MESH)
    for dx, dz in CONTEXT:
        pl.semaphore_signal(barrier, 1, device_id=dev(dxh=dx, dz=dz), device_id_type=MESH)
    pl.semaphore_signal(barrier, 1, device_id=dev(dk=1), device_id_type=MESH)

    for copy in l_hist:
        copy.wait()
    lim_in, lim_w = hist_in[0], hist_w[0]
    for i in range(1, 16):
        lim_in = jnp.maximum(lim_in, hist_in[i])
        lim_w = jnp.maximum(lim_w, hist_w[i])

    l_wraw.wait()

    def clip_w(i, amax):
        rows = pl.ds(pl.multiple_of(16 * i, 16), 16)
        for n in range(8):
            cols = pl.ds(1024 * n, 1024)
            v = wraw[rows, cols].astype(F32)
            amax = jnp.maximum(amax, fold(jnp.maximum, jnp.abs(v)))
            wraw[rows, cols] = jnp.clip(v, -lim_w, lim_w).astype(BF16)
        return amax

    amax_w = lax.fori_loop(0, 2, clip_w, jnp.zeros((8, 128), F32))

    pl.semaphore_wait(barrier, len(TENSOR) + len(CONTEXT) + 1)

    def wcols(d):
        return pl.ds(pl.multiple_of(2048 * ((y + d) % 4), 2048), 2048)

    w_y = send_all(
        [(wraw.at[:, wcols(d)], W.at[4 - d, pl.ds(slab, 32)], {"dy": d}) for d in (2, 1, 3)]
    )
    l_proj.wait()

    def pblock(dxh=0, dz=0):
        at = ((xh + dxh) % 2) * 8 + ((z + dz) % 4) * 2 + k
        return PR.at[pl.ds(pl.multiple_of(256 * at, 256), 256)]

    p_x = send(pblock(), pblock(), dxh=1)
    p_up = send(pblock(), pblock(), dz=UP)
    p_dn = send(pblock(), pblock(), dz=DOWN)
    p_sib = [send(pblock(), pblock(), dk=1)]

    l_stu.wait()
    l_sgain.wait()

    @pl.loop(0, 8)
    def _(i):
        rows = pl.ds(pl.multiple_of(16 * i, 16), 16)
        v = sraw[rows, :].astype(F32)
        mean = jnp.mean(v * v, axis=1, keepdims=True)
        S[0, rows, :] = (v * lax.rsqrt(mean + EPS) * sgain[...]).astype(BF16)

    own, far = pl.ds(0, 128), pl.ds(128, 128)
    x_cols, y_cols = pl.ds(0, XCOLS), pl.ds(XCOLS, 4096 - XCOLS)
    own_x, own_y, far_x, far_y = (own, x_cols), (own, y_cols), (far, x_cols), (far, y_cols)
    sy_up = send(S.at[0, *own_y], S.at[3, *own_y], dy=UP)
    sy_dn = send(S.at[0, *own_y], S.at[1, *own_y], dy=DOWN)
    sxy = [send(S.at[0, *own_y], S.at[0, *far_y], dxl=1)]

    l_tin.wait()

    def clip_t(i, amax):
        rows = pl.ds(pl.multiple_of(32 * i, 32), 32)
        v = T[rows, pl.ds(0, 512)].astype(F32)
        T[rows, pl.ds(0, 512)] = jnp.clip(v, -lim_in, lim_in).astype(BF16)
        return jnp.maximum(amax, fold(jnp.maximum, jnp.abs(v)))

    amax_in = lax.fori_loop(0, 32, clip_t, jnp.zeros((8, 128), F32))
    low, high = pl.ds(0, 512), pl.ds(512, 512)

    def tblock(r, rows):
        return T.at[rows, pl.ds(512 * r, 512)]

    t_up = send(tblock(0, low), tblock(3, low), "t", dy=UP)
    t_dn = send(tblock(0, high), tblock(1, high), "t", dy=DOWN)
    t_up1 = send(tblock(0, high), tblock(3, high), "t", dy=UP)
    t_dn1 = send(tblock(0, low), tblock(1, low), "t", dy=DOWN)

    def wslab(dz=0, dxh=None):
        at = pl.multiple_of(64 * (2 * ((z + dz) % 4) + k), 64)
        if dxh is None:
            return W.at[pl.ds(1, 3), pl.ds(at, 64)]
        return W.at[pl.ds(1, 3), pl.ds(pl.multiple_of(at + 32 * ((xh + dxh) % 2), 32), 32)]

    await_group(w_y)
    w_x = send(wslab(0, 0), wslab(0, 0), "w", dxh=1)
    w_up = send(wslab(0, 0), wslab(0, 0), "w", dz=UP)
    w_dn = send(wslab(0, 0), wslab(0, 0), "w", dz=DOWN)
    sx = send(S.at[0, *own_x], S.at[0, *far_x], dxl=1)

    l_wown.wait()

    @pl.loop(0, 32)
    def _(i):
        rows = pl.ds(pl.multiple_of(16 * i, 16), 16)
        v = W[0, rows, :].astype(F32)
        W[0, rows, :] = jnp.clip(v, -lim_w, lim_w).astype(BF16)

    sy_up.wait_recv()
    sxy.append(send(S.at[3, *own_y], S.at[3, *far_y], dxl=1))
    sy_dn.wait_recv()
    sxy.append(send(S.at[1, *own_y], S.at[1, *far_y], dxl=1))
    w_x.wait_recv()
    v_dn = send(wslab(0, 1), wslab(0, 1), "w", dz=DOWN)
    v_up = send(wslab(0, 1), wslab(0, 1), "w", dz=UP)
    w_sib = [send(wslab(), wslab(), "w", dk=1)]

    upper, lower = (pl.ds(0, 64), y_cols), (pl.ds(64, 64), y_cols)
    t_up.wait_recv()
    t_up2 = send(tblock(3, low), tblock(2, low), "t", dy=UP)
    t_dn.wait_recv()
    t_dn2 = send(tblock(1, high), tblock(2, high), "t", dy=DOWN)
    sy_up2 = send(S.at[3, *upper], S.at[2, *upper], dy=UP)
    sy_dn2 = send(S.at[1, *lower], S.at[2, *lower], dy=DOWN)
    a_up = send(S.at[0, *own_x], S.at[3, *own_x], dy=UP)

    w_up.wait_recv()
    w_up2 = send(wslab(DOWN, 0), wslab(DOWN, 0), "w", dz=UP)
    v_dn.wait_recv()
    v_dn2 = send(wslab(UP, 1), wslab(UP, 1), "w", dz=DOWN)
    v_up.wait_recv()
    w_sib.append(send(wslab(DOWN), wslab(DOWN), "w", dk=1))
    w_dn.wait_recv()
    w_sib.append(send(wslab(UP), wslab(UP), "w", dk=1))

    sx.wait_recv()
    b_dn = send(S.at[0, *far_x], S.at[1, *far_x], dy=DOWN)
    b_up = send(S.at[0, *far_x], S.at[3, *far_x], dy=UP)
    a_dn = send(S.at[0, *own_x], S.at[1, *own_x], dy=DOWN)

    w_up2.wait_recv()
    v_dn2.wait_recv()
    w_sib.append(send(wslab(2), wslab(2), "w", dk=1))
    p_x.wait_recv()
    p_sib.append(send(pblock(1), pblock(1), dk=1))
    q_dn = send(pblock(1), pblock(1), dz=DOWN)
    q_up = send(pblock(1), pblock(1), dz=UP)
    p_up.wait_recv()
    p_up2 = send(pblock(0, DOWN), pblock(0, DOWN), dz=UP)
    p_sib.append(send(pblock(0, DOWN), pblock(0, DOWN), dk=1))
    p_dn.wait_recv()
    p_sib.append(send(pblock(0, UP), pblock(0, UP), dk=1))

    for copy in t_up1, t_dn1, t_up2, t_dn2, *w_sib:
        copy.wait_recv()

    def product(rows, col0, n):
        cols = pl.ds(pl.multiple_of(col0 + 256 * n, 256), 256)
        w = W[:, :, cols].reshape(2048, 256)
        return jnp.dot(T[rows, :], w, preferred_element_type=F32)

    rs_t = []
    for q in range(4):
        rows = pl.ds(256 * q, 256)

        @pl.loop(0, 4)
        def _(n):
            cols = pl.ds(pl.multiple_of(256 * n, 256), 256)
            psend[rows, cols] = product(rows, 1024 * (1 - xl), n).astype(BF16)

        for rows in (rows,) if q < 3 else (pl.ds(768, 128), pl.ds(896, 128)):
            rs_t.append(send(psend.at[rows], precv.at[rows], "r", dxl=1))


    sy_up2.wait_recv()
    sy_dn2.wait_recv()
    sxy.append(send(S.at[2, *own_y], S.at[2, *far_y], dxl=1))
    l_res.wait()
    for q in range(4):
        rows = pl.ds(256 * q, 256)

        @pl.loop(0, 4)
        def _(n):
            cols = pl.ds(pl.multiple_of(256 * n, 256), 256)
            H[rows, cols] = product(rows, 1024 * xl, n) + R[rows, cols].astype(F32)

    q_dn.wait_recv()
    q_dn2 = send(pblock(1, UP), pblock(1, UP), dz=DOWN)
    p_sib.append(send(pblock(1, UP), pblock(1, UP), dk=1))
    q_up.wait_recv()
    p_sib.append(send(pblock(1, DOWN), pblock(1, DOWN), dk=1))
    p_up2.wait_recv()
    p_sib.append(send(pblock(0, 2), pblock(0, 2), dk=1))
    first, second, last = [pl.ds(*piece) for piece in PIECES]
    a_up.wait_recv()
    a_up2, a_up3 = [send(S.at[3, own, n], S.at[2, own, n], dy=UP) for n in (first, second)]
    b_dn.wait_recv()
    b_dn2, b_dn3 = [send(S.at[1, far, n], S.at[2, far, n], dy=DOWN) for n in (first, second)]
    q_dn2.wait_recv()
    p_sib.append(send(pblock(1, 2), pblock(1, 2), dk=1))

    def mapped(r):
        @pl.loop(0, 2)
        def _(n):
            cols = pl.ds(pl.multiple_of(512 * n, 512), 512)
            M[pl.ds(256 * r, 256), cols] = jnp.dot(
                S[r], PR[:, cols], preferred_element_type=F32
            )

    def mapped_part(inner, add_up):
        @pl.loop(0, 2)
        def _(n):
            cols = pl.ds(pl.multiple_of(512 * n, 512), 512)
            out = jnp.dot(S[2, :, inner], PR[inner, cols], preferred_element_type=F32)
            M[pl.ds(512, 256), cols] = M[pl.ds(512, 256), cols] + out if add_up else out

    ORDER = [(1, 2), (0, 2), (1, 1), (1, 3), (1, 0), (0, 1), (0, 3), (0, 0)]

    def turned(g):
        if g < 4:
            return T, 512 * (g % 2), 1024 * (g // 2)
        return (R, psend)[g // 2 - 2], 512 * (g % 2), 0

    def turn(g, r):
        dxh, dz = ORDER[g]
        chip = ((xh + dxh) % 2) * 4 + (z + dz) % 4
        ref, row0, col0 = turned(g)
        for own in (0, 1):
            cols = pl.ds(pl.multiple_of(512 * chip + 256 * ((k + 1 - own) % 2), 256), 256)
            ref[pl.ds(row0 + 256 * own, 256), pl.ds(col0 + 256 * r, 256)] = S[r, :, cols].T

    def turn_first(r):
        for g in range(4):
            turn(g, r)

    l_tgain.wait()
    gains = tgain[...]

    def squares(q):
        rs_t[q].wait_recv()
        first, count = (256 * q, 256) if q < 3 else (128 * q + 384, 128)

        @pl.loop(0, count // 16)
        def _(i):
            rows = pl.ds(pl.multiple_of(first + 16 * i, 16), 16)
            h = H[rows, :] + precv[rows, :].astype(F32)
            H[rows, :] = h * gains
            col[rows, :] = jnp.broadcast_to(jnp.sum(h * h, axis=1, keepdims=True), (16, 128))

    for copy in p_sib:
        copy.wait_recv()
    sxy[0].wait_recv()
    mapped(0)
    sent("t")
    turn_first(0)
    squares(0)
    squares(1)
    squares(2)
    b_up.wait_recv()
    sxy[1].wait_recv()
    mapped(3)
    turn_first(3)
    a_dn.wait_recv()
    sxy[2].wait_recv()
    mapped(1)
    squares(3)
    a_up2.wait_recv()
    b_dn2.wait_recv()
    mapped_part(first, False)
    squares(4)
    row = lax.broadcasted_iota(jnp.int32, (8, 128), 0)
    packed = jnp.zeros((8, 128), F32)
    for i in range(8):
        packed = jnp.where(row == i, col[pl.ds(128 * i, 128), :].T[0:8, :], packed)
    sq[0] = packed
    sq_c = send_all(
        [(sq.at[0], sq.at[dy * 2 + dx], {"dy": dy, "dxl": dx}) for dy, dx in TENSOR], "s"
    )
    a_up4 = send(S.at[3, own, last], S.at[2, own, last], dy=UP)
    b_dn4 = send(S.at[1, far, last], S.at[2, far, last], dy=DOWN)
    turn_first(1)

    def errors(r, acc):
        for b in range(2):
            base = 128 * (2 * ((y + r) % 4) + (xl + b) % 2)

            def step(i, acc):
                there = pl.ds(pl.multiple_of(base + 16 * i, 16), 16)
                here = pl.ds(pl.multiple_of(256 * r + 128 * b + 16 * i, 16), 16)
                scale = jnp.concatenate([col[there, :]] * 8, axis=1)
                e = M[here, :] - H[there, :] * scale
                E[here, :] = e.astype(BF16)
                return acc + fold(jnp.add, e * e)

            acc = lax.fori_loop(0, 8, step, acc, unroll=2)
        return acc

    a_up3.wait_recv()
    b_dn3.wait_recv()
    mapped_part(second, True)
    await_group(sq_c)
    total = sq[0]
    for i in range(1, 8):
        total = total + sq[i]
    inv = lax.rsqrt(total * (1.0 / 8192) + EPS)
    for i in range(8):
        col[pl.ds(128 * i, 128), :] = jnp.broadcast_to(inv[i : i + 1, :], (128, 128)).T
    acc = jnp.zeros((8, 128), F32)
    for r in (0, 3, 1):
        acc = errors(r, acc)

    @pl.loop(0, 2)
    def _(n):
        cols = pl.ds(pl.multiple_of(512 * n, 512), 512)
        M[pl.ds(0, 256), cols] = jnp.dot(
            T[pl.ds(0, 256), pl.ds(0, 512)], E[pl.ds(0, 512), cols], preferred_element_type=F32
        ) + jnp.dot(
            T[pl.ds(0, 256), pl.ds(768, 256)], E[pl.ds(768, 256), cols], preferred_element_type=F32
        )

    sxy[3].wait_recv()
    a_up4.wait_recv()
    b_dn4.wait_recv()
    mapped_part(pl.ds(PIECES[2][0], 4096 - PIECES[2][0]), True)
    acc = errors(2, acc)

    tile = jnp.where(row == 0, jnp.max(amax_in), jnp.where(row == 1, jnp.max(amax_w), jnp.sum(acc)))

    def merge(first, count):
        out = scal[first]
        for i in range(1, count):
            v = scal[first + i]
            out = jnp.where(row < 2, jnp.maximum(out, v), out + v)
        return out

    scal[t] = tile
    sc1 = send_all([(scal.at[t], scal.at[t], {"dy": dy, "dxl": dx}) for dy, dx in TENSOR], "s")

    sent("w")
    sent("r")

    a_rows, b_rows = (0, AROWS), (AROWS, 256 - AROWS)
    a_up_rows, a_dn_rows = (0, 48), (48, AROWS - 48)
    b_up_rows, b_dn_rows = (AROWS, 80), (AROWS + 80, 176 - AROWS)

    def gslot(dxh, dz, rows=(0, 256), other=0):
        g = ORDER.index((dxh, dz))
        return W.at[g // 2, pl.ds(256 * (g % 2) + rows[0], rows[1]), pl.ds(1024 * other, 1024)]

    to_sib, a_1, b_1, a_2, a_m, b_m = [], {}, {}, {}, {}, {}

    def half_term(g, own):
        dxh, dz = ORDER[g]
        ref, row0, col0 = turned(g)

        @pl.loop(0, 2)
        def _(n):
            at = pl.multiple_of(512 * n, 512)
            rows, cols = pl.ds(row0 + 256 * own, 256), pl.ds(at, 512)
            if (g, own) == (0, 0):
                one = M[rows, cols] + jnp.dot(
                    ref[rows, pl.ds(512, 256)], E[pl.ds(512, 256), cols], preferred_element_type=F32
                )
            else:
                one = jnp.dot(ref[rows, pl.ds(col0, 1024)], E[:, cols], preferred_element_type=F32)
            start = pl.multiple_of(1024 * (1 - own) + at, 512)
            W[g // 2, pl.ds(256 * (g % 2), 256), pl.ds(start, 512)] = one.astype(BF16)

        if own == 0:
            to_sib.append(send(gslot(dxh, dz, other=1), sib.at[g], dk=1))

    def term(g):
        dxh, dz = ORDER[g]
        ref, row0, col0 = turned(g)

        @pl.loop(0, 2)
        def _(n):
            at = pl.multiple_of(512 * n, 512)
            both = jnp.dot(
                ref[pl.ds(row0, 512), pl.ds(col0, 1024)],
                E[:, pl.ds(at, 512)],
                preferred_element_type=F32,
            ).astype(BF16)
            rows = pl.ds(256 * (g % 2), 256)
            W[g // 2, rows, pl.ds(pl.multiple_of(1024 + at, 512), 512)] = both[:256]
            W[g // 2, rows, pl.ds(at, 512)] = both[256:]

        to_sib.append(send(gslot(dxh, dz, other=1), sib.at[g], dk=1))

    def add(dxh, dz, rows, others):
        g = ORDER.index((dxh, dz))

        @pl.loop(0, rows[1] // 16)
        def _(i):
            here = pl.ds(pl.multiple_of(16 * i, 16), 16)
            there = pl.ds(pl.multiple_of(256 * (g % 2) + rows[0] + 16 * i, 16), 16)
            total = W[g // 2, there, pl.ds(0, 1024)].astype(F32)
            for ref, index in others:
                total = total + ref[index, here, :].astype(F32)
            W[g // 2, there, pl.ds(0, 1024)] = total.astype(BF16)

    def along_z(dxh, dz, rows, up, dn, mid, at, far, gone, passed):
        if dz == 2:
            passed[dxh, UP] = send(gslot(dxh, 2, up), mid.at[at, pl.ds(0, up[1])], dz=UP)
            passed[dxh, DOWN] = send(gslot(dxh, 2, dn), mid.at[at + 1, pl.ds(0, dn[1])], dz=DOWN)
        elif dz:
            passed[dxh, dz].wait_recv()
            add(dxh, dz, up if dz == UP else dn, [(mid, at + dz // 2)])
            gone[dxh, dz] = send(gslot(dxh, dz, rows), far.at[at + dz // 2], dz=dz)

    def finish(g):
        dxh, dz = ORDER[g]
        to_sib[g].wait_recv()
        add(dxh, dz, (0, 256), [(sib, g)])
        if dxh:
            a_1[dz] = send(gslot(dxh, dz, a_rows), ra1.at[dz], dxh=1)

    def second_b(dxh, dz):
        along_z(dxh, dz, b_rows, b_up_rows, b_dn_rows, bm, 2 * dxh, rb1, b_1, b_m)

    def second_a(dz):
        a_1[dz].wait_recv()
        add(0, dz, a_rows, [(ra1, dz)])
        along_z(0, dz, a_rows, a_up_rows, a_dn_rows, am, 0, ra2, a_2, a_m)

    def term_of(g):
        for r in range(4) if g >= 4 else (2,):
            turn(g, r)
        term(g)

    turn(0, 2)
    half_term(0, 0)
    half_term(0, 1)
    turn(1, 2)
    half_term(1, 0)
    finish(0)
    second_b(1, 2)
    half_term(1, 1)
    await_group(sc1)
    at = 8 + xh * 4 + z
    scal[at] = merge(0, 8)
    sc2 = send_all([(scal.at[at], scal.at[at], {"dxh": dx, "dz": dz}) for dx, dz in CONTEXT], "s")
    term_of(2)
    finish(1)
    second_b(0, 2)
    term_of(3)
    finish(2)
    second_b(1, 1)
    term_of(4)
    finish(3)
    second_b(1, 3)
    second_a(2)
    term_of(5)
    finish(4)
    term_of(6)
    finish(5)
    second_b(0, 1)
    term_of(7)
    finish(6)
    second_b(0, 3)
    for n in (UP, DOWN):
        b_1[1, n].wait_recv()
    add(1, 0, b_rows, [(rb1, 2), (rb1, 3)])
    b_2 = send(gslot(1, 0, b_rows), rb2.at[0], dxh=1)
    second_a(1)
    second_a(3)
    await_group(sc2)
    scal[16 + k] = merge(8, 8)
    sc3 = send(scal.at[16 + k], scal.at[16 + k], "s", dk=1)
    finish(7)
    second_a(0)
    sc3.wait_recv()
    scal[18] = merge(16, 2)
    written = [load(scal.at[18], parts.at[pl.ds(256, 8), pl.ds(0, 128)])]

    for n in (UP, DOWN):
        b_1[0, n].wait_recv()
        a_2[0, n].wait_recv()
    b_2.wait_recv()
    scale = 1.0 / math.sqrt(tokens_all)
    for (first, count), landed in (
        (b_rows, [(rb1, 0), (rb1, 1), (rb2, 0)]),
        (a_rows, [(ra2, 0), (ra2, 1)]),
    ):

        @pl.loop(0, count // 16)
        def _(i):
            here = pl.ds(pl.multiple_of(16 * i, 16), 16)
            mine = pl.ds(pl.multiple_of(256 + first + 16 * i, 16), 16)
            total = W[3, mine, pl.ds(0, 1024)].astype(F32)
            for ref, index in landed:
                total = total + ref[index, here, :].astype(F32)
            total_g[pl.ds(pl.multiple_of(first + 16 * i, 16), 16), :] = total * scale

        rows = pl.ds(first, count)
        written.append(load(total_g.at[rows], parts.at[rows]))

    assert len(groups) <= SEND_SEMS and len(received) <= RECV_SEMS
    for group in groups:
        if group not in ("t", "w", "r"):
            sent(group)
    for copy in written:
        copy.wait()


def results(
    tokens_all, parts, hist_in, hist_w, grad, loss, hist_in_new, hist_w_new,
    held, tile, s_in, s_w, s_in_new, s_w_new, s_loss, sem_in, sem_out,
):
    pieces = [pl.ds(64 * i, 64) for i in range(4)]
    copies = [
        (parts.at[pl.ds(256, 8), pl.ds(0, 128)], tile),
        (hist_in, s_in),
        (hist_w, s_w),
        *((parts.at[rows], held.at[rows]) for rows in pieces),
    ]
    copies = [pltpu.make_async_copy(a, b, sem_in.at[i]) for i, (a, b) in enumerate(copies)]
    for copy in copies:
        copy.start()
    backs = [
        *((held.at[rows], grad.at[rows]) for rows in pieces),
        (s_in_new, hist_in_new),
        (s_w_new, hist_w_new),
        (s_loss, loss),
    ]
    backs = [pltpu.make_async_copy(a, b, sem_out.at[i]) for i, (a, b) in enumerate(backs)]
    for copy in copies[:3]:
        copy.wait()
    s_in_new[0] = jnp.max(tile[0:1, :])
    s_w_new[0] = jnp.max(tile[1:2, :])
    s_loss[0] = jnp.max(tile[2:3, :]) * (0.5 / (tokens_all * 8192))
    for i in range(15):
        s_in_new[i + 1] = s_in[i]
        s_w_new[i + 1] = s_w[i]
    for back in backs[4:]:
        back.start()
    for copy, back in zip(copies[3:], backs):
        copy.wait()
        back.start()
    for back in backs:
        back.wait()


def local(
    teacher_in, teacher_resid, teacher_wo, teacher_gain, input_history, weight_history,
    student_hidden, student_gain, projection,
):
    tokens_all = teacher_in.shape[0] * lax.axis_size("context")
    hbm = pl.BlockSpec(memory_space=pl.ANY)
    parts = pl.pallas_call(
        functools.partial(kernel, tokens_all),
        name="distill",
        out_shape=jax.ShapeDtypeStruct((264, 1024), F32),
        in_specs=[hbm] * 9,
        out_specs=hbm,
        scratch_shapes=[
            pltpu.VMEM((1024, 2048), BF16),
            pltpu.VMEM((4, 512, 2048), BF16),
            pltpu.VMEM((4, 256, 4096), BF16),
            pltpu.VMEM((4096, 1024), BF16),
            pltpu.VMEM((1024, 1024), BF16),
            pltpu.VMEM((1024, 1024), F32),
            pltpu.VMEM((1024, 1024), F32),
            pltpu.VMEM((1024, 1024), BF16),
            pltpu.VMEM((1024, 1024), BF16),
            pltpu.VMEM((1024, 1024), BF16),
            pltpu.VMEM((128, 4096), BF16),
            pltpu.VMEM((32, 8192), BF16),
            pltpu.VMEM((1024, 128), F32),
            pltpu.VMEM((8, 8, 128), F32),
            pltpu.VMEM((19, 8, 128), F32),
            pltpu.VMEM((8, 256, 1024), BF16),
            pltpu.VMEM((4, AROWS, 1024), BF16),
            pltpu.VMEM((2, AROWS, 1024), BF16),
            pltpu.VMEM((4, 256 - AROWS, 1024), BF16),
            pltpu.VMEM((1, 256 - AROWS, 1024), BF16),
            pltpu.VMEM((2, 64, 1024), BF16),
            pltpu.VMEM((4, 80, 1024), BF16),
            pltpu.VMEM((256, 1024), F32),
            pltpu.VMEM((1, 4096), F32),
            pltpu.VMEM((1, 1024), F32),
            pltpu.SMEM((16,), F32),
            pltpu.SMEM((16,), F32),
            pltpu.SemaphoreType.DMA((SEND_SEMS,)),
            pltpu.SemaphoreType.DMA((RECV_SEMS,)),
            pltpu.SemaphoreType.DMA((13,)),
        ],
        compiler_params=pltpu.CompilerParams(
            collective_id=0, has_side_effects=True, vmem_limit_bytes=62 << 20
        ),
        cost_estimate=pl.CostEstimate(
            flops=3 * 2 * 1024 * 1024 * 4096, bytes_accessed=16 << 20, transcendentals=1024
        ),
    )(
        input_history,
        weight_history,
        student_gain.reshape(1, -1),
        teacher_gain.reshape(1, -1),
        teacher_in,
        teacher_resid,
        teacher_wo,
        student_hidden,
        projection,
    )
    grad, loss, hist_in, hist_w = pl.pallas_call(
        functools.partial(results, tokens_all),
        name="results",
        out_shape=(
            jax.ShapeDtypeStruct((256, 1024), F32),
            jax.ShapeDtypeStruct((1,), F32),
            jax.ShapeDtypeStruct((16,), F32),
            jax.ShapeDtypeStruct((16,), F32),
        ),
        in_specs=[hbm] * 3,
        out_specs=(hbm,) * 4,
        scratch_shapes=[
            pltpu.VMEM((256, 1024), F32),
            pltpu.VMEM((8, 128), F32),
            *(pltpu.SMEM((n,), F32) for n in (16, 16, 16, 16, 1)),
            pltpu.SemaphoreType.DMA((7,)),
            pltpu.SemaphoreType.DMA((7,)),
        ],
    )(parts, input_history, weight_history)
    return grad, loss.reshape(()), hist_in, hist_w


def solution(mesh):
    placed = (
        P("context", "tensor"),
        P("context", "tensor"),
        P("tensor", None),
        P(),
        P(),
        P(),
        P(("context", "tensor"), None),
        P(),
        P("context", "tensor"),
    )
    return jax.shard_map(
        local,
        mesh=mesh,
        in_specs=placed,
        out_specs=(P("context", "tensor"), P(), P(), P()),
        check_vma=False,
    )
```

```python
import functools
import math

import jax
import jax.numpy as jnp
from jax import lax
from jax.experimental import pallas as pl
from jax.experimental.pallas import tpu as pltpu
from jax.sharding import PartitionSpec as P

MESH = pl.DeviceIdType.MESH
F32, BF16 = jnp.float32, jnp.bfloat16
EPS = 1e-05
SEND_SEMS, RECV_SEMS = 7, 73
GROUP = 8 << 20
XCOLS = 3456
PIECES = (0, 1408), (1408, 1408), (2816, 640)
AROWS = 112


def lanes(tile):
    rows, width = tile.shape
    return [
        tile[r : r + 8, c : c + 128]
        for r in range(0, rows, 8)
        for c in range(0, width, 128)
    ]


def fold(op, tile):
    parts = lanes(tile)
    while len(parts) > 1:
        parts = [op(a, b) for a, b in zip(parts[::2], parts[1::2])] + (
            [parts[-1]] if len(parts) % 2 else []
        )
    return parts[0]


def kernel(
    tokens_all,
    hist_in_all, hist_w_all, stu_gain, tea_gain, tin, resid, wo, stu, proj,
    parts, ra2, rb2,
    T, W, S, PR, R, H, M, E, psend, precv, sraw, wraw, col, sq, scal, sib, ra1, rb1, am, bm, total_g, sgain, tgain, hist_in, hist_w,
    ssem, rsem, lsem,
):
    t, c = lax.axis_index("tensor"), lax.axis_index("context")
    y, xl = t // 2, t % 2
    xh, z, k = c // 8, (c // 2) % 4, c % 2

    def dev(dy=0, dxl=0, dxh=0, dz=0, dk=0):
        ny, nz = (y + dy) % 4, (z + dz) % 4
        nxl, nxh, nk = (xl + dxl) % 2, (xh + dxh) % 2, (k + dk) % 2
        return {"tensor": ny * 2 + nxl, "context": nxh * 8 + nz * 2 + nk}

    received, groups = [], {}

    def remote(src, dst, send_sem, recv_sem, to):
        return pltpu.make_async_remote_copy(
            src_ref=src,
            dst_ref=dst,
            send_sem=ssem.at[send_sem],
            recv_sem=rsem.at[recv_sem],
            device_id=to,
            device_id_type=MESH,
        )

    def size(ref):
        return math.prod(ref.shape) * jnp.dtype(ref.dtype).itemsize

    landing = {}

    def send(src, dst, group=None, land=None, **to):
        if group is None:
            group = next((n for n in range(50) if groups.get(n, (0, 0))[1] + size(src) <= GROUP), 0)
        index, held = groups.get(group, (len(groups), 0))
        groups[group] = index, held + size(src)
        if land is None or land not in landing:
            received.append(len(received))
        at, total = landing.get(land, (received[-1], 0))
        if land is not None:
            landing[land] = at, total + size(src)
        copy = remote(src, dst, index, at, dev(**to))
        copy.start()
        return copy

    def span(count):
        if count % 32768 == 0:
            return PR.at[pl.ds(0, count // 2048)]
        return col.at[pl.ds(0, count // 512)]

    def sent(group):
        index, held = groups[group]
        rows = span(held)
        remote(rows, rows, index, 0, dev(dk=1)).wait_send()

    def send_all(pieces, group=None):
        received.append(len(received))
        at, total = received[-1], 0
        for src, dst, to in pieces:
            key = group
            if key is None:
                key = next(n for n in range(50) if groups.get(n, (0, 0))[1] + size(src) <= GROUP)
            index, held = groups.get(key, (len(groups), 0))
            groups[key] = index, held + size(src)
            remote(src, dst, index, at, dev(**to)).start()
            total += size(src)
        return at, total

    def await_group(landed):
        at, total = landed
        rows = span(total)
        remote(rows, rows, 0, at, dev(dk=1)).wait_recv()

    local = []

    def load(src, dst):
        copy = pltpu.make_async_copy(src, dst, lsem.at[len(local)])
        copy.start()
        local.append(copy)
        return copy

    TENSOR = [(dy, dx) for dy in range(4) for dx in range(2) if (dy, dx) != (0, 0)]
    CONTEXT = [(dx, dz) for dx in range(2) for dz in range(4) if (dx, dz) != (0, 0)]
    UP, DOWN = 1, 3

    slab = pl.multiple_of(64 * (2 * z + k) + 32 * xh, 32)
    l_wraw = load(wo.at[pl.ds(slab, 32)], wraw)
    l_hist = load(hist_in_all, hist_in), load(hist_w_all, hist_w)
    l_sgain = load(stu_gain, sgain)
    l_tgain = load(tea_gain.at[:, pl.ds(pl.multiple_of(1024 * t, 1024), 1024)], tgain)
    l_proj = load(proj, PR.at[pl.ds(pl.multiple_of(256 * c, 256), 256)])
    l_stu = load(stu, sraw)
    l_tin = load(tin, T.at[:, pl.ds(0, 512)])
    l_wown = load(wo.at[:, pl.ds(pl.multiple_of(2048 * y, 2048), 2048)], W.at[0])
    l_res = load(resid, R)

    barrier = pltpu.get_barrier_semaphore()
    for dy, dx in TENSOR:
        pl.semaphore_signal(barrier, 1, device_id=dev(dy=dy, dxl=dx), device_id_type=MESH)
    for dx, dz in CONTEXT:
        pl.semaphore_signal(barrier, 1, device_id=dev(dxh=dx, dz=dz), device_id_type=MESH)
    pl.semaphore_signal(barrier, 1, device_id=dev(dk=1), device_id_type=MESH)

    for copy in l_hist:
        copy.wait()
    lim_in, lim_w = hist_in[0], hist_w[0]
    for i in range(1, 16):
        lim_in = jnp.maximum(lim_in, hist_in[i])
        lim_w = jnp.maximum(lim_w, hist_w[i])

    l_wraw.wait()

    def clip_w(i, amax):
        rows = pl.ds(pl.multiple_of(16 * i, 16), 16)
        for n in range(8):
            cols = pl.ds(1024 * n, 1024)
            v = wraw[rows, cols].astype(F32)
            amax = jnp.maximum(amax, fold(jnp.maximum, jnp.abs(v)))
            wraw[rows, cols] = jnp.clip(v, -lim_w, lim_w).astype(BF16)
        return amax

    amax_w = lax.fori_loop(0, 2, clip_w, jnp.zeros((8, 128), F32))

    pl.semaphore_wait(barrier, len(TENSOR) + len(CONTEXT) + 1)

    def wcols(d):
        return pl.ds(pl.multiple_of(2048 * ((y + d) % 4), 2048), 2048)

    w_y = send_all(
        [(wraw.at[:, wcols(d)], W.at[4 - d, pl.ds(slab, 32)], {"dy": d}) for d in (2, 1, 3)]
    )
    l_proj.wait()

    def pblock(dxh=0, dz=0):
        at = ((xh + dxh) % 2) * 8 + ((z + dz) % 4) * 2 + k
        return PR.at[pl.ds(pl.multiple_of(256 * at, 256), 256)]

    p_x = send(pblock(), pblock(), dxh=1)
    p_up = send(pblock(), pblock(), dz=UP)
    p_dn = send(pblock(), pblock(), dz=DOWN)
    p_sib = [send(pblock(), pblock(), land="p", dk=1)]

    l_stu.wait()
    l_sgain.wait()

    @pl.loop(0, 8)
    def _(i):
        rows = pl.ds(pl.multiple_of(16 * i, 16), 16)
        v = sraw[rows, :].astype(F32)
        mean = jnp.mean(v * v, axis=1, keepdims=True)
        S[0, rows, :] = (v * lax.rsqrt(mean + EPS) * sgain[...]).astype(BF16)

    own, far = pl.ds(0, 128), pl.ds(128, 128)
    x_cols, y_cols = pl.ds(0, XCOLS), pl.ds(XCOLS, 4096 - XCOLS)
    own_x, own_y, far_x, far_y = (own, x_cols), (own, y_cols), (far, x_cols), (far, y_cols)
    sy_up = send(S.at[0, *own_y], S.at[3, *own_y], dy=UP)
    sy_dn = send(S.at[0, *own_y], S.at[1, *own_y], dy=DOWN)
    sxy = [send(S.at[0, *own_y], S.at[0, *far_y], dxl=1)]

    l_tin.wait()

    def clip_t(i, amax):
        rows = pl.ds(pl.multiple_of(32 * i, 32), 32)
        v = T[rows, pl.ds(0, 512)].astype(F32)
        T[rows, pl.ds(0, 512)] = jnp.clip(v, -lim_in, lim_in).astype(BF16)
        return jnp.maximum(amax, fold(jnp.maximum, jnp.abs(v)))

    amax_in = lax.fori_loop(0, 32, clip_t, jnp.zeros((8, 128), F32))
    low, high = pl.ds(0, 512), pl.ds(512, 512)

    def tblock(r, rows):
        return T.at[rows, pl.ds(512 * r, 512)]

    t_up = send(tblock(0, low), tblock(3, low), "t", dy=UP)
    t_dn = send(tblock(0, high), tblock(1, high), "t", dy=DOWN)
    t_up1 = send(tblock(0, high), tblock(3, high), "t", "t", dy=UP)
    t_dn1 = send(tblock(0, low), tblock(1, low), "t", "t", dy=DOWN)

    def wslab(dz=0, dxh=None):
        at = pl.multiple_of(64 * (2 * ((z + dz) % 4) + k), 64)
        if dxh is None:
            return W.at[pl.ds(1, 3), pl.ds(at, 64)]
        return W.at[pl.ds(1, 3), pl.ds(pl.multiple_of(at + 32 * ((xh + dxh) % 2), 32), 32)]

    await_group(w_y)
    w_x = send(wslab(0, 0), wslab(0, 0), "w", dxh=1)
    w_up = send(wslab(0, 0), wslab(0, 0), "w", dz=UP)
    w_dn = send(wslab(0, 0), wslab(0, 0), "w", dz=DOWN)
    sx = send(S.at[0, *own_x], S.at[0, *far_x], dxl=1)

    l_wown.wait()

    @pl.loop(0, 32)
    def _(i):
        rows = pl.ds(pl.multiple_of(16 * i, 16), 16)
        v = W[0, rows, :].astype(F32)
        W[0, rows, :] = jnp.clip(v, -lim_w, lim_w).astype(BF16)

    sy_up.wait_recv()
    sxy.append(send(S.at[3, *own_y], S.at[3, *far_y], dxl=1))
    sy_dn.wait_recv()
    sxy.append(send(S.at[1, *own_y], S.at[1, *far_y], dxl=1))
    w_x.wait_recv()
    v_dn = send(wslab(0, 1), wslab(0, 1), "w", dz=DOWN)
    v_up = send(wslab(0, 1), wslab(0, 1), "w", dz=UP)
    w_sib = [send(wslab(), wslab(), "w", "w", dk=1)]

    upper, lower = (pl.ds(0, 64), y_cols), (pl.ds(64, 64), y_cols)
    t_up.wait_recv()
    t_up2 = send(tblock(3, low), tblock(2, low), "t", "t", dy=UP)
    t_dn.wait_recv()
    t_dn2 = send(tblock(1, high), tblock(2, high), "t", "t", dy=DOWN)
    sy_up2 = send(S.at[3, *upper], S.at[2, *upper], dy=UP)
    sy_dn2 = send(S.at[1, *lower], S.at[2, *lower], dy=DOWN)
    a_up = send(S.at[0, *own_x], S.at[3, *own_x], dy=UP)

    w_up.wait_recv()
    w_up2 = send(wslab(DOWN, 0), wslab(DOWN, 0), "w", dz=UP)
    v_dn.wait_recv()
    v_dn2 = send(wslab(UP, 1), wslab(UP, 1), "w", dz=DOWN)
    v_up.wait_recv()
    w_sib.append(send(wslab(DOWN), wslab(DOWN), "w", "w", dk=1))
    w_dn.wait_recv()
    w_sib.append(send(wslab(UP), wslab(UP), "w", "w", dk=1))

    sx.wait_recv()
    b_dn = send(S.at[0, *far_x], S.at[1, *far_x], dy=DOWN)
    b_up = send(S.at[0, *far_x], S.at[3, *far_x], dy=UP)
    a_dn = send(S.at[0, *own_x], S.at[1, *own_x], dy=DOWN)

    w_up2.wait_recv()
    v_dn2.wait_recv()
    w_sib.append(send(wslab(2), wslab(2), "w", "w", dk=1))
    p_x.wait_recv()
    p_sib.append(send(pblock(1), pblock(1), land="p", dk=1))
    q_dn = send(pblock(1), pblock(1), dz=DOWN)
    q_up = send(pblock(1), pblock(1), dz=UP)
    p_up.wait_recv()
    p_up2 = send(pblock(0, DOWN), pblock(0, DOWN), dz=UP)
    p_sib.append(send(pblock(0, DOWN), pblock(0, DOWN), land="p", dk=1))
    p_dn.wait_recv()
    p_sib.append(send(pblock(0, UP), pblock(0, UP), land="p", dk=1))

    await_group(landing["t"])
    await_group(landing["w"])

    def product(rows, col0, n):
        cols = pl.ds(pl.multiple_of(col0 + 256 * n, 256), 256)
        w = W[:, :, cols].reshape(2048, 256)
        return jnp.dot(T[rows, :], w, preferred_element_type=F32)

    rs_t = []
    for q in range(4):
        rows = pl.ds(256 * q, 256)

        @pl.loop(0, 4)
        def _(n):
            cols = pl.ds(pl.multiple_of(256 * n, 256), 256)
            psend[rows, cols] = product(rows, 1024 * (1 - xl), n).astype(BF16)

        for rows in (rows,) if q < 3 else (pl.ds(768, 128), pl.ds(896, 128)):
            rs_t.append(send(psend.at[rows], precv.at[rows], "r", dxl=1))


    sy_up2.wait_recv()
    sy_dn2.wait_recv()
    sxy.append(send(S.at[2, *own_y], S.at[2, *far_y], dxl=1))
    l_res.wait()
    for q in range(4):
        rows = pl.ds(256 * q, 256)

        @pl.loop(0, 4)
        def _(n):
            cols = pl.ds(pl.multiple_of(256 * n, 256), 256)
            H[rows, cols] = product(rows, 1024 * xl, n) + R[rows, cols].astype(F32)

    q_dn.wait_recv()
    q_dn2 = send(pblock(1, UP), pblock(1, UP), dz=DOWN)
    p_sib.append(send(pblock(1, UP), pblock(1, UP), land="p", dk=1))
    q_up.wait_recv()
    p_sib.append(send(pblock(1, DOWN), pblock(1, DOWN), land="p", dk=1))
    p_up2.wait_recv()
    p_sib.append(send(pblock(0, 2), pblock(0, 2), land="p", dk=1))
    first, second, last = [pl.ds(*piece) for piece in PIECES]
    a_up.wait_recv()
    a_up2, a_up3 = [send(S.at[3, own, n], S.at[2, own, n], dy=UP) for n in (first, second)]
    b_dn.wait_recv()
    b_dn2, b_dn3 = [send(S.at[1, far, n], S.at[2, far, n], dy=DOWN) for n in (first, second)]
    q_dn2.wait_recv()
    p_sib.append(send(pblock(1, 2), pblock(1, 2), land="p", dk=1))

    def mapped(r):
        @pl.loop(0, 2)
        def _(n):
            cols = pl.ds(pl.multiple_of(512 * n, 512), 512)
            M[pl.ds(256 * r, 256), cols] = jnp.dot(
                S[r], PR[:, cols], preferred_element_type=F32
            )

    def mapped_part(inner, add_up):
        @pl.loop(0, 2)
        def _(n):
            cols = pl.ds(pl.multiple_of(512 * n, 512), 512)
            out = jnp.dot(S[2, :, inner], PR[inner, cols], preferred_element_type=F32)
            M[pl.ds(512, 256), cols] = M[pl.ds(512, 256), cols] + out if add_up else out

    ORDER = [(1, 2), (0, 2), (1, 1), (1, 3), (1, 0), (0, 1), (0, 3), (0, 0)]

    def turned(g):
        if g < 4:
            return T, 512 * (g % 2), 1024 * (g // 2)
        return (R, psend)[g // 2 - 2], 512 * (g % 2), 0

    def turn(g, r):
        dxh, dz = ORDER[g]
        chip = ((xh + dxh) % 2) * 4 + (z + dz) % 4
        ref, row0, col0 = turned(g)
        for own in (0, 1):
            cols = pl.ds(pl.multiple_of(512 * chip + 256 * ((k + 1 - own) % 2), 256), 256)
            ref[pl.ds(row0 + 256 * own, 256), pl.ds(col0 + 256 * r, 256)] = S[r, :, cols].T

    def turn_first(r):
        for g in range(4):
            turn(g, r)

    l_tgain.wait()
    gains = tgain[...]

    def squares(q):
        rs_t[q].wait_recv()
        first, count = (256 * q, 256) if q < 3 else (128 * q + 384, 128)

        @pl.loop(0, count // 16)
        def _(i):
            rows = pl.ds(pl.multiple_of(first + 16 * i, 16), 16)
            h = H[rows, :] + precv[rows, :].astype(F32)
            H[rows, :] = h * gains
            col[rows, :] = jnp.broadcast_to(jnp.sum(h * h, axis=1, keepdims=True), (16, 128))

    await_group(landing["p"])
    sxy[0].wait_recv()
    mapped(0)
    sent("t")
    turn_first(0)
    squares(0)
    squares(1)
    squares(2)
    b_up.wait_recv()
    sxy[1].wait_recv()
    mapped(3)
    turn_first(3)
    a_dn.wait_recv()
    sxy[2].wait_recv()
    mapped(1)
    squares(3)
    a_up2.wait_recv()
    b_dn2.wait_recv()
    mapped_part(first, False)
    squares(4)
    row = lax.broadcasted_iota(jnp.int32, (8, 128), 0)
    packed = jnp.zeros((8, 128), F32)
    for i in range(8):
        packed = jnp.where(row == i, col[pl.ds(128 * i, 128), :].T[0:8, :], packed)
    sq[0] = packed
    sq_c = send_all(
        [(sq.at[0], sq.at[dy * 2 + dx], {"dy": dy, "dxl": dx}) for dy, dx in TENSOR], "s"
    )
    a_up4 = send(S.at[3, own, last], S.at[2, own, last], dy=UP)
    b_dn4 = send(S.at[1, far, last], S.at[2, far, last], dy=DOWN)
    turn_first(1)

    def errors(r, acc):
        for b in range(2):
            base = 128 * (2 * ((y + r) % 4) + (xl + b) % 2)

            def step(i, acc):
                there = pl.ds(pl.multiple_of(base + 16 * i, 16), 16)
                here = pl.ds(pl.multiple_of(256 * r + 128 * b + 16 * i, 16), 16)
                scale = jnp.concatenate([col[there, :]] * 8, axis=1)
                e = M[here, :] - H[there, :] * scale
                E[here, :] = e.astype(BF16)
                return acc + fold(jnp.add, e * e)

            acc = lax.fori_loop(0, 8, step, acc, unroll=2)
        return acc

    a_up3.wait_recv()
    b_dn3.wait_recv()
    mapped_part(second, True)
    sxy[3].wait_recv()
    mapped_part(y_cols, True)
    await_group(sq_c)
    total = sq[0]
    for i in range(1, 8):
        total = total + sq[i]
    inv = lax.rsqrt(total * (1.0 / 8192) + EPS)
    for i in range(8):
        col[pl.ds(128 * i, 128), :] = jnp.broadcast_to(inv[i : i + 1, :], (128, 128)).T
    acc = jnp.zeros((8, 128), F32)
    for r in (0, 3, 1):
        acc = errors(r, acc)

    @pl.loop(0, 2)
    def _(n):
        cols = pl.ds(pl.multiple_of(512 * n, 512), 512)
        M[pl.ds(0, 256), cols] = jnp.dot(
            T[pl.ds(0, 256), pl.ds(0, 512)], E[pl.ds(0, 512), cols], preferred_element_type=F32
        ) + jnp.dot(
            T[pl.ds(0, 256), pl.ds(768, 256)], E[pl.ds(768, 256), cols], preferred_element_type=F32
        )

    a_up4.wait_recv()
    b_dn4.wait_recv()
    mapped_part(last, True)
    acc = errors(2, acc)

    tile = jnp.where(row == 0, jnp.max(amax_in), jnp.where(row == 1, jnp.max(amax_w), jnp.sum(acc)))

    def merge(first, count):
        out = scal[first]
        for i in range(1, count):
            v = scal[first + i]
            out = jnp.where(row < 2, jnp.maximum(out, v), out + v)
        return out

    scal[t] = tile
    sc1 = send_all([(scal.at[t], scal.at[t], {"dy": dy, "dxl": dx}) for dy, dx in TENSOR], "s")

    sent("w")
    sent("r")

    a_rows, b_rows = (0, AROWS), (AROWS, 256 - AROWS)
    a_up_rows, a_dn_rows = (0, 48), (48, AROWS - 48)
    b_up_rows, b_dn_rows = (AROWS, 80), (AROWS + 80, 176 - AROWS)

    def gslot(dxh, dz, rows=(0, 256), other=0):
        g = ORDER.index((dxh, dz))
        return W.at[g // 2, pl.ds(256 * (g % 2) + rows[0], rows[1]), pl.ds(1024 * other, 1024)]

    to_sib, a_1, b_1, a_2, a_m, b_m = [], {}, {}, {}, {}, {}

    def half_term(g, own):
        dxh, dz = ORDER[g]
        ref, row0, col0 = turned(g)

        @pl.loop(0, 2)
        def _(n):
            at = pl.multiple_of(512 * n, 512)
            rows, cols = pl.ds(row0 + 256 * own, 256), pl.ds(at, 512)
            if (g, own) == (0, 0):
                one = M[rows, cols] + jnp.dot(
                    ref[rows, pl.ds(512, 256)], E[pl.ds(512, 256), cols], preferred_element_type=F32
                )
            else:
                one = jnp.dot(ref[rows, pl.ds(col0, 1024)], E[:, cols], preferred_element_type=F32)
            start = pl.multiple_of(1024 * (1 - own) + at, 512)
            W[g // 2, pl.ds(256 * (g % 2), 256), pl.ds(start, 512)] = one.astype(BF16)

        if own == 0:
            to_sib.append(send(gslot(dxh, dz, other=1), sib.at[g], dk=1))

    def term(g):
        dxh, dz = ORDER[g]
        ref, row0, col0 = turned(g)

        @pl.loop(0, 2)
        def _(n):
            at = pl.multiple_of(512 * n, 512)
            both = jnp.dot(
                ref[pl.ds(row0, 512), pl.ds(col0, 1024)],
                E[:, pl.ds(at, 512)],
                preferred_element_type=F32,
            ).astype(BF16)
            rows = pl.ds(256 * (g % 2), 256)
            W[g // 2, rows, pl.ds(pl.multiple_of(1024 + at, 512), 512)] = both[:256]
            W[g // 2, rows, pl.ds(at, 512)] = both[256:]

        to_sib.append(send(gslot(dxh, dz, other=1), sib.at[g], dk=1))

    def add(dxh, dz, rows, others):
        g = ORDER.index((dxh, dz))

        @pl.loop(0, rows[1] // 16)
        def _(i):
            here = pl.ds(pl.multiple_of(16 * i, 16), 16)
            there = pl.ds(pl.multiple_of(256 * (g % 2) + rows[0] + 16 * i, 16), 16)
            total = W[g // 2, there, pl.ds(0, 1024)].astype(F32)
            for ref, index in others:
                total = total + ref[index, here, :].astype(F32)
            W[g // 2, there, pl.ds(0, 1024)] = total.astype(BF16)

    def along_z(dxh, dz, rows, up, dn, mid, at, far, gone, passed):
        if dz == 2:
            passed[dxh, UP] = send(gslot(dxh, 2, up), mid.at[at, pl.ds(0, up[1])], dz=UP)
            passed[dxh, DOWN] = send(gslot(dxh, 2, dn), mid.at[at + 1, pl.ds(0, dn[1])], dz=DOWN)
        elif dz:
            passed[dxh, dz].wait_recv()
            add(dxh, dz, up if dz == UP else dn, [(mid, at + dz // 2)])
            gone[dxh, dz] = send(gslot(dxh, dz, rows), far.at[at + dz // 2], dz=dz)

    def finish(g):
        dxh, dz = ORDER[g]
        to_sib[g].wait_recv()
        add(dxh, dz, (0, 256), [(sib, g)])
        if dxh:
            a_1[dz] = send(gslot(dxh, dz, a_rows), ra1.at[dz], dxh=1)

    def second_b(dxh, dz):
        along_z(dxh, dz, b_rows, b_up_rows, b_dn_rows, bm, 2 * dxh, rb1, b_1, b_m)

    def second_a(dz):
        a_1[dz].wait_recv()
        add(0, dz, a_rows, [(ra1, dz)])
        along_z(0, dz, a_rows, a_up_rows, a_dn_rows, am, 0, ra2, a_2, a_m)

    def term_of(g):
        for r in range(4) if g >= 4 else (2,):
            turn(g, r)
        term(g)

    turn(0, 2)
    half_term(0, 0)
    half_term(0, 1)
    turn(1, 2)
    half_term(1, 0)
    finish(0)
    second_b(1, 2)
    half_term(1, 1)
    await_group(sc1)
    at = 8 + xh * 4 + z
    scal[at] = merge(0, 8)
    sc2 = send_all([(scal.at[at], scal.at[at], {"dxh": dx, "dz": dz}) for dx, dz in CONTEXT], "s")
    term_of(2)
    finish(1)
    second_b(0, 2)
    term_of(3)
    finish(2)
    second_b(1, 1)
    term_of(4)
    finish(3)
    second_b(1, 3)
    second_a(2)
    term_of(5)
    finish(4)
    term_of(6)
    finish(5)
    second_b(0, 1)
    term_of(7)
    finish(6)
    second_b(0, 3)
    for n in (UP, DOWN):
        b_1[1, n].wait_recv()
    add(1, 0, b_rows, [(rb1, 2), (rb1, 3)])
    b_2 = send(gslot(1, 0, b_rows), rb2.at[0], dxh=1)
    second_a(1)
    second_a(3)
    await_group(sc2)
    scal[16 + k] = merge(8, 8)
    sc3 = send(scal.at[16 + k], scal.at[16 + k], "s", dk=1)
    finish(7)
    second_a(0)
    sc3.wait_recv()
    scal[18] = merge(16, 2)
    written = [load(scal.at[18], parts.at[pl.ds(256, 8), pl.ds(0, 128)])]

    for n in (UP, DOWN):
        b_1[0, n].wait_recv()
    for (first, count), landed in ((a_rows, []), (b_rows, [(rb1, 0), (rb1, 1)])):

        @pl.loop(0, count // 16)
        def _(i):
            here = pl.ds(pl.multiple_of(16 * i, 16), 16)
            mine = pl.ds(pl.multiple_of(256 + first + 16 * i, 16), 16)
            total = W[3, mine, pl.ds(0, 1024)].astype(F32)
            for ref, index in landed:
                total = total + ref[index, here, :].astype(F32)
            total_g[pl.ds(pl.multiple_of(first + 16 * i, 16), 16), :] = total

        rows = pl.ds(first, count)
        written.append(load(total_g.at[rows], parts.at[rows]))
    for n in (UP, DOWN):
        a_2[0, n].wait_recv()
    b_2.wait_recv()

    assert len(groups) <= SEND_SEMS and len(received) <= RECV_SEMS
    for group in groups:
        if group not in ("t", "w", "r"):
            sent(group)
    for copy in written:
        copy.wait()


def results(
    tokens_all, parts, ra2, rb2, hist_in, hist_w, grad, loss, hist_in_new, hist_w_new,
    held, late_a, late_b, tile, s_in, s_w, s_in_new, s_w_new, s_loss, sem_in, sem_out,
):
    a_rows, b_rows = pl.ds(0, AROWS), pl.ds(AROWS, 256 - AROWS)
    copies = [
        (parts.at[pl.ds(256, 8), pl.ds(0, 128)], tile),
        (hist_in, s_in),
        (hist_w, s_w),
        (parts.at[a_rows], held.at[a_rows]),
        (ra2, late_a),
        (parts.at[b_rows], held.at[b_rows]),
        (rb2, late_b),
    ]
    copies = [pltpu.make_async_copy(a, b, sem_in.at[i]) for i, (a, b) in enumerate(copies)]
    for copy in copies:
        copy.start()
    backs = [
        (s_in_new, hist_in_new),
        (s_w_new, hist_w_new),
        (s_loss, loss),
        (held.at[a_rows], grad.at[a_rows]),
        (held.at[b_rows], grad.at[b_rows]),
    ]
    backs = [pltpu.make_async_copy(a, b, sem_out.at[i]) for i, (a, b) in enumerate(backs)]
    for copy in copies[:3]:
        copy.wait()
    s_in_new[0] = jnp.max(tile[0:1, :])
    s_w_new[0] = jnp.max(tile[1:2, :])
    s_loss[0] = jnp.max(tile[2:3, :]) * (0.5 / (tokens_all * 8192))
    for i in range(15):
        s_in_new[i + 1] = s_in[i]
        s_w_new[i + 1] = s_w[i]
    for back in backs[:3]:
        back.start()
    scale = 1.0 / math.sqrt(tokens_all)
    for first, count, late, n in (0, AROWS, late_a, 2), (AROWS, 256 - AROWS, late_b, 1):
        for copy in copies[3:5] if first == 0 else copies[5:]:
            copy.wait()

        @pl.loop(0, count // 16)
        def _(i):
            here = pl.ds(pl.multiple_of(16 * i, 16), 16)
            rows = pl.ds(pl.multiple_of(first + 16 * i, 16), 16)
            total = held[rows, :]
            for index in range(n):
                total = total + late[index, here, :].astype(F32)
            held[rows, :] = total * scale

        backs[3 if first == 0 else 4].start()
    for back in backs:
        back.wait()


def local(
    teacher_in, teacher_resid, teacher_wo, teacher_gain, input_history, weight_history,
    student_hidden, student_gain, projection,
):
    tokens_all = teacher_in.shape[0] * lax.axis_size("context")
    hbm = pl.BlockSpec(memory_space=pl.ANY)
    parts, late_a, late_b = pl.pallas_call(
        functools.partial(kernel, tokens_all),
        name="distill",
        out_shape=(
            jax.ShapeDtypeStruct((264, 1024), F32),
            jax.ShapeDtypeStruct((2, AROWS, 1024), BF16),
            jax.ShapeDtypeStruct((1, 256 - AROWS, 1024), BF16),
        ),
        in_specs=[hbm] * 9,
        out_specs=(hbm,) * 3,
        scratch_shapes=[
            pltpu.VMEM((1024, 2048), BF16),
            pltpu.VMEM((4, 512, 2048), BF16),
            pltpu.VMEM((4, 256, 4096), BF16),
            pltpu.VMEM((4096, 1024), BF16),
            pltpu.VMEM((1024, 1024), BF16),
            pltpu.VMEM((1024, 1024), F32),
            pltpu.VMEM((1024, 1024), F32),
            pltpu.VMEM((1024, 1024), BF16),
            pltpu.VMEM((1024, 1024), BF16),
            pltpu.VMEM((1024, 1024), BF16),
            pltpu.VMEM((128, 4096), BF16),
            pltpu.VMEM((32, 8192), BF16),
            pltpu.VMEM((1024, 128), F32),
            pltpu.VMEM((8, 8, 128), F32),
            pltpu.VMEM((19, 8, 128), F32),
            pltpu.VMEM((8, 256, 1024), BF16),
            pltpu.VMEM((4, AROWS, 1024), BF16),
            pltpu.VMEM((4, 256 - AROWS, 1024), BF16),
            pltpu.VMEM((2, 64, 1024), BF16),
            pltpu.VMEM((4, 80, 1024), BF16),
            pltpu.VMEM((256, 1024), F32),
            pltpu.VMEM((1, 4096), F32),
            pltpu.VMEM((1, 1024), F32),
            pltpu.SMEM((16,), F32),
            pltpu.SMEM((16,), F32),
            pltpu.SemaphoreType.DMA((SEND_SEMS,)),
            pltpu.SemaphoreType.DMA((RECV_SEMS,)),
            pltpu.SemaphoreType.DMA((13,)),
        ],
        compiler_params=pltpu.CompilerParams(
            collective_id=0, has_side_effects=True, vmem_limit_bytes=62 << 20
        ),
        cost_estimate=pl.CostEstimate(
            flops=3 * 2 * 1024 * 1024 * 4096, bytes_accessed=16 << 20, transcendentals=1024
        ),
    )(
        input_history,
        weight_history,
        student_gain.reshape(1, -1),
        teacher_gain.reshape(1, -1),
        teacher_in,
        teacher_resid,
        teacher_wo,
        student_hidden,
        projection,
    )
    grad, loss, hist_in, hist_w = pl.pallas_call(
        functools.partial(results, tokens_all),
        name="results",
        out_shape=(
            jax.ShapeDtypeStruct((256, 1024), F32),
            jax.ShapeDtypeStruct((1,), F32),
            jax.ShapeDtypeStruct((16,), F32),
            jax.ShapeDtypeStruct((16,), F32),
        ),
        in_specs=[hbm] * 5,
        out_specs=(hbm,) * 4,
        scratch_shapes=[
            pltpu.VMEM((256, 1024), F32),
            pltpu.VMEM((2, AROWS, 1024), BF16),
            pltpu.VMEM((1, 256 - AROWS, 1024), BF16),
            pltpu.VMEM((8, 128), F32),
            *(pltpu.SMEM((n,), F32) for n in (16, 16, 16, 16, 1)),
            pltpu.SemaphoreType.DMA((7,)),
            pltpu.SemaphoreType.DMA((5,)),
        ],
    )(parts, late_a, late_b, input_history, weight_history)
    return grad, loss.reshape(()), hist_in, hist_w


def solution(mesh):
    placed = (
        P("context", "tensor"),
        P("context", "tensor"),
        P("tensor", None),
        P(),
        P(),
        P(),
        P(("context", "tensor"), None),
        P(),
        P("context", "tensor"),
    )
    return jax.shard_map(
        local,
        mesh=mesh,
        in_specs=placed,
        out_specs=(P("context", "tensor"), P(), P(), P()),
        check_vma=False,
    )
```

```python
import functools
import math

import jax
import jax.numpy as jnp
from jax import lax
from jax.experimental import pallas as pl
from jax.experimental.pallas import tpu as pltpu
from jax.sharding import PartitionSpec as P

MESH = pl.DeviceIdType.MESH
F32, BF16 = jnp.float32, jnp.bfloat16
EPS = 1e-05
SEND_SEMS, RECV_SEMS = 7, 73
GROUP = 8 << 20
XCOLS = 3456
PIECES = (0, 1408), (1408, 1408), (2816, 640)
AROWS = 112


def lanes(tile):
    rows, width = tile.shape
    return [
        tile[r : r + 8, c : c + 128]
        for r in range(0, rows, 8)
        for c in range(0, width, 128)
    ]


def fold(op, tile):
    parts = lanes(tile)
    while len(parts) > 1:
        parts = [op(a, b) for a, b in zip(parts[::2], parts[1::2])] + (
            [parts[-1]] if len(parts) % 2 else []
        )
    return parts[0]


def kernel(
    tokens_all,
    hist_in_all, hist_w_all, stu_gain, tea_gain, tin, resid, wo, stu, proj,
    parts, ra2, rb2,
    T, W, S, PR, R, H, M, E, psend, precv, sraw, wraw, col, sq, scal, sib, ra1, rb1, am, bm, total_g, sgain, tgain, hist_in, hist_w,
    ssem, rsem, lsem,
):
    t, c = lax.axis_index("tensor"), lax.axis_index("context")
    y, xl = t // 2, t % 2
    xh, z, k = c // 8, (c // 2) % 4, c % 2

    def dev(dy=0, dxl=0, dxh=0, dz=0, dk=0):
        ny, nz = (y + dy) % 4, (z + dz) % 4
        nxl, nxh, nk = (xl + dxl) % 2, (xh + dxh) % 2, (k + dk) % 2
        return {"tensor": ny * 2 + nxl, "context": nxh * 8 + nz * 2 + nk}

    received, groups = [], {}

    def remote(src, dst, send_sem, recv_sem, to):
        return pltpu.make_async_remote_copy(
            src_ref=src,
            dst_ref=dst,
            send_sem=ssem.at[send_sem],
            recv_sem=rsem.at[recv_sem],
            device_id=to,
            device_id_type=MESH,
        )

    def size(ref):
        return math.prod(ref.shape) * jnp.dtype(ref.dtype).itemsize

    landing = {}

    def send(src, dst, group=None, land=None, **to):
        if group is None:
            group = next((n for n in range(50) if groups.get(n, (0, 0))[1] + size(src) <= GROUP), 0)
        index, held = groups.get(group, (len(groups), 0))
        groups[group] = index, held + size(src)
        if land is None or land not in landing:
            received.append(len(received))
        at, total = landing.get(land, (received[-1], 0))
        if land is not None:
            landing[land] = at, total + size(src)
        copy = remote(src, dst, index, at, dev(**to))
        copy.start()
        return copy

    def span(count):
        if count % 32768 == 0:
            return PR.at[pl.ds(0, count // 2048)]
        return col.at[pl.ds(0, count // 512)]

    def sent(group):
        index, held = groups[group]
        rows = span(held)
        remote(rows, rows, index, 0, dev(dk=1)).wait_send()

    def send_all(pieces, group=None):
        received.append(len(received))
        at, total = received[-1], 0
        for src, dst, to in pieces:
            key = group
            if key is None:
                key = next(n for n in range(50) if groups.get(n, (0, 0))[1] + size(src) <= GROUP)
            index, held = groups.get(key, (len(groups), 0))
            groups[key] = index, held + size(src)
            remote(src, dst, index, at, dev(**to)).start()
            total += size(src)
        return at, total

    def await_group(landed):
        at, total = landed
        rows = span(total)
        remote(rows, rows, 0, at, dev(dk=1)).wait_recv()

    local = []

    def load(src, dst):
        copy = pltpu.make_async_copy(src, dst, lsem.at[len(local)])
        copy.start()
        local.append(copy)
        return copy

    TENSOR = [(dy, dx) for dy in range(4) for dx in range(2) if (dy, dx) != (0, 0)]
    CONTEXT = [(dx, dz) for dx in range(2) for dz in range(4) if (dx, dz) != (0, 0)]
    UP, DOWN = 1, 3

    slab = pl.multiple_of(64 * (2 * z + k) + 32 * xh, 32)
    l_wraw = load(wo.at[pl.ds(slab, 32)], wraw)
    l_hist = load(hist_in_all, hist_in), load(hist_w_all, hist_w)
    l_sgain = load(stu_gain, sgain)
    l_tgain = load(tea_gain.at[:, pl.ds(pl.multiple_of(1024 * t, 1024), 1024)], tgain)
    l_proj = load(proj, PR.at[pl.ds(pl.multiple_of(256 * c, 256), 256)])
    l_stu = load(stu, sraw)
    l_tin = load(tin, T.at[:, pl.ds(0, 512)])
    l_wown = load(wo.at[:, pl.ds(pl.multiple_of(2048 * y, 2048), 2048)], W.at[0])
    l_res = load(resid, R)

    barrier = pltpu.get_barrier_semaphore()
    for dy, dx in TENSOR:
        pl.semaphore_signal(barrier, 1, device_id=dev(dy=dy, dxl=dx), device_id_type=MESH)
    for dx, dz in CONTEXT:
        pl.semaphore_signal(barrier, 1, device_id=dev(dxh=dx, dz=dz), device_id_type=MESH)
    pl.semaphore_signal(barrier, 1, device_id=dev(dk=1), device_id_type=MESH)

    for copy in l_hist:
        copy.wait()
    lim_in, lim_w = hist_in[0], hist_w[0]
    for i in range(1, 16):
        lim_in = jnp.maximum(lim_in, hist_in[i])
        lim_w = jnp.maximum(lim_w, hist_w[i])

    l_wraw.wait()

    def clip_w(i, amax):
        rows = pl.ds(pl.multiple_of(16 * i, 16), 16)
        for n in range(8):
            cols = pl.ds(1024 * n, 1024)
            v = wraw[rows, cols].astype(F32)
            amax = jnp.maximum(amax, fold(jnp.maximum, jnp.abs(v)))
            wraw[rows, cols] = jnp.clip(v, -lim_w, lim_w).astype(BF16)
        return amax

    amax_w = lax.fori_loop(0, 2, clip_w, jnp.zeros((8, 128), F32))

    pl.semaphore_wait(barrier, len(TENSOR) + len(CONTEXT) + 1)

    def wcols(d):
        return pl.ds(pl.multiple_of(2048 * ((y + d) % 4), 2048), 2048)

    w_y = send_all(
        [(wraw.at[:, wcols(d)], W.at[4 - d, pl.ds(slab, 32)], {"dy": d}) for d in (2, 1, 3)]
    )
    l_proj.wait()

    def pblock(dxh=0, dz=0):
        at = ((xh + dxh) % 2) * 8 + ((z + dz) % 4) * 2 + k
        return PR.at[pl.ds(pl.multiple_of(256 * at, 256), 256)]

    p_x = send(pblock(), pblock(), dxh=1)
    p_up = send(pblock(), pblock(), dz=UP)
    p_dn = send(pblock(), pblock(), dz=DOWN)
    p_sib = [send(pblock(), pblock(), land="p", dk=1)]

    l_stu.wait()
    l_sgain.wait()

    @pl.loop(0, 8)
    def _(i):
        rows = pl.ds(pl.multiple_of(16 * i, 16), 16)
        v = sraw[rows, :].astype(F32)
        mean = jnp.mean(v * v, axis=1, keepdims=True)
        S[0, rows, :] = (v * lax.rsqrt(mean + EPS) * sgain[...]).astype(BF16)

    own, far = pl.ds(0, 128), pl.ds(128, 128)
    x_cols, y_cols = pl.ds(0, XCOLS), pl.ds(XCOLS, 4096 - XCOLS)
    own_x, own_y, far_x, far_y = (own, x_cols), (own, y_cols), (far, x_cols), (far, y_cols)
    sy_up = send(S.at[0, *own_y], S.at[3, *own_y], dy=UP)
    sy_dn = send(S.at[0, *own_y], S.at[1, *own_y], dy=DOWN)
    sxy = [send(S.at[0, *own_y], S.at[0, *far_y], dxl=1)]

    l_tin.wait()

    def clip_t(i, amax):
        rows = pl.ds(pl.multiple_of(32 * i, 32), 32)
        v = T[rows, pl.ds(0, 512)].astype(F32)
        T[rows, pl.ds(0, 512)] = jnp.clip(v, -lim_in, lim_in).astype(BF16)
        return jnp.maximum(amax, fold(jnp.maximum, jnp.abs(v)))

    amax_in = lax.fori_loop(0, 32, clip_t, jnp.zeros((8, 128), F32))
    low, high = pl.ds(0, 512), pl.ds(512, 512)

    def tblock(r, rows):
        return T.at[rows, pl.ds(512 * r, 512)]

    t_up = send(tblock(0, low), tblock(3, low), "t", dy=UP)
    t_dn = send(tblock(0, high), tblock(1, high), "t", dy=DOWN)
    t_up1 = send(tblock(0, high), tblock(3, high), "t", "t", dy=UP)
    t_dn1 = send(tblock(0, low), tblock(1, low), "t", "t", dy=DOWN)

    def wslab(dz=0, dxh=None):
        at = pl.multiple_of(64 * (2 * ((z + dz) % 4) + k), 64)
        if dxh is None:
            return W.at[pl.ds(1, 3), pl.ds(at, 64)]
        return W.at[pl.ds(1, 3), pl.ds(pl.multiple_of(at + 32 * ((xh + dxh) % 2), 32), 32)]

    await_group(w_y)
    w_x = send(wslab(0, 0), wslab(0, 0), "w", dxh=1)
    w_up = send(wslab(0, 0), wslab(0, 0), "w", dz=UP)
    w_dn = send(wslab(0, 0), wslab(0, 0), "w", dz=DOWN)
    sx = send(S.at[0, *own_x], S.at[0, *far_x], dxl=1)

    l_wown.wait()

    @pl.loop(0, 32)
    def _(i):
        rows = pl.ds(pl.multiple_of(16 * i, 16), 16)
        v = W[0, rows, :].astype(F32)
        W[0, rows, :] = jnp.clip(v, -lim_w, lim_w).astype(BF16)

    sy_up.wait_recv()
    sxy.append(send(S.at[3, *own_y], S.at[3, *far_y], dxl=1))
    sy_dn.wait_recv()
    sxy.append(send(S.at[1, *own_y], S.at[1, *far_y], dxl=1))
    w_x.wait_recv()
    v_dn = send(wslab(0, 1), wslab(0, 1), "w", dz=DOWN)
    v_up = send(wslab(0, 1), wslab(0, 1), "w", dz=UP)
    w_sib = [send(wslab(), wslab(), "w", "w", dk=1)]

    upper, lower = (pl.ds(0, 64), y_cols), (pl.ds(64, 64), y_cols)
    t_up.wait_recv()
    t_up2 = send(tblock(3, low), tblock(2, low), "t", "t", dy=UP)
    t_dn.wait_recv()
    t_dn2 = send(tblock(1, high), tblock(2, high), "t", "t", dy=DOWN)
    sy_up2 = send(S.at[3, *upper], S.at[2, *upper], dy=UP)
    sy_dn2 = send(S.at[1, *lower], S.at[2, *lower], dy=DOWN)
    a_up = send(S.at[0, *own_x], S.at[3, *own_x], dy=UP)

    w_up.wait_recv()
    w_up2 = send(wslab(DOWN, 0), wslab(DOWN, 0), "w", dz=UP)
    v_dn.wait_recv()
    v_dn2 = send(wslab(UP, 1), wslab(UP, 1), "w", dz=DOWN)
    v_up.wait_recv()
    w_sib.append(send(wslab(DOWN), wslab(DOWN), "w", "w", dk=1))
    w_dn.wait_recv()
    w_sib.append(send(wslab(UP), wslab(UP), "w", "w", dk=1))

    sx.wait_recv()
    b_dn = send(S.at[0, *far_x], S.at[1, *far_x], dy=DOWN)
    b_up = send(S.at[0, *far_x], S.at[3, *far_x], dy=UP)
    a_dn = send(S.at[0, *own_x], S.at[1, *own_x], dy=DOWN)

    w_up2.wait_recv()
    v_dn2.wait_recv()
    w_sib.append(send(wslab(2), wslab(2), "w", "w", dk=1))
    p_x.wait_recv()
    p_sib.append(send(pblock(1), pblock(1), land="p", dk=1))
    q_dn = send(pblock(1), pblock(1), dz=DOWN)
    q_up = send(pblock(1), pblock(1), dz=UP)
    p_up.wait_recv()
    p_up2 = send(pblock(0, DOWN), pblock(0, DOWN), dz=UP)
    p_sib.append(send(pblock(0, DOWN), pblock(0, DOWN), land="p", dk=1))
    p_dn.wait_recv()
    p_sib.append(send(pblock(0, UP), pblock(0, UP), land="p", dk=1))

    await_group(landing["t"])
    await_group(landing["w"])

    def product(rows, col0, n):
        cols = pl.ds(pl.multiple_of(col0 + 256 * n, 256), 256)
        w = W[:, :, cols].reshape(2048, 256)
        return jnp.dot(T[rows, :], w, preferred_element_type=F32)

    rs_t = []
    for q in range(4):
        rows = pl.ds(256 * q, 256)

        @pl.loop(0, 4)
        def _(n):
            cols = pl.ds(pl.multiple_of(256 * n, 256), 256)
            psend[rows, cols] = product(rows, 1024 * (1 - xl), n).astype(BF16)

        for rows in (rows,) if q < 3 else (pl.ds(768, 128), pl.ds(896, 128)):
            rs_t.append(send(psend.at[rows], precv.at[rows], "r", dxl=1))


    sy_up2.wait_recv()
    sy_dn2.wait_recv()
    sxy.append(send(S.at[2, *own_y], S.at[2, *far_y], dxl=1))
    l_res.wait()
    for q in range(4):
        rows = pl.ds(256 * q, 256)

        @pl.loop(0, 4)
        def _(n):
            cols = pl.ds(pl.multiple_of(256 * n, 256), 256)
            H[rows, cols] = product(rows, 1024 * xl, n) + R[rows, cols].astype(F32)

    q_dn.wait_recv()
    q_dn2 = send(pblock(1, UP), pblock(1, UP), dz=DOWN)
    p_sib.append(send(pblock(1, UP), pblock(1, UP), land="p", dk=1))
    q_up.wait_recv()
    p_sib.append(send(pblock(1, DOWN), pblock(1, DOWN), land="p", dk=1))
    p_up2.wait_recv()
    p_sib.append(send(pblock(0, 2), pblock(0, 2), land="p", dk=1))
    first, second, last = [pl.ds(*piece) for piece in PIECES]
    a_up.wait_recv()
    a_up2, a_up3 = [send(S.at[3, own, n], S.at[2, own, n], dy=UP) for n in (first, second)]
    b_dn.wait_recv()
    b_dn2, b_dn3 = [send(S.at[1, far, n], S.at[2, far, n], dy=DOWN) for n in (first, second)]
    q_dn2.wait_recv()
    p_sib.append(send(pblock(1, 2), pblock(1, 2), land="p", dk=1))

    def mapped(r):
        @pl.loop(0, 2)
        def _(n):
            cols = pl.ds(pl.multiple_of(512 * n, 512), 512)
            M[pl.ds(256 * r, 256), cols] = jnp.dot(
                S[r], PR[:, cols], preferred_element_type=F32
            )

    def mapped_part(inner, add_up):
        @pl.loop(0, 2)
        def _(n):
            cols = pl.ds(pl.multiple_of(512 * n, 512), 512)
            out = jnp.dot(S[2, :, inner], PR[inner, cols], preferred_element_type=F32)
            M[pl.ds(512, 256), cols] = M[pl.ds(512, 256), cols] + out if add_up else out

    ORDER = [(1, 2), (0, 2), (1, 1), (1, 3), (1, 0), (0, 1), (0, 3), (0, 0)]

    def turned(g):
        if g < 4:
            return T, 512 * (g % 2), 1024 * (g // 2)
        return (R, psend)[g // 2 - 2], 512 * (g % 2), 0

    def turn(g, r):
        dxh, dz = ORDER[g]
        chip = ((xh + dxh) % 2) * 4 + (z + dz) % 4
        ref, row0, col0 = turned(g)
        for own in (0, 1):
            cols = pl.ds(pl.multiple_of(512 * chip + 256 * ((k + 1 - own) % 2), 256), 256)
            ref[pl.ds(row0 + 256 * own, 256), pl.ds(col0 + 256 * r, 256)] = S[r, :, cols].T

    def turn_first(r):
        for g in range(6):
            turn(g, r)

    l_tgain.wait()
    gains = tgain[...]

    def squares(q):
        rs_t[q].wait_recv()
        first, count = (256 * q, 256) if q < 3 else (128 * q + 384, 128)

        @pl.loop(0, count // 16)
        def _(i):
            rows = pl.ds(pl.multiple_of(first + 16 * i, 16), 16)
            h = H[rows, :] + precv[rows, :].astype(F32)
            H[rows, :] = h * gains
            col[rows, :] = jnp.broadcast_to(jnp.sum(h * h, axis=1, keepdims=True), (16, 128))

    await_group(landing["p"])
    sxy[0].wait_recv()
    mapped(0)
    sent("t")
    turn_first(0)
    squares(0)
    squares(1)
    squares(2)
    b_up.wait_recv()
    sxy[1].wait_recv()
    mapped(3)
    turn_first(3)
    a_dn.wait_recv()
    sxy[2].wait_recv()
    mapped(1)
    squares(3)
    a_up2.wait_recv()
    b_dn2.wait_recv()
    mapped_part(first, False)
    squares(4)
    row = lax.broadcasted_iota(jnp.int32, (8, 128), 0)
    packed = jnp.zeros((8, 128), F32)
    for i in range(8):
        packed = jnp.where(row == i, col[pl.ds(128 * i, 128), :].T[0:8, :], packed)
    sq[0] = packed
    sq_c = send_all(
        [(sq.at[0], sq.at[dy * 2 + dx], {"dy": dy, "dxl": dx}) for dy, dx in TENSOR], "s"
    )
    a_up4 = send(S.at[3, own, last], S.at[2, own, last], dy=UP)
    b_dn4 = send(S.at[1, far, last], S.at[2, far, last], dy=DOWN)
    turn_first(1)
    sent("r")
    for r in (0, 3, 1):
        turn(6, r)
        turn(7, r)

    def errors(r, acc):
        for b in range(2):
            base = 128 * (2 * ((y + r) % 4) + (xl + b) % 2)

            def step(i, acc):
                there = pl.ds(pl.multiple_of(base + 16 * i, 16), 16)
                here = pl.ds(pl.multiple_of(256 * r + 128 * b + 16 * i, 16), 16)
                scale = jnp.concatenate([col[there, :]] * 8, axis=1)
                e = M[here, :] - H[there, :] * scale
                E[here, :] = e.astype(BF16)
                return acc + fold(jnp.add, e * e)

            acc = lax.fori_loop(0, 8, step, acc, unroll=2)
        return acc

    a_up3.wait_recv()
    b_dn3.wait_recv()
    mapped_part(second, True)
    sxy[3].wait_recv()
    mapped_part(y_cols, True)
    await_group(sq_c)
    total = sq[0]
    for i in range(1, 8):
        total = total + sq[i]
    inv = lax.rsqrt(total * (1.0 / 8192) + EPS)
    for i in range(8):
        col[pl.ds(128 * i, 128), :] = jnp.broadcast_to(inv[i : i + 1, :], (128, 128)).T
    acc = jnp.zeros((8, 128), F32)
    for r in (0, 3, 1):
        acc = errors(r, acc)

    @pl.loop(0, 2)
    def _(n):
        cols = pl.ds(pl.multiple_of(512 * n, 512), 512)
        M[pl.ds(0, 256), cols] = jnp.dot(
            T[pl.ds(0, 256), pl.ds(0, 512)], E[pl.ds(0, 512), cols], preferred_element_type=F32
        ) + jnp.dot(
            T[pl.ds(0, 256), pl.ds(768, 256)], E[pl.ds(768, 256), cols], preferred_element_type=F32
        )

    a_up4.wait_recv()
    b_dn4.wait_recv()
    mapped_part(last, True)
    acc = errors(2, acc)

    tile = jnp.where(row == 0, jnp.max(amax_in), jnp.where(row == 1, jnp.max(amax_w), jnp.sum(acc)))

    def merge(first, count):
        out = scal[first]
        for i in range(1, count):
            v = scal[first + i]
            out = jnp.where(row < 2, jnp.maximum(out, v), out + v)
        return out

    scal[t] = tile
    sc1 = send_all([(scal.at[t], scal.at[t], {"dy": dy, "dxl": dx}) for dy, dx in TENSOR], "s")

    sent("w")

    a_rows, b_rows = (0, AROWS), (AROWS, 256 - AROWS)
    a_up_rows, a_dn_rows = (0, 80), (80, AROWS - 80)
    b_up_rows, b_dn_rows = (AROWS, 64), (AROWS + 64, 192 - AROWS)

    def gslot(dxh, dz, rows=(0, 256), other=0):
        g = ORDER.index((dxh, dz))
        return W.at[g // 2, pl.ds(256 * (g % 2) + rows[0], rows[1]), pl.ds(1024 * other, 1024)]

    to_sib, a_1, b_1, a_2, a_m, b_m = [], {}, {}, {}, {}, {}

    def half_term(g, own):
        dxh, dz = ORDER[g]
        ref, row0, col0 = turned(g)

        @pl.loop(0, 2)
        def _(n):
            at = pl.multiple_of(512 * n, 512)
            rows, cols = pl.ds(row0 + 256 * own, 256), pl.ds(at, 512)
            one = jnp.dot(ref[rows, pl.ds(col0, 1024)], E[:, cols], preferred_element_type=F32)
            start = pl.multiple_of(1024 * (1 - own) + at, 512)
            W[g // 2, pl.ds(256 * (g % 2), 256), pl.ds(start, 512)] = one.astype(BF16)

        if own == 0:
            to_sib.append(send(gslot(dxh, dz, other=1), sib.at[g], dk=1))

    def first_half_term():
        for n in range(2):
            cols, there = pl.ds(512 * n, 512), pl.ds(1024 + 512 * n, 512)
            one = M[pl.ds(0, 256), cols] + jnp.dot(
                T[pl.ds(0, 256), pl.ds(512, 256)], E[pl.ds(512, 256), cols], preferred_element_type=F32
            )
            W[0, pl.ds(0, 256), there] = one.astype(BF16)
            send(W.at[0, pl.ds(0, 256), there], sib.at[0, pl.ds(0, 256), cols], land="first", dk=1)
        to_sib.append(None)

    def term(g):
        dxh, dz = ORDER[g]
        ref, row0, col0 = turned(g)

        @pl.loop(0, 2)
        def _(n):
            at = pl.multiple_of(512 * n, 512)
            both = jnp.dot(
                ref[pl.ds(row0, 512), pl.ds(col0, 1024)],
                E[:, pl.ds(at, 512)],
                preferred_element_type=F32,
            ).astype(BF16)
            rows = pl.ds(256 * (g % 2), 256)
            W[g // 2, rows, pl.ds(pl.multiple_of(1024 + at, 512), 512)] = both[:256]
            W[g // 2, rows, pl.ds(at, 512)] = both[256:]

        to_sib.append(send(gslot(dxh, dz, other=1), sib.at[g], dk=1))

    def add(dxh, dz, rows, others, base=0):
        g = ORDER.index((dxh, dz))

        @pl.loop(0, rows[1] // 16)
        def _(i):
            here = pl.ds(pl.multiple_of(base + 16 * i, 16), 16)
            there = pl.ds(pl.multiple_of(256 * (g % 2) + rows[0] + 16 * i, 16), 16)
            total = W[g // 2, there, pl.ds(0, 1024)].astype(F32)
            for ref, index in others:
                total = total + ref[index, here, :].astype(F32)
            W[g // 2, there, pl.ds(0, 1024)] = total.astype(BF16)

    def along_z(dxh, dz, rows, up, dn, mid, at, far, gone, passed):
        if dz == 2:
            passed[dxh, UP] = send(gslot(dxh, 2, up), mid.at[at, pl.ds(0, up[1])], dz=UP)
            passed[dxh, DOWN] = send(gslot(dxh, 2, dn), mid.at[at + 1, pl.ds(0, dn[1])], dz=DOWN)
        elif dz:
            passed[dxh, dz].wait_recv()
            add(dxh, dz, up if dz == UP else dn, [(mid, at + dz // 2)])
            gone[dxh, dz] = send(gslot(dxh, dz, rows), far.at[at + dz // 2], dz=dz)

    def finish(g):
        dxh, dz = ORDER[g]
        to_sib[g].wait_recv()
        add(dxh, dz, (0, 256), [(sib, g)])
        if dxh:
            a_1[dz] = send(gslot(dxh, dz, a_rows), ra1.at[dz], dxh=1)

    def second_b(dxh, dz):
        along_z(dxh, dz, b_rows, b_up_rows, b_dn_rows, bm, 2 * dxh, rb1, b_1, b_m)

    def second_a(dz):
        a_1[dz].wait_recv()
        add(0, dz, a_rows, [(ra1, dz)])
        along_z(0, dz, a_rows, a_up_rows, a_dn_rows, am, 0, ra2, a_2, a_m)

    def term_of(g):
        turn(g, 2)
        term(g)

    turn(0, 2)
    first_half_term()
    half_term(0, 1)
    turn(1, 2)
    half_term(1, 0)
    await_group(landing["first"])
    add(1, 2, b_rows, [(sib, 0)], AROWS)
    second_b(1, 2)
    add(1, 2, a_rows, [(sib, 0)])
    a_1[2] = send(gslot(1, 2, a_rows), ra1.at[2], dxh=1)
    half_term(1, 1)
    await_group(sc1)
    at = 8 + xh * 4 + z
    scal[at] = merge(0, 8)
    sc2 = send_all([(scal.at[at], scal.at[at], {"dxh": dx, "dz": dz}) for dx, dz in CONTEXT], "s")
    term_of(2)
    finish(1)
    second_b(0, 2)
    term_of(3)
    finish(2)
    second_b(1, 1)
    term_of(4)
    finish(3)
    second_b(1, 3)
    second_a(2)
    term_of(5)
    finish(4)
    term_of(6)
    finish(5)
    second_b(0, 1)
    term_of(7)
    finish(6)
    second_b(0, 3)
    for n in (UP, DOWN):
        b_1[1, n].wait_recv()
    add(1, 0, b_rows, [(rb1, 2), (rb1, 3)])
    b_2 = send(gslot(1, 0, b_rows), rb2.at[0], dxh=1)
    second_a(1)
    second_a(3)
    await_group(sc2)
    scal[16 + k] = merge(8, 8)
    sc3 = send(scal.at[16 + k], scal.at[16 + k], "s", dk=1)
    finish(7)
    second_a(0)
    sc3.wait_recv()
    scal[18] = merge(16, 2)
    written = [load(scal.at[18], parts.at[pl.ds(256, 8), pl.ds(0, 128)])]

    for n in (UP, DOWN):
        b_1[0, n].wait_recv()
    for (first, count), landed in ((a_rows, []), (b_rows, [(rb1, 0), (rb1, 1)])):

        @pl.loop(0, count // 16)
        def _(i):
            here = pl.ds(pl.multiple_of(16 * i, 16), 16)
            mine = pl.ds(pl.multiple_of(256 + first + 16 * i, 16), 16)
            total = W[3, mine, pl.ds(0, 1024)].astype(F32)
            for ref, index in landed:
                total = total + ref[index, here, :].astype(F32)
            total_g[pl.ds(pl.multiple_of(first + 16 * i, 16), 16), :] = total

        rows = pl.ds(first, count)
        written.append(load(total_g.at[rows], parts.at[rows]))
    for n in (UP, DOWN):
        a_2[0, n].wait_recv()
    b_2.wait_recv()

    assert len(groups) <= SEND_SEMS and len(received) <= RECV_SEMS
    for group in groups:
        if group not in ("t", "w", "r"):
            sent(group)
    for copy in written:
        copy.wait()


def results(
    tokens_all, parts, ra2, rb2, hist_in, hist_w, grad, loss, hist_in_new, hist_w_new,
    held, late_a, late_b, tile, s_in, s_w, s_in_new, s_w_new, s_loss, sem_in, sem_out,
):
    a_rows, b_rows = pl.ds(0, AROWS), pl.ds(AROWS, 256 - AROWS)
    copies = [
        (parts.at[pl.ds(256, 8), pl.ds(0, 128)], tile),
        (hist_in, s_in),
        (hist_w, s_w),
        (parts.at[a_rows], held.at[a_rows]),
        (ra2, late_a),
        (parts.at[b_rows], held.at[b_rows]),
        (rb2, late_b),
    ]
    copies = [pltpu.make_async_copy(a, b, sem_in.at[i]) for i, (a, b) in enumerate(copies)]
    for copy in copies:
        copy.start()
    backs = [
        (s_in_new, hist_in_new),
        (s_w_new, hist_w_new),
        (s_loss, loss),
        (held.at[a_rows], grad.at[a_rows]),
        (held.at[b_rows], grad.at[b_rows]),
    ]
    backs = [pltpu.make_async_copy(a, b, sem_out.at[i]) for i, (a, b) in enumerate(backs)]
    for copy in copies[:3]:
        copy.wait()
    s_in_new[0] = jnp.max(tile[0:1, :])
    s_w_new[0] = jnp.max(tile[1:2, :])
    s_loss[0] = jnp.max(tile[2:3, :]) * (0.5 / (tokens_all * 8192))
    for i in range(15):
        s_in_new[i + 1] = s_in[i]
        s_w_new[i + 1] = s_w[i]
    for back in backs[:3]:
        back.start()
    scale = 1.0 / math.sqrt(tokens_all)
    for first, count, late, n in (0, AROWS, late_a, 2), (AROWS, 256 - AROWS, late_b, 1):
        for copy in copies[3:5] if first == 0 else copies[5:]:
            copy.wait()

        @pl.loop(0, count // 16)
        def _(i):
            here = pl.ds(pl.multiple_of(16 * i, 16), 16)
            rows = pl.ds(pl.multiple_of(first + 16 * i, 16), 16)
            total = held[rows, :]
            for index in range(n):
                total = total + late[index, here, :].astype(F32)
            held[rows, :] = total * scale

        backs[3 if first == 0 else 4].start()
    for back in backs:
        back.wait()


def local(
    teacher_in, teacher_resid, teacher_wo, teacher_gain, input_history, weight_history,
    student_hidden, student_gain, projection,
):
    tokens_all = teacher_in.shape[0] * lax.axis_size("context")
    hbm = pl.BlockSpec(memory_space=pl.ANY)
    parts, late_a, late_b = pl.pallas_call(
        functools.partial(kernel, tokens_all),
        name="distill",
        out_shape=(
            jax.ShapeDtypeStruct((264, 1024), F32),
            jax.ShapeDtypeStruct((2, AROWS, 1024), BF16),
            jax.ShapeDtypeStruct((1, 256 - AROWS, 1024), BF16),
        ),
        in_specs=[hbm] * 9,
        out_specs=(hbm,) * 3,
        scratch_shapes=[
            pltpu.VMEM((1024, 2048), BF16),
            pltpu.VMEM((4, 512, 2048), BF16),
            pltpu.VMEM((4, 256, 4096), BF16),
            pltpu.VMEM((4096, 1024), BF16),
            pltpu.VMEM((1024, 1024), BF16),
            pltpu.VMEM((1024, 1024), F32),
            pltpu.VMEM((1024, 1024), F32),
            pltpu.VMEM((1024, 1024), BF16),
            pltpu.VMEM((1024, 1024), BF16),
            pltpu.VMEM((1024, 1024), BF16),
            pltpu.VMEM((128, 4096), BF16),
            pltpu.VMEM((32, 8192), BF16),
            pltpu.VMEM((1024, 128), F32),
            pltpu.VMEM((8, 8, 128), F32),
            pltpu.VMEM((19, 8, 128), F32),
            pltpu.VMEM((8, 256, 1024), BF16),
            pltpu.VMEM((4, AROWS, 1024), BF16),
            pltpu.VMEM((4, 256 - AROWS, 1024), BF16),
            pltpu.VMEM((2, 96, 1024), BF16),
            pltpu.VMEM((4, 96, 1024), BF16),
            pltpu.VMEM((256, 1024), F32),
            pltpu.VMEM((1, 4096), F32),
            pltpu.VMEM((1, 1024), F32),
            pltpu.SMEM((16,), F32),
            pltpu.SMEM((16,), F32),
            pltpu.SemaphoreType.DMA((SEND_SEMS,)),
            pltpu.SemaphoreType.DMA((RECV_SEMS,)),
            pltpu.SemaphoreType.DMA((13,)),
        ],
        compiler_params=pltpu.CompilerParams(
            collective_id=0, has_side_effects=True, vmem_limit_bytes=62 << 20
        ),
        cost_estimate=pl.CostEstimate(
            flops=3 * 2 * 1024 * 1024 * 4096, bytes_accessed=16 << 20, transcendentals=1024
        ),
    )(
        input_history,
        weight_history,
        student_gain.reshape(1, -1),
        teacher_gain.reshape(1, -1),
        teacher_in,
        teacher_resid,
        teacher_wo,
        student_hidden,
        projection,
    )
    grad, loss, hist_in, hist_w = pl.pallas_call(
        functools.partial(results, tokens_all),
        name="results",
        out_shape=(
            jax.ShapeDtypeStruct((256, 1024), F32),
            jax.ShapeDtypeStruct((1,), F32),
            jax.ShapeDtypeStruct((16,), F32),
            jax.ShapeDtypeStruct((16,), F32),
        ),
        in_specs=[hbm] * 5,
        out_specs=(hbm,) * 4,
        scratch_shapes=[
            pltpu.VMEM((256, 1024), F32),
            pltpu.VMEM((2, AROWS, 1024), BF16),
            pltpu.VMEM((1, 256 - AROWS, 1024), BF16),
            pltpu.VMEM((8, 128), F32),
            *(pltpu.SMEM((n,), F32) for n in (16, 16, 16, 16, 1)),
            pltpu.SemaphoreType.DMA((7,)),
            pltpu.SemaphoreType.DMA((5,)),
        ],
    )(parts, late_a, late_b, input_history, weight_history)
    return grad, loss.reshape(()), hist_in, hist_w


def solution(mesh):
    placed = (
        P("context", "tensor"),
        P("context", "tensor"),
        P("tensor", None),
        P(),
        P(),
        P(),
        P(("context", "tensor"), None),
        P(),
        P("context", "tensor"),
    )
    return jax.shard_map(
        local,
        mesh=mesh,
        in_specs=placed,
        out_specs=(P("context", "tensor"), P(), P(), P()),
        check_vma=False,
    )
```

```python
import functools
import math

import jax
import jax.numpy as jnp
from jax import lax
from jax.experimental import pallas as pl
from jax.experimental.pallas import tpu as pltpu
from jax.sharding import PartitionSpec as P

MESH = pl.DeviceIdType.MESH
F32, BF16 = jnp.float32, jnp.bfloat16
EPS = 1e-05
SEND_SEMS, RECV_SEMS = 7, 73
GROUP = 8 << 20
XCOLS = 3456
PIECES = (0, 1408), (1408, 1408), (2816, 640)
AROWS = 112


def lanes(tile):
    rows, width = tile.shape
    return [
        tile[r : r + 8, c : c + 128]
        for r in range(0, rows, 8)
        for c in range(0, width, 128)
    ]


def fold(op, tile):
    parts = lanes(tile)
    while len(parts) > 1:
        parts = [op(a, b) for a, b in zip(parts[::2], parts[1::2])] + (
            [parts[-1]] if len(parts) % 2 else []
        )
    return parts[0]


def kernel(
    tokens_all,
    hist_in_all, hist_w_all, stu_gain, tea_gain, tin, resid, wo, stu, proj,
    parts, ra2, rb2,
    T, W, S, PR, R, H, M, E, psend, precv, sraw, wraw, col, sq, scal, sib, ra1, rb1, am, bm, total_g, sgain, tgain, hist_in, hist_w,
    ssem, rsem, lsem,
):
    t, c = lax.axis_index("tensor"), lax.axis_index("context")
    y, xl = t // 2, t % 2
    xh, z, k = c // 8, (c // 2) % 4, c % 2

    def dev(dy=0, dxl=0, dxh=0, dz=0, dk=0):
        ny, nz = (y + dy) % 4, (z + dz) % 4
        nxl, nxh, nk = (xl + dxl) % 2, (xh + dxh) % 2, (k + dk) % 2
        return {"tensor": ny * 2 + nxl, "context": nxh * 8 + nz * 2 + nk}

    received, groups = [], {}

    def remote(src, dst, send_sem, recv_sem, to):
        return pltpu.make_async_remote_copy(
            src_ref=src,
            dst_ref=dst,
            send_sem=ssem.at[send_sem],
            recv_sem=rsem.at[recv_sem],
            device_id=to,
            device_id_type=MESH,
        )

    def size(ref):
        return math.prod(ref.shape) * jnp.dtype(ref.dtype).itemsize

    landing = {}

    def send(src, dst, group=None, land=None, **to):
        if group is None:
            group = next((n for n in range(50) if groups.get(n, (0, 0))[1] + size(src) <= GROUP), 0)
        index, held = groups.get(group, (len(groups), 0))
        groups[group] = index, held + size(src)
        if land is None or land not in landing:
            received.append(len(received))
        at, total = landing.get(land, (received[-1], 0))
        if land is not None:
            landing[land] = at, total + size(src)
        copy = remote(src, dst, index, at, dev(**to))
        copy.start()
        return copy

    def span(count):
        if count % 32768 == 0:
            return PR.at[pl.ds(0, count // 2048)]
        return col.at[pl.ds(0, count // 512)]

    def sent(group):
        index, held = groups[group]
        rows = span(held)
        remote(rows, rows, index, 0, dev(dk=1)).wait_send()

    def send_all(pieces, group=None):
        received.append(len(received))
        at, total = received[-1], 0
        for src, dst, to in pieces:
            key = group
            if key is None:
                key = next(n for n in range(50) if groups.get(n, (0, 0))[1] + size(src) <= GROUP)
            index, held = groups.get(key, (len(groups), 0))
            groups[key] = index, held + size(src)
            remote(src, dst, index, at, dev(**to)).start()
            total += size(src)
        return at, total

    def await_group(landed):
        at, total = landed
        rows = span(total)
        remote(rows, rows, 0, at, dev(dk=1)).wait_recv()

    local = []

    def load(src, dst):
        copy = pltpu.make_async_copy(src, dst, lsem.at[len(local)])
        copy.start()
        local.append(copy)
        return copy

    TENSOR = [(dy, dx) for dy in range(4) for dx in range(2) if (dy, dx) != (0, 0)]
    CONTEXT = [(dx, dz) for dx in range(2) for dz in range(4) if (dx, dz) != (0, 0)]
    UP, DOWN = 1, 3

    slab = pl.multiple_of(64 * (2 * z + k) + 32 * xh, 32)
    l_wraw = load(wo.at[pl.ds(slab, 32)], wraw)
    l_hist = load(hist_in_all, hist_in), load(hist_w_all, hist_w)
    l_sgain = load(stu_gain, sgain)
    l_tgain = load(tea_gain.at[:, pl.ds(pl.multiple_of(1024 * t, 1024), 1024)], tgain)
    l_proj = load(proj, PR.at[pl.ds(pl.multiple_of(256 * c, 256), 256)])
    l_stu = load(stu, sraw)
    l_tin = load(tin, T.at[:, pl.ds(0, 512)])
    l_wown = load(wo.at[:, pl.ds(pl.multiple_of(2048 * y, 2048), 2048)], W.at[0])
    l_res = load(resid, R)

    barrier = pltpu.get_barrier_semaphore()
    for dy, dx in TENSOR:
        pl.semaphore_signal(barrier, 1, device_id=dev(dy=dy, dxl=dx), device_id_type=MESH)
    for dx, dz in CONTEXT:
        pl.semaphore_signal(barrier, 1, device_id=dev(dxh=dx, dz=dz), device_id_type=MESH)
    pl.semaphore_signal(barrier, 1, device_id=dev(dk=1), device_id_type=MESH)

    for copy in l_hist:
        copy.wait()
    lim_in, lim_w = hist_in[0], hist_w[0]
    for i in range(1, 16):
        lim_in = jnp.maximum(lim_in, hist_in[i])
        lim_w = jnp.maximum(lim_w, hist_w[i])

    l_wraw.wait()

    def clip_w(i, amax):
        rows = pl.ds(pl.multiple_of(16 * i, 16), 16)
        for n in range(8):
            cols = pl.ds(1024 * n, 1024)
            v = wraw[rows, cols].astype(F32)
            amax = jnp.maximum(amax, fold(jnp.maximum, jnp.abs(v)))
            wraw[rows, cols] = jnp.clip(v, -lim_w, lim_w).astype(BF16)
        return amax

    amax_w = lax.fori_loop(0, 2, clip_w, jnp.zeros((8, 128), F32))

    pl.semaphore_wait(barrier, len(TENSOR) + len(CONTEXT) + 1)

    def wcols(d):
        return pl.ds(pl.multiple_of(2048 * ((y + d) % 4), 2048), 2048)

    w_y = send_all(
        [(wraw.at[:, wcols(d)], W.at[4 - d, pl.ds(slab, 32)], {"dy": d}) for d in (2, 1, 3)]
    )
    l_proj.wait()

    def pblock(dxh=0, dz=0):
        at = ((xh + dxh) % 2) * 8 + ((z + dz) % 4) * 2 + k
        return PR.at[pl.ds(pl.multiple_of(256 * at, 256), 256)]

    p_x = send(pblock(), pblock(), dxh=1)
    p_up = send(pblock(), pblock(), dz=UP)
    p_dn = send(pblock(), pblock(), dz=DOWN)
    p_sib = [send(pblock(), pblock(), land="p", dk=1)]

    l_stu.wait()
    l_sgain.wait()

    @pl.loop(0, 8)
    def _(i):
        rows = pl.ds(pl.multiple_of(16 * i, 16), 16)
        v = sraw[rows, :].astype(F32)
        mean = jnp.mean(v * v, axis=1, keepdims=True)
        S[0, rows, :] = (v * lax.rsqrt(mean + EPS) * sgain[...]).astype(BF16)

    own, far = pl.ds(0, 128), pl.ds(128, 128)
    x_cols, y_cols = pl.ds(0, XCOLS), pl.ds(XCOLS, 4096 - XCOLS)
    own_x, own_y, far_x, far_y = (own, x_cols), (own, y_cols), (far, x_cols), (far, y_cols)
    sy_up = send(S.at[0, *own_y], S.at[3, *own_y], dy=UP)
    sy_dn = send(S.at[0, *own_y], S.at[1, *own_y], dy=DOWN)
    sxy = [send(S.at[0, *own_y], S.at[0, *far_y], dxl=1)]

    l_tin.wait()

    def clip_t(i, amax):
        rows = pl.ds(pl.multiple_of(32 * i, 32), 32)
        v = T[rows, pl.ds(0, 512)].astype(F32)
        T[rows, pl.ds(0, 512)] = jnp.clip(v, -lim_in, lim_in).astype(BF16)
        return jnp.maximum(amax, fold(jnp.maximum, jnp.abs(v)))

    amax_in = lax.fori_loop(0, 32, clip_t, jnp.zeros((8, 128), F32))
    low, high = pl.ds(0, 512), pl.ds(512, 512)

    def tblock(r, rows):
        return T.at[rows, pl.ds(512 * r, 512)]

    t_up = send(tblock(0, low), tblock(3, low), "t", dy=UP)
    t_dn = send(tblock(0, high), tblock(1, high), "t", dy=DOWN)
    t_up1 = send(tblock(0, high), tblock(3, high), "t", "t", dy=UP)
    t_dn1 = send(tblock(0, low), tblock(1, low), "t", "t", dy=DOWN)

    def wslab(dz=0, dxh=None):
        at = pl.multiple_of(64 * (2 * ((z + dz) % 4) + k), 64)
        if dxh is None:
            return W.at[pl.ds(1, 3), pl.ds(at, 64)]
        return W.at[pl.ds(1, 3), pl.ds(pl.multiple_of(at + 32 * ((xh + dxh) % 2), 32), 32)]

    await_group(w_y)
    w_x = send(wslab(0, 0), wslab(0, 0), "w", dxh=1)
    w_up = send(wslab(0, 0), wslab(0, 0), "w", dz=UP)
    w_dn = send(wslab(0, 0), wslab(0, 0), "w", dz=DOWN)
    sx = send(S.at[0, *own_x], S.at[0, *far_x], dxl=1)

    l_wown.wait()

    @pl.loop(0, 32)
    def _(i):
        rows = pl.ds(pl.multiple_of(16 * i, 16), 16)
        v = W[0, rows, :].astype(F32)
        W[0, rows, :] = jnp.clip(v, -lim_w, lim_w).astype(BF16)

    sy_up.wait_recv()
    sxy.append(send(S.at[3, *own_y], S.at[3, *far_y], dxl=1))
    sy_dn.wait_recv()
    sxy.append(send(S.at[1, *own_y], S.at[1, *far_y], dxl=1))
    w_x.wait_recv()
    v_dn = send(wslab(0, 1), wslab(0, 1), "w", dz=DOWN)
    v_up = send(wslab(0, 1), wslab(0, 1), "w", dz=UP)
    w_sib = [send(wslab(), wslab(), "w", "w", dk=1)]

    upper, lower = (pl.ds(0, 64), y_cols), (pl.ds(64, 64), y_cols)
    t_up.wait_recv()
    t_up2 = send(tblock(3, low), tblock(2, low), "t", "t", dy=UP)
    t_dn.wait_recv()
    t_dn2 = send(tblock(1, high), tblock(2, high), "t", "t", dy=DOWN)
    sy_up2 = send(S.at[3, *upper], S.at[2, *upper], dy=UP)
    sy_dn2 = send(S.at[1, *lower], S.at[2, *lower], dy=DOWN)
    a_up = send(S.at[0, *own_x], S.at[3, *own_x], dy=UP)

    w_up.wait_recv()
    w_up2 = send(wslab(DOWN, 0), wslab(DOWN, 0), "w", dz=UP)
    v_dn.wait_recv()
    v_dn2 = send(wslab(UP, 1), wslab(UP, 1), "w", dz=DOWN)
    v_up.wait_recv()
    w_sib.append(send(wslab(DOWN), wslab(DOWN), "w", "w", dk=1))
    w_dn.wait_recv()
    w_sib.append(send(wslab(UP), wslab(UP), "w", "w", dk=1))

    sx.wait_recv()
    b_dn = send(S.at[0, *far_x], S.at[1, *far_x], dy=DOWN)
    b_up = send(S.at[0, *far_x], S.at[3, *far_x], dy=UP)
    a_dn = send(S.at[0, *own_x], S.at[1, *own_x], dy=DOWN)

    w_up2.wait_recv()
    v_dn2.wait_recv()
    w_sib.append(send(wslab(2), wslab(2), "w", "w", dk=1))
    p_x.wait_recv()
    p_sib.append(send(pblock(1), pblock(1), land="p", dk=1))
    q_dn = send(pblock(1), pblock(1), dz=DOWN)
    q_up = send(pblock(1), pblock(1), dz=UP)
    p_up.wait_recv()
    p_up2 = send(pblock(0, DOWN), pblock(0, DOWN), dz=UP)
    p_sib.append(send(pblock(0, DOWN), pblock(0, DOWN), land="p", dk=1))
    p_dn.wait_recv()
    p_sib.append(send(pblock(0, UP), pblock(0, UP), land="p", dk=1))

    await_group(landing["t"])
    await_group(landing["w"])

    def product(rows, col0, n):
        cols = pl.ds(pl.multiple_of(col0 + 256 * n, 256), 256)
        w = W[:, :, cols].reshape(2048, 256)
        return jnp.dot(T[rows, :], w, preferred_element_type=F32)

    rs_t = []
    for q in range(4):
        rows = pl.ds(256 * q, 256)

        @pl.loop(0, 4)
        def _(n):
            cols = pl.ds(pl.multiple_of(256 * n, 256), 256)
            psend[rows, cols] = product(rows, 1024 * (1 - xl), n).astype(BF16)

        for rows in (rows,) if q < 3 else (pl.ds(768, 192), pl.ds(960, 64)):
            rs_t.append(send(psend.at[rows], precv.at[rows], "r", dxl=1))


    sy_up2.wait_recv()
    sy_dn2.wait_recv()
    sxy.append(send(S.at[2, *own_y], S.at[2, *far_y], dxl=1))
    l_res.wait()
    for q in range(4):
        rows = pl.ds(256 * q, 256)

        @pl.loop(0, 4)
        def _(n):
            cols = pl.ds(pl.multiple_of(256 * n, 256), 256)
            H[rows, cols] = product(rows, 1024 * xl, n) + R[rows, cols].astype(F32)

    q_dn.wait_recv()
    q_dn2 = send(pblock(1, UP), pblock(1, UP), dz=DOWN)
    p_sib.append(send(pblock(1, UP), pblock(1, UP), land="p", dk=1))
    q_up.wait_recv()
    p_sib.append(send(pblock(1, DOWN), pblock(1, DOWN), land="p", dk=1))
    p_up2.wait_recv()
    p_sib.append(send(pblock(0, 2), pblock(0, 2), land="p", dk=1))
    first, second, last = [pl.ds(*piece) for piece in PIECES]
    a_up.wait_recv()
    a_up2, a_up3 = [send(S.at[3, own, n], S.at[2, own, n], dy=UP) for n in (first, second)]
    b_dn.wait_recv()
    b_dn2, b_dn3 = [send(S.at[1, far, n], S.at[2, far, n], dy=DOWN) for n in (first, second)]
    q_dn2.wait_recv()
    p_sib.append(send(pblock(1, 2), pblock(1, 2), land="p", dk=1))

    def mapped(r):
        @pl.loop(0, 2)
        def _(n):
            cols = pl.ds(pl.multiple_of(512 * n, 512), 512)
            M[pl.ds(256 * r, 256), cols] = jnp.dot(
                S[r], PR[:, cols], preferred_element_type=F32
            )

    def mapped_part(inner, add_up):
        @pl.loop(0, 2)
        def _(n):
            cols = pl.ds(pl.multiple_of(512 * n, 512), 512)
            out = jnp.dot(S[2, :, inner], PR[inner, cols], preferred_element_type=F32)
            M[pl.ds(512, 256), cols] = M[pl.ds(512, 256), cols] + out if add_up else out

    ORDER = [(1, 2), (0, 2), (1, 1), (1, 3), (1, 0), (0, 1), (0, 3), (0, 0)]

    def turned(g):
        if g < 4:
            return T, 512 * (g % 2), 1024 * (g // 2)
        return (R, psend)[g // 2 - 2], 512 * (g % 2), 0

    def turn(g, r):
        dxh, dz = ORDER[g]
        chip = ((xh + dxh) % 2) * 4 + (z + dz) % 4
        ref, row0, col0 = turned(g)
        for own in (0, 1):
            cols = pl.ds(pl.multiple_of(512 * chip + 256 * ((k + 1 - own) % 2), 256), 256)
            ref[pl.ds(row0 + 256 * own, 256), pl.ds(col0 + 256 * r, 256)] = S[r, :, cols].T

    def turn_first(r):
        for g in range(6):
            turn(g, r)

    l_tgain.wait()
    gains = tgain[...]

    def squares(q):
        rs_t[q].wait_recv()
        first, count = (256 * q, 256) if q < 3 else (192 * q + 192, 192 if q == 3 else 64)

        @pl.loop(0, count // 16)
        def _(i):
            rows = pl.ds(pl.multiple_of(first + 16 * i, 16), 16)
            h = H[rows, :] + precv[rows, :].astype(F32)
            H[rows, :] = h * gains
            col[rows, :] = jnp.broadcast_to(jnp.sum(h * h, axis=1, keepdims=True), (16, 128))

    await_group(landing["p"])
    sxy[0].wait_recv()
    mapped(0)
    sent("t")
    turn_first(0)
    squares(0)
    squares(1)
    squares(2)
    b_up.wait_recv()
    sxy[1].wait_recv()
    mapped(3)
    turn_first(3)
    a_dn.wait_recv()
    sxy[2].wait_recv()
    mapped(1)
    squares(3)
    a_up2.wait_recv()
    b_dn2.wait_recv()
    mapped_part(first, False)
    squares(4)
    row = lax.broadcasted_iota(jnp.int32, (8, 128), 0)
    packed = jnp.zeros((8, 128), F32)
    for i in range(8):
        packed = jnp.where(row == i, col[pl.ds(128 * i, 128), :].T[0:8, :], packed)
    sq[0] = packed
    sq_c = send_all(
        [(sq.at[0], sq.at[dy * 2 + dx], {"dy": dy, "dxl": dx}) for dy, dx in TENSOR], "s"
    )
    a_up4 = send(S.at[3, own, last], S.at[2, own, last], dy=UP)
    b_dn4 = send(S.at[1, far, last], S.at[2, far, last], dy=DOWN)
    turn_first(1)
    sent("r")
    for r in (0, 3, 1):
        turn(6, r)
        turn(7, r)

    def errors(r, acc):
        for b in range(2):
            base = 128 * (2 * ((y + r) % 4) + (xl + b) % 2)

            def step(i, acc):
                there = pl.ds(pl.multiple_of(base + 16 * i, 16), 16)
                here = pl.ds(pl.multiple_of(256 * r + 128 * b + 16 * i, 16), 16)
                scale = jnp.concatenate([col[there, :]] * 8, axis=1)
                e = M[here, :] - H[there, :] * scale
                E[here, :] = e.astype(BF16)
                return acc + fold(jnp.add, e * e)

            acc = lax.fori_loop(0, 8, step, acc, unroll=2)
        return acc

    a_up3.wait_recv()
    b_dn3.wait_recv()
    mapped_part(second, True)
    sxy[3].wait_recv()
    mapped_part(y_cols, True)
    await_group(sq_c)
    total = sq[0]
    for i in range(1, 8):
        total = total + sq[i]
    inv = lax.rsqrt(total * (1.0 / 8192) + EPS)
    for i in range(8):
        col[pl.ds(128 * i, 128), :] = jnp.broadcast_to(inv[i : i + 1, :], (128, 128)).T
    acc = jnp.zeros((8, 128), F32)
    for r in (0, 3, 1):
        acc = errors(r, acc)

    @pl.loop(0, 2)
    def _(n):
        cols = pl.ds(pl.multiple_of(512 * n, 512), 512)
        M[pl.ds(0, 256), cols] = jnp.dot(
            T[pl.ds(0, 256), pl.ds(0, 512)], E[pl.ds(0, 512), cols], preferred_element_type=F32
        ) + jnp.dot(
            T[pl.ds(0, 256), pl.ds(768, 256)], E[pl.ds(768, 256), cols], preferred_element_type=F32
        )

    a_up4.wait_recv()
    b_dn4.wait_recv()
    mapped_part(last, True)
    acc = errors(2, acc)

    tile = jnp.where(row == 0, jnp.max(amax_in), jnp.where(row == 1, jnp.max(amax_w), jnp.sum(acc)))

    def merge(first, count):
        out = scal[first]
        for i in range(1, count):
            v = scal[first + i]
            out = jnp.where(row < 2, jnp.maximum(out, v), out + v)
        return out

    scal[t] = tile
    sc1 = send_all([(scal.at[t], scal.at[t], {"dy": dy, "dxl": dx}) for dy, dx in TENSOR], "s")

    sent("w")

    a_rows, b_rows = (0, AROWS), (AROWS, 256 - AROWS)
    a_up_rows, a_dn_rows = (0, 80), (80, AROWS - 80)
    b_up_rows, b_dn_rows = (AROWS, 64), (AROWS + 64, 192 - AROWS)

    def gslot(dxh, dz, rows=(0, 256), other=0):
        g = ORDER.index((dxh, dz))
        return W.at[g // 2, pl.ds(256 * (g % 2) + rows[0], rows[1]), pl.ds(1024 * other, 1024)]

    to_sib, a_1, b_1, a_2, a_m, b_m = [], {}, {}, {}, {}, {}

    def half_term(g, own):
        dxh, dz = ORDER[g]
        ref, row0, col0 = turned(g)

        @pl.loop(0, 2)
        def _(n):
            at = pl.multiple_of(512 * n, 512)
            rows, cols = pl.ds(row0 + 256 * own, 256), pl.ds(at, 512)
            one = jnp.dot(ref[rows, pl.ds(col0, 1024)], E[:, cols], preferred_element_type=F32)
            start = pl.multiple_of(1024 * (1 - own) + at, 512)
            W[g // 2, pl.ds(256 * (g % 2), 256), pl.ds(start, 512)] = one.astype(BF16)

        if own == 0:
            to_sib.append(send(gslot(dxh, dz, other=1), sib.at[g], dk=1))

    def first_half_term():
        for n in range(2):
            cols, there = pl.ds(512 * n, 512), pl.ds(1024 + 512 * n, 512)
            one = M[pl.ds(0, 256), cols] + jnp.dot(
                T[pl.ds(0, 256), pl.ds(512, 256)], E[pl.ds(512, 256), cols], preferred_element_type=F32
            )
            W[0, pl.ds(0, 256), there] = one.astype(BF16)
            send(W.at[0, pl.ds(0, 256), there], sib.at[0, pl.ds(0, 256), cols], land="first", dk=1)
        to_sib.append(None)

    def term(g):
        dxh, dz = ORDER[g]
        ref, row0, col0 = turned(g)

        @pl.loop(0, 2)
        def _(n):
            at = pl.multiple_of(512 * n, 512)
            both = jnp.dot(
                ref[pl.ds(row0, 512), pl.ds(col0, 1024)],
                E[:, pl.ds(at, 512)],
                preferred_element_type=F32,
            ).astype(BF16)
            rows = pl.ds(256 * (g % 2), 256)
            W[g // 2, rows, pl.ds(pl.multiple_of(1024 + at, 512), 512)] = both[:256]
            W[g // 2, rows, pl.ds(at, 512)] = both[256:]

        to_sib.append(send(gslot(dxh, dz, other=1), sib.at[g], dk=1))

    def add(dxh, dz, rows, others, base=0):
        g = ORDER.index((dxh, dz))

        @pl.loop(0, rows[1] // 16)
        def _(i):
            here = pl.ds(pl.multiple_of(base + 16 * i, 16), 16)
            there = pl.ds(pl.multiple_of(256 * (g % 2) + rows[0] + 16 * i, 16), 16)
            total = W[g // 2, there, pl.ds(0, 1024)].astype(F32)
            for ref, index in others:
                total = total + ref[index, here, :].astype(F32)
            W[g // 2, there, pl.ds(0, 1024)] = total.astype(BF16)

    def along_z(dxh, dz, rows, up, dn, mid, at, far, gone, passed):
        if dz == 2:
            passed[dxh, UP] = send(gslot(dxh, 2, up), mid.at[at, pl.ds(0, up[1])], dz=UP)
            passed[dxh, DOWN] = send(gslot(dxh, 2, dn), mid.at[at + 1, pl.ds(0, dn[1])], dz=DOWN)
        elif dz:
            passed[dxh, dz].wait_recv()
            add(dxh, dz, up if dz == UP else dn, [(mid, at + dz // 2)])
            gone[dxh, dz] = send(gslot(dxh, dz, rows), far.at[at + dz // 2], dz=dz)

    def finish(g):
        dxh, dz = ORDER[g]
        to_sib[g].wait_recv()
        add(dxh, dz, (0, 256), [(sib, g)])
        if dxh:
            a_1[dz] = send(gslot(dxh, dz, a_rows), ra1.at[dz], dxh=1)

    def second_b(dxh, dz):
        along_z(dxh, dz, b_rows, b_up_rows, b_dn_rows, bm, 2 * dxh, rb1, b_1, b_m)

    def second_a(dz):
        a_1[dz].wait_recv()
        add(0, dz, a_rows, [(ra1, dz)])
        along_z(0, dz, a_rows, a_up_rows, a_dn_rows, am, 0, ra2, a_2, a_m)

    def term_of(g):
        turn(g, 2)
        term(g)

    turn(0, 2)
    first_half_term()
    half_term(0, 1)
    turn(1, 2)
    half_term(1, 0)
    await_group(landing["first"])
    add(1, 2, b_rows, [(sib, 0)], AROWS)
    second_b(1, 2)
    add(1, 2, a_rows, [(sib, 0)])
    a_1[2] = send(gslot(1, 2, a_rows), ra1.at[2], dxh=1)
    half_term(1, 1)
    await_group(sc1)
    at = 8 + xh * 4 + z
    scal[at] = merge(0, 8)
    sc2 = send_all([(scal.at[at], scal.at[at], {"dxh": dx, "dz": dz}) for dx, dz in CONTEXT], "s")
    term_of(2)
    finish(1)
    second_b(0, 2)
    term_of(3)
    finish(2)
    second_b(1, 1)
    term_of(4)
    finish(3)
    second_b(1, 3)
    second_a(2)
    term_of(5)
    finish(4)
    term_of(6)
    finish(5)
    second_b(0, 1)
    term_of(7)
    finish(6)
    second_b(0, 3)
    for n in (UP, DOWN):
        b_1[1, n].wait_recv()
    add(1, 0, b_rows, [(rb1, 2), (rb1, 3)])
    b_2 = send(gslot(1, 0, b_rows), rb2.at[0], dxh=1)
    second_a(1)
    second_a(3)
    await_group(sc2)
    scal[16 + k] = merge(8, 8)
    sc3 = send(scal.at[16 + k], scal.at[16 + k], "s", dk=1)
    finish(7)
    second_a(0)
    sc3.wait_recv()
    scal[18] = merge(16, 2)
    written = [load(scal.at[18], parts.at[pl.ds(256, 8), pl.ds(0, 128)])]

    for n in (UP, DOWN):
        b_1[0, n].wait_recv()
    for (first, count), landed in ((a_rows, []), (b_rows, [(rb1, 0), (rb1, 1)])):

        @pl.loop(0, count // 16)
        def _(i):
            here = pl.ds(pl.multiple_of(16 * i, 16), 16)
            mine = pl.ds(pl.multiple_of(256 + first + 16 * i, 16), 16)
            total = W[3, mine, pl.ds(0, 1024)].astype(F32)
            for ref, index in landed:
                total = total + ref[index, here, :].astype(F32)
            total_g[pl.ds(pl.multiple_of(first + 16 * i, 16), 16), :] = total

        rows = pl.ds(first, count)
        written.append(load(total_g.at[rows], parts.at[rows]))
    for n in (UP, DOWN):
        a_2[0, n].wait_recv()
    b_2.wait_recv()

    assert len(groups) <= SEND_SEMS and len(received) <= RECV_SEMS
    for group in groups:
        if group not in ("t", "w", "r"):
            sent(group)
    for copy in written:
        copy.wait()


def results(
    tokens_all, parts, ra2, rb2, hist_in, hist_w, grad, loss, hist_in_new, hist_w_new,
    held, late_a, late_b, tile, s_in, s_w, s_in_new, s_w_new, s_loss, sem_in, sem_out,
):
    a_rows, b_rows = pl.ds(0, AROWS), pl.ds(AROWS, 256 - AROWS)
    copies = [
        (parts.at[pl.ds(256, 8), pl.ds(0, 128)], tile),
        (hist_in, s_in),
        (hist_w, s_w),
        (parts.at[a_rows], held.at[a_rows]),
        (ra2, late_a),
        (parts.at[b_rows], held.at[b_rows]),
        (rb2, late_b),
    ]
    copies = [pltpu.make_async_copy(a, b, sem_in.at[i]) for i, (a, b) in enumerate(copies)]
    for copy in copies:
        copy.start()
    backs = [
        (s_in_new, hist_in_new),
        (s_w_new, hist_w_new),
        (s_loss, loss),
        (held.at[a_rows], grad.at[a_rows]),
        (held.at[b_rows], grad.at[b_rows]),
    ]
    backs = [pltpu.make_async_copy(a, b, sem_out.at[i]) for i, (a, b) in enumerate(backs)]
    for copy in copies[:3]:
        copy.wait()
    s_in_new[0] = jnp.max(tile[0:1, :])
    s_w_new[0] = jnp.max(tile[1:2, :])
    s_loss[0] = jnp.max(tile[2:3, :]) * (0.5 / (tokens_all * 8192))
    for i in range(15):
        s_in_new[i + 1] = s_in[i]
        s_w_new[i + 1] = s_w[i]
    for back in backs[:3]:
        back.start()
    scale = 1.0 / math.sqrt(tokens_all)
    for first, count, late, n in (0, AROWS, late_a, 2), (AROWS, 256 - AROWS, late_b, 1):
        for copy in copies[3:5] if first == 0 else copies[5:]:
            copy.wait()

        @pl.loop(0, count // 16)
        def _(i):
            here = pl.ds(pl.multiple_of(16 * i, 16), 16)
            rows = pl.ds(pl.multiple_of(first + 16 * i, 16), 16)
            total = held[rows, :]
            for index in range(n):
                total = total + late[index, here, :].astype(F32)
            held[rows, :] = total * scale

        backs[3 if first == 0 else 4].start()
    for back in backs:
        back.wait()


def local(
    teacher_in, teacher_resid, teacher_wo, teacher_gain, input_history, weight_history,
    student_hidden, student_gain, projection,
):
    tokens_all = teacher_in.shape[0] * lax.axis_size("context")
    hbm = pl.BlockSpec(memory_space=pl.ANY)
    parts, late_a, late_b = pl.pallas_call(
        functools.partial(kernel, tokens_all),
        name="distill",
        out_shape=(
            jax.ShapeDtypeStruct((264, 1024), F32),
            jax.ShapeDtypeStruct((2, AROWS, 1024), BF16),
            jax.ShapeDtypeStruct((1, 256 - AROWS, 1024), BF16),
        ),
        in_specs=[hbm] * 9,
        out_specs=(hbm,) * 3,
        scratch_shapes=[
            pltpu.VMEM((1024, 2048), BF16),
            pltpu.VMEM((4, 512, 2048), BF16),
            pltpu.VMEM((4, 256, 4096), BF16),
            pltpu.VMEM((4096, 1024), BF16),
            pltpu.VMEM((1024, 1024), BF16),
            pltpu.VMEM((1024, 1024), F32),
            pltpu.VMEM((1024, 1024), F32),
            pltpu.VMEM((1024, 1024), BF16),
            pltpu.VMEM((1024, 1024), BF16),
            pltpu.VMEM((1024, 1024), BF16),
            pltpu.VMEM((128, 4096), BF16),
            pltpu.VMEM((32, 8192), BF16),
            pltpu.VMEM((1024, 128), F32),
            pltpu.VMEM((8, 8, 128), F32),
            pltpu.VMEM((19, 8, 128), F32),
            pltpu.VMEM((8, 256, 1024), BF16),
            pltpu.VMEM((4, AROWS, 1024), BF16),
            pltpu.VMEM((4, 256 - AROWS, 1024), BF16),
            pltpu.VMEM((2, 96, 1024), BF16),
            pltpu.VMEM((4, 96, 1024), BF16),
            pltpu.VMEM((256, 1024), F32),
            pltpu.VMEM((1, 4096), F32),
            pltpu.VMEM((1, 1024), F32),
            pltpu.SMEM((16,), F32),
            pltpu.SMEM((16,), F32),
            pltpu.SemaphoreType.DMA((SEND_SEMS,)),
            pltpu.SemaphoreType.DMA((RECV_SEMS,)),
            pltpu.SemaphoreType.DMA((13,)),
        ],
        compiler_params=pltpu.CompilerParams(
            collective_id=0, has_side_effects=True, vmem_limit_bytes=62 << 20
        ),
        cost_estimate=pl.CostEstimate(
            flops=3 * 2 * 1024 * 1024 * 4096, bytes_accessed=16 << 20, transcendentals=1024
        ),
    )(
        input_history,
        weight_history,
        student_gain.reshape(1, -1),
        teacher_gain.reshape(1, -1),
        teacher_in,
        teacher_resid,
        teacher_wo,
        student_hidden,
        projection,
    )
    grad, loss, hist_in, hist_w = pl.pallas_call(
        functools.partial(results, tokens_all),
        name="results",
        out_shape=(
            jax.ShapeDtypeStruct((256, 1024), F32),
            jax.ShapeDtypeStruct((1,), F32),
            jax.ShapeDtypeStruct((16,), F32),
            jax.ShapeDtypeStruct((16,), F32),
        ),
        in_specs=[hbm] * 5,
        out_specs=(hbm,) * 4,
        scratch_shapes=[
            pltpu.VMEM((256, 1024), F32),
            pltpu.VMEM((2, AROWS, 1024), BF16),
            pltpu.VMEM((1, 256 - AROWS, 1024), BF16),
            pltpu.VMEM((8, 128), F32),
            *(pltpu.SMEM((n,), F32) for n in (16, 16, 16, 16, 1)),
            pltpu.SemaphoreType.DMA((7,)),
            pltpu.SemaphoreType.DMA((5,)),
        ],
    )(parts, late_a, late_b, input_history, weight_history)
    return grad, loss.reshape(()), hist_in, hist_w


def solution(mesh):
    placed = (
        P("context", "tensor"),
        P("context", "tensor"),
        P("tensor", None),
        P(),
        P(),
        P(),
        P(("context", "tensor"), None),
        P(),
        P("context", "tensor"),
    )
    return jax.shard_map(
        local,
        mesh=mesh,
        in_specs=placed,
        out_specs=(P("context", "tensor"), P(), P(), P()),
        check_vma=False,
    )
```
